128 devices in a mesh: seq: 8 (over z, x_lo), fsdp: 16 (over y, x_hi, core).
Axes of the slice: x: 4 (x_hi: 2, x_lo: 2; x = x_hi * 2 + x_lo), y: 4, z: 4, core: 2. Of those that a mesh axis runs over, the one named last changes fastest.
Arguments:
- block_input: bfloat16 [16384, 1024], P(('seq', 'fsdp')), may hold values from -8 to 8
- first_gain: bfloat16 [1024], P('fsdp'), may hold values from 0.5 to 1.5
- first_shift: bfloat16 [1024], P('fsdp'), may hold values from -1 to 1
- attention_weight: bfloat16 [1024, 3072], P('fsdp'), may hold values from -1.2 to 1.2
- query_bias: bfloat16 [1024], P('fsdp'), may hold values from -1 to 1
- value_bias: bfloat16 [1024], P('fsdp'), may hold values from -1 to 1
- output_weight: bfloat16 [1024, 1024], P('fsdp'), may hold values from -0.75 to 0.75
- output_bias: bfloat16 [1024], P('fsdp'), may hold values from -1 to 1
- second_gain: bfloat16 [1024], P('fsdp'), may hold values from 0.5 to 1.5
- second_shift: bfloat16 [1024], P('fsdp'), may hold values from -1 to 1
- upward_weight: bfloat16 [1024, 4096], P('fsdp'), may hold values from -0.1875 to 0.1875
- upward_bias: bfloat16 [4096], P('fsdp'), may hold values from -1 to 1
- downward_weight: bfloat16 [4096, 1024], P('fsdp'), may hold values from -0.09375 to 0.09375
- downward_bias: bfloat16 [1024], P('fsdp'), may hold values from -1 to 1
- cotangent: bfloat16 [16384, 1024], P(('seq', 'fsdp')), may hold values from -6 to 6
Outputs:
- block_output: bfloat16 [16384, 1024], P(('seq', 'fsdp'))
- input_gradient: float32 [16384, 1024], P(('seq', 'fsdp'))
- first_gain_gradient: float32 [1024], P('fsdp')
- first_shift_gradient: float32 [1024], P('fsdp')
- attention_weight_gradient: float32 [1024, 3072], P('fsdp')
- query_bias_gradient: float32 [1024], P('fsdp')
- value_bias_gradient: float32 [1024], P('fsdp')
- output_weight_gradient: float32 [1024, 1024], P('fsdp')
- output_bias_gradient: float32 [1024], P('fsdp')
- second_gain_gradient: float32 [1024], P('fsdp')
- second_shift_gradient: float32 [1024], P('fsdp')
- upward_weight_gradient: float32 [1024, 4096], P('fsdp')
- upward_bias_gradient: float32 [4096], P('fsdp')
- downward_weight_gradient: float32 [4096, 1024], P('fsdp')
- downward_bias_gradient: float32 [1024], P('fsdp')
The draws below stay inside these ranges and needn't reach their ends.
All inputs are finite; a program needn't handle non-finite values.
Results may differ from the reference program's by a relative error of at most 0.024.
Values may be sent and summed in bfloat16 or wider, within the bound.
No kernel may reach another device: no remote copies, remote signals or barrier semaphores. Data moves between devices by JAX's collectives and lax.ppermute only.
A program may use at most 128 MiB of HBM per device.

```python
import math
import jax
import jax.numpy as jnp
from jax import lax

D = 1024
HEADS = 16
HEAD = 64
FF = 4096
SEQS = 8
TOKENS = 16384
LENGTH = 2048


def shared_parts(key):
    first_direction = jnp.clip(jax.random.normal(jax.random.fold_in(key, 71), (D,), jnp.float32), -3.0, 3.0)
    second_direction = jnp.clip(jax.random.normal(jax.random.fold_in(key, 72), (D,), jnp.float32), -3.0, 3.0)
    pairing = 2.0 * jnp.clip(jax.random.normal(jax.random.fold_in(key, 73), (D,), jnp.float32), -3.0, 3.0)
    return (first_direction, second_direction, pairing)


def draw_block_input(key, part):
    first_direction, second_direction, pairing = shared_parts(key)
    key = jax.random.fold_in(key, 5)
    noise = jnp.clip(jax.random.normal(key, (TOKENS, D), jnp.float32), -4.0, 4.0)
    place = (jnp.arange(TOKENS, dtype=jnp.int32) % LENGTH).astype(jnp.float32) / LENGTH
    ramp = 1.0 - place
    total = noise + 0.5 * first_direction[None, :] + ramp[:, None] * second_direction[None, :]
    return jnp.clip(total, -8.0, 8.0).astype(jnp.bfloat16)


def draw_attention_weight(key, part):
    first_direction, second_direction, pairing = shared_parts(key)
    key = jax.random.fold_in(key, 6)
    base = jnp.clip(jax.random.normal(key, (D, 3 * D), jnp.float32), -6.0, 6.0) / math.sqrt(D)
    extra_query = first_direction[:, None] * pairing[None, :] / D
    extra_key = second_direction[:, None] * pairing[None, :] / D
    extra = jnp.concatenate([extra_query, extra_key, jnp.zeros((D, D), jnp.float32)], axis=1)
    return jnp.clip(base + extra, -1.2, 1.2).astype(jnp.bfloat16)


def level_of(stream_key, shape, shards, least, largest):
    level, own = 1.0, jax.random.fold_in(stream_key, 6)
    for dim, parts in shards:
        draws = jnp.exp(jax.random.uniform(jax.random.fold_in(own, dim), (parts,), jnp.float32, least / len(shards), largest / len(shards)))
        level = level * jnp.repeat(draws, shape[dim] // parts).reshape([-1 if axis == dim else 1 for axis in range(len(shape))])
    return level


def gaussian(own_key, dims, scale, reach, pieces=(), kind=jnp.bfloat16):
    drawn = scale * jax.random.normal(own_key, dims, jnp.float32)
    if pieces:
        drawn = drawn * level_of(own_key, dims, pieces, -0.22, 0.18)
    return jnp.clip(drawn, -reach, reach).astype(kind)


def setup_inputs(seed: int = 0) -> dict:
    streams_of = jax.random.split(jax.random.key(seed), 16)
    return {
        "block_input": draw_block_input(jax.random.fold_in(streams_of[15], 71), 0),
        "first_gain": jnp.clip(1.0 + 0.1 * jax.random.normal(streams_of[1], (D,), jnp.float32), 0.5, 1.5).astype(jnp.bfloat16),
        "first_shift": gaussian(streams_of[2], (D,), 0.2, 1.0, ((0, 16),)),
        "attention_weight": draw_attention_weight(jax.random.fold_in(streams_of[15], 71), 0),
        "query_bias": gaussian(streams_of[4], (D,), 0.2, 1.0, ((0, 16),)),
        "value_bias": gaussian(streams_of[5], (D,), 0.2, 1.0, ((0, 16),)),
        "output_weight": gaussian(streams_of[6], (D, D), (D // 16) ** -0.5, 0.75, ((0, 16),)),
        "output_bias": gaussian(streams_of[7], (D,), 0.2, 1.0, ((0, 16),)),
        "second_gain": jnp.clip(1.0 + 0.1 * jax.random.normal(streams_of[8], (D,), jnp.float32), 0.5, 1.5).astype(jnp.bfloat16),
        "second_shift": gaussian(streams_of[9], (D,), 0.2, 1.0, ((0, 16),)),
        "upward_weight": gaussian(streams_of[10], (D, FF), D ** -0.5, 0.1875, ((0, 16),)),
        "upward_bias": gaussian(streams_of[11], (FF,), 0.2, 1.0, ((0, 16),)),
        "downward_weight": gaussian(streams_of[12], (FF, D), FF ** -0.5, 0.09375, ((0, 16),)),
        "downward_bias": gaussian(streams_of[13], (D,), 0.2, 1.0, ((0, 16),)),
        "cotangent": gaussian(streams_of[14], (TOKENS, D), 1.0, 6.0, ((0, 128),)),
    }


@jax.custom_vjp
def low(v):
    return lax.optimization_barrier(v.astype(jnp.bfloat16)).astype(jnp.float32)

@jax.custom_vjp
def low_back(v):
    return v

def low_keep(v):
    return (low(v), None)

def low_pass(kept, grad):
    return (grad,)

def back_keep(v):
    return (v, None)

def back_low(kept, grad):
    return (low(grad),)
low.defvjp(low_keep, low_pass)
low_back.defvjp(back_keep, back_low)
epsilon = 1e-05
score_scale = 0.125
highest = lax.Precision.HIGHEST

def layer_norm(values, gain, shift):
    centre = lax.optimization_barrier(jnp.mean(values, axis=-1, keepdims=True))
    centred = values - centre
    spread = lax.optimization_barrier(jnp.mean(centred * centred, axis=-1, keepdims=True))
    return centred * lax.rsqrt(spread + epsilon) * gain + shift

def gelu_tanh(values):
    return 0.5 * values * (1.0 + jnp.tanh(0.7978845608028654 * (values + 0.044715 * values * values * values)))

def attention(query, key, value):
    length = query.shape[0] // SEQS
    block = min(512, length)
    slopes = jnp.exp2(-8.0 * jnp.arange(1, HEADS + 1, dtype=jnp.int32).astype(jnp.float32) / HEADS)
    key_pos = jnp.arange(length, dtype=jnp.int32)

    def one_sequence(operands):
        query_seq, key_seq, value_seq = operands

        def one_block(start):
            query_block = lax.dynamic_slice_in_dim(query_seq, start, block, 0)
            raw = jnp.einsum('qhe,khe->hqk', query_block, key_seq, precision=highest)
            query_pos = start + jnp.arange(block, dtype=jnp.int32)
            distance = (query_pos[:, None] - key_pos[None, :]).astype(jnp.float32)
            biased = low_back(raw * score_scale - slopes[:, None, None] * distance[None, :, :])
            biased = jnp.where((distance >= 0.0)[None, :, :], biased, -1e+30)
            peak = lax.optimization_barrier(jnp.max(biased, axis=-1, keepdims=True))
            log_total = peak + jnp.log(lax.optimization_barrier(jnp.sum(jnp.exp(biased - peak), axis=-1, keepdims=True)))
            attend = low(jnp.exp(biased - log_total))
            return jnp.einsum('hqk,khe->qhe', attend, value_seq, precision=highest)
        starts = jnp.arange(0, length, block, dtype=jnp.int32)
        blocks = lax.map(jax.checkpoint(one_block), starts)
        return blocks.reshape(length, HEADS, HEAD)
    shaped = (query.reshape(SEQS, length, HEADS, HEAD), key.reshape(SEQS, length, HEADS, HEAD), value.reshape(SEQS, length, HEADS, HEAD))
    result = lax.map(one_sequence, shaped)
    return result.reshape(SEQS * length, HEADS * HEAD)

def forward(block_input, first_gain, first_shift, attention_weight, query_bias, value_bias, output_weight, output_bias, second_gain, second_shift, upward_weight, upward_bias, downward_weight, downward_bias):
    normed_first = low(layer_norm(block_input, first_gain, first_shift))
    projected = jnp.dot(normed_first, attention_weight, precision=highest, preferred_element_type=jnp.float32)
    query = low_back(low(projected[:, 0:D] + query_bias))
    key = low_back(low(projected[:, D:2 * D]))
    value = low_back(low(projected[:, 2 * D:3 * D] + value_bias))
    mixed = low_back(low(attention(query, key, value)))
    branch = low_back(jnp.dot(mixed, output_weight, precision=highest, preferred_element_type=jnp.float32) + output_bias)
    residual_mid = block_input + branch
    normed_second = low(layer_norm(residual_mid, second_gain, second_shift))
    upward = low_back(jnp.dot(normed_second, upward_weight, precision=highest, preferred_element_type=jnp.float32) + upward_bias)
    activated = low(gelu_tanh(upward))
    return residual_mid + jnp.dot(activated, downward_weight, precision=highest, preferred_element_type=jnp.float32) + downward_bias

def reference(block_input, first_gain, first_shift, attention_weight, query_bias, value_bias, output_weight, output_bias, second_gain, second_shift, upward_weight, upward_bias, downward_weight, downward_bias, cotangent):
    arrays = (block_input, first_gain, first_shift, attention_weight, query_bias, value_bias, output_weight, output_bias, second_gain, second_shift, upward_weight, upward_bias, downward_weight, downward_bias)
    widened = tuple((item.astype(jnp.float32) for item in arrays))
    result, pullback = jax.vjp(forward, *widened)
    grads = pullback(cotangent.astype(jnp.float32))
    return (result.astype(jnp.bfloat16), grads[0], grads[1], grads[2], grads[3], grads[4], grads[5], grads[6], grads[7], grads[8], grads[9], grads[10], grads[11], grads[12], grads[13])
```

```python
import jax
import jax.numpy as jnp
import numpy as np
from jax import lax
from jax.experimental import pallas as pl
from jax.experimental.pallas import tpu as pltpu
from jax.sharding import Mesh
from jax.sharding import PartitionSpec as P

D = 1024
HEADS = 16
HEAD = 64
FF = 4096

epsilon = 1e-05
score_scale = 0.125
bf16 = jnp.bfloat16
f32 = jnp.float32

SEQ = ("z", "xl")
FSDP = ("y", "xh", "c")
ALL = SEQ + FSDP
ROWS = 128
TILE = 256
TILES = 8
LENGTH = TILE * TILES

NT = (((1,), (1,)), ((), ()))


def dot(a, b):
    return jnp.dot(a, b, preferred_element_type=f32)


def dot_nt(a, b):
    return lax.dot_general(a, b, NT, preferred_element_type=f32)


def dot_tn(a, b):
    return lax.dot_general(a, b, (((0,), (0,)), ((), ())), preferred_element_type=f32)


def stage_blocks(tab_ref, slope_ref, x_ref, qa, ka, emit_rest):
    lane = lax.broadcasted_iota(jnp.int32, (ROWS, HEAD), 1)
    row = lax.broadcasted_iota(jnp.int32, (ROWS, HEAD), 0)
    ones = jnp.where(lane < 3, 1.0, 0.0).astype(bf16)
    slope = slope_ref[0]
    for a in range(HEADS):
        block = x_ref[tab_ref[a]]
        rows = slice(a * ROWS, (a + 1) * ROWS)
        place = slope * (row + (a * ROWS - LENGTH // 2)).astype(f32)
        high = place.astype(bf16)
        rest = place - high.astype(f32)
        middle = rest.astype(bf16)
        low = (rest - middle.astype(f32)).astype(bf16)
        extra = jnp.where(
            lane == 0,
            high.astype(f32),
            jnp.where(
                lane == 1, middle.astype(f32), jnp.where(lane == 2, low.astype(f32), 0.0)
            ),
        ).astype(bf16)
        scaled = (block[:, 0:HEAD].astype(f32) * score_scale).astype(bf16)
        qa[rows, :] = jnp.concatenate([scaled, ones], axis=1)
        ka[rows, :] = jnp.concatenate([block[:, HEAD : 2 * HEAD], extra], axis=1)
        emit_rest(a, rows, block)


def fold(tile, op):
    parts = [tile[8 * g : 8 * g + 8] for g in range(TILE // 8)]
    while len(parts) > 1:
        parts = [op(parts[2 * g], parts[2 * g + 1]) for g in range(len(parts) // 2)]
    return parts[0]


def future():
    key = lax.broadcasted_iota(jnp.int32, (TILE, TILE), 0)
    query = lax.broadcasted_iota(jnp.int32, (TILE, TILE), 1)
    return key > query


def forward_kernel(tab_ref, slope_ref, x_ref, o_ref, lse_ref, qa, ka, vt, s_sc, p_sc):
    def rest(a, rows, block):
        vt[:, rows] = block[:, 2 * HEAD :].astype(f32).T.astype(bf16)

    stage_blocks(tab_ref, slope_ref, x_ref, qa, ka, rest)
    hidden = future()
    for i in range(TILES):
        q = qa[i * TILE : (i + 1) * TILE, :]
        peak = None
        for j in range(i + 1):
            s = dot_nt(ka[j * TILE : (j + 1) * TILE, :], q)
            if j == i:
                s = jnp.where(hidden, -1e30, s)
            s_sc[j * TILE : (j + 1) * TILE, :] = s
            top = fold(s, jnp.maximum)
            peak = top if peak is None else jnp.maximum(peak, top)
        peak = jnp.max(peak, axis=0, keepdims=True)
        total = None
        for j in range(i + 1):
            p = jnp.exp(s_sc[j * TILE : (j + 1) * TILE, :] - peak)
            p_sc[j * TILE : (j + 1) * TILE, :] = p.astype(bf16)
            part = fold(p, jnp.add)
            total = part if total is None else total + part
        total = jnp.sum(total, axis=0, keepdims=True)
        n = (i + 1) * TILE
        out = dot(vt[:, 0:n], p_sc[0:n, :]) / total
        out = out.T.astype(bf16)
        o_ref[tab_ref[2 * i]] = out[0:ROWS]
        o_ref[tab_ref[2 * i + 1]] = out[ROWS:]
        lse_ref[i] = peak + jnp.log(total)


def backward_kernel(
    tab_ref, slope_ref, x_ref, do_ref, lse_ref, dx_ref,
    qa, ka, va, kt, da, dq, dk, dv, p_sc, dp_sc, ds_sc,
):
    def rest(a, rows, block):
        va[rows, :] = block[:, 2 * HEAD :]
        kt[:, rows] = block[:, HEAD : 2 * HEAD].astype(f32).T.astype(bf16)
        da[rows, :] = do_ref[tab_ref[a]]

    stage_blocks(tab_ref, slope_ref, x_ref, qa, ka, rest)
    hidden = future()
    for i in range(TILES):
        here = slice(i * TILE, (i + 1) * TILE)
        q = qa[here, :]
        q_plain = q[:, 0:HEAD]
        grad = da[here, :]
        lse = lse_ref[i]
        delta = None
        for j in range(i + 1):
            there = slice(j * TILE, (j + 1) * TILE)
            s = dot_nt(ka[there, :], q)
            if j == i:
                s = jnp.where(hidden, -1e30, s)
            p = jnp.exp(s - lse)
            dp = dot_nt(va[there, :], grad)
            p_sc[there, :] = p
            dp_sc[there, :] = dp
            part = fold(p * dp, jnp.add)
            delta = part if delta is None else delta + part
            value = dot(p.astype(bf16), grad)
            dv[there, :] = value if j == i else dv[there, :] + value
        delta = jnp.sum(delta, axis=0, keepdims=True)
        for j in range(i + 1):
            there = slice(j * TILE, (j + 1) * TILE)
            ds = (p_sc[there, :] * (dp_sc[there, :] - delta)).astype(bf16)
            ds_sc[there, :] = ds
            key = dot(ds, q_plain)
            dk[there, :] = key if j == i else dk[there, :] + key
        n = (i + 1) * TILE
        dq[here, :] = (dot(kt[:, 0:n], ds_sc[0:n, :]) * score_scale).T
    for a in range(HEADS):
        rows = slice(a * ROWS, (a + 1) * ROWS)
        dx_ref[tab_ref[a]] = jnp.concatenate(
            [dq[rows, :], dk[rows, :], dv[rows, :]], axis=1
        ).astype(bf16)


smem = pl.BlockSpec(memory_space=pltpu.SMEM)
vmem = pl.BlockSpec(memory_space=pltpu.VMEM)


def attention_forward(tab, slope, x):
    return pl.pallas_call(
        forward_kernel,
        out_shape=(
            jax.ShapeDtypeStruct((HEADS, ROWS, HEAD), bf16),
            jax.ShapeDtypeStruct((TILES, 1, TILE), f32),
        ),
        in_specs=[smem, smem, vmem],
        out_specs=(vmem, vmem),
        scratch_shapes=[
            pltpu.VMEM((LENGTH, 2 * HEAD), bf16),
            pltpu.VMEM((LENGTH, 2 * HEAD), bf16),
            pltpu.VMEM((HEAD, LENGTH), bf16),
            pltpu.VMEM((LENGTH, TILE), f32),
            pltpu.VMEM((LENGTH, TILE), bf16),
        ],
        compiler_params=pltpu.CompilerParams(vmem_limit_bytes=40 * 2**20),
        cost_estimate=pl.CostEstimate(
            flops=2 * 10**9, bytes_accessed=2 * 10**6, transcendentals=24 * 10**5
        ),
        name="attention_forward",
    )(tab, slope, x)


def attention_backward(tab, slope, x, grad, lse):
    return pl.pallas_call(
        backward_kernel,
        out_shape=jax.ShapeDtypeStruct((HEADS, ROWS, 3 * HEAD), bf16),
        in_specs=[smem, smem, vmem, vmem, vmem],
        out_specs=vmem,
        scratch_shapes=[
            pltpu.VMEM((LENGTH, 2 * HEAD), bf16),
            pltpu.VMEM((LENGTH, 2 * HEAD), bf16),
            pltpu.VMEM((LENGTH, HEAD), bf16),
            pltpu.VMEM((HEAD, LENGTH), bf16),
            pltpu.VMEM((LENGTH, HEAD), bf16),
            pltpu.VMEM((LENGTH, HEAD), f32),
            pltpu.VMEM((LENGTH, HEAD), f32),
            pltpu.VMEM((LENGTH, HEAD), f32),
            pltpu.VMEM((LENGTH, TILE), f32),
            pltpu.VMEM((LENGTH, TILE), f32),
            pltpu.VMEM((LENGTH, TILE), bf16),
        ],
        compiler_params=pltpu.CompilerParams(vmem_limit_bytes=40 * 2**20),
        cost_estimate=pl.CostEstimate(
            flops=5 * 10**9, bytes_accessed=3 * 10**6, transcendentals=24 * 10**5
        ),
        name="attention_backward",
    )(tab, slope, x, grad, lse)


def shift(value, axis, step):
    size = lax.axis_size(axis)
    return lax.ppermute(value, axis, [(i, (i + step) % size) for i in range(size)])


def gather(own):
    half = own.shape[1] // 2
    third = shift(own, "y", 1)
    first = shift(own, "y", -1)
    second = jnp.concatenate(
        [shift(third[:, :half], "y", 1), shift(first[:, half:], "y", -1)], axis=1
    )
    mine = [own, first, second, third]
    other = [shift(block, "c", 1) for block in mine]
    return jnp.concatenate(mine + other, axis=0)


def scatter(mine, other):
    width = mine.shape[1]
    half = width // 2
    mine = mine.reshape(4, ROWS, width)
    other = other.reshape(4, ROWS, width)
    far = mine[2] + shift(other[2], "c", 1).astype(f32)
    far = far.astype(bf16)
    to_next = shift(far[:, :half], "y", 1).astype(f32)
    to_last = shift(far[:, half:], "y", -1).astype(f32)
    near = mine[1] + shift(other[1], "c", 1).astype(f32)
    back = mine[3] + shift(other[3], "c", 1).astype(f32)
    near = jnp.concatenate([near[:, :half] + to_next, near[:, half:]], axis=1).astype(bf16)
    back = jnp.concatenate([back[:, :half], back[:, half:] + to_last], axis=1).astype(bf16)
    here = mine[0] + shift(other[0], "c", 1).astype(f32)
    return here + shift(near, "y", 1).astype(f32) + shift(back, "y", -1).astype(f32)


def exchange(value, axes):
    return lax.all_to_all(value, axes, split_axis=0, concat_axis=0, tiled=True)


def normalize(values):
    centre = jnp.mean(values, axis=-1, keepdims=True)
    centred = values - centre
    spread = jnp.mean(centred * centred, axis=-1, keepdims=True)
    inverse = lax.rsqrt(spread + epsilon)
    return centred * inverse, inverse


def gelu_tanh(values):
    return (
        0.5
        * values
        * (1.0 + jnp.tanh(0.7978845608028654 * (values + 0.044715 * values * values * values)))
    )


def norm_back(grad, gain, normal, inverse):
    scaled = grad * gain
    return inverse * (
        scaled
        - jnp.mean(scaled, axis=-1, keepdims=True)
        - normal * jnp.mean(scaled * normal, axis=-1, keepdims=True)
    )


def on_device(
    block_input,
    first_gain,
    first_shift,
    attention_weight,
    query_bias,
    value_bias,
    output_weight,
    output_bias,
    second_gain,
    second_shift,
    upward_weight,
    upward_bias,
    downward_weight,
    downward_bias,
    cotangent,
):
    y = lax.axis_index("y")
    xh = lax.axis_index("xh")
    c = lax.axis_index("c")
    shard = 4 * y + 2 * xh + c

    with jax.named_scope("weights_attention"):
        split = attention_weight.reshape(64, 3, 4, 2, 2, HEAD).transpose(2, 3, 4, 0, 1, 5)
        split = split.reshape(4, 2, 2, 64, 3 * HEAD)
        paired = jnp.concatenate([split, split[:, ::-1]], axis=-1)
        small = jnp.concatenate(
            [first_gain, first_shift, output_bias, second_gain, second_shift, downward_bias]
        )
        small = jnp.pad(small[None, :], ((0, 7), (0, 0)))
        payload = jnp.concatenate(
            [
                paired.reshape(16, 64, 6 * HEAD),
                jnp.broadcast_to(small[None], (16, 8, 6 * HEAD)),
            ],
            axis=1,
        )
        arrived = exchange(payload, FSDP)
        project = arrived[:, :64].reshape(D, 6 * HEAD)
        vectors = arrived[:, 64].reshape(16, 6, 64).transpose(1, 0, 2).reshape(6, D).astype(f32)
        gain_first, shift_first, bias_output, gain_second, shift_second, bias_downward = [
            vectors[g] for g in range(6)
        ]
    with jax.named_scope("weights_pair"):
        biases = jnp.concatenate(
            [query_bias, value_bias, upward_bias, jnp.zeros((D - 384,), bf16)]
        )
        own_rows = jnp.concatenate(
            [output_weight, jnp.broadcast_to(biases[None], (16, D)), downward_weight], axis=0
        )
        other_rows = shift(own_rows, "xh", 1)
        output_pair = jnp.concatenate([output_weight, other_rows[:64]], axis=0)
        downward_pair = jnp.concatenate([downward_weight, other_rows[80:]], axis=0)
        other_biases = other_rows[64]
        zero = jnp.zeros((HEAD,), bf16)
        bias_own = jnp.concatenate([query_bias, zero, value_bias]).astype(f32)
        bias_other = jnp.concatenate([other_biases[0:64], zero, other_biases[64:128]]).astype(f32)
        bias_upward = jnp.concatenate([upward_bias, other_biases[128:384]]).astype(f32)
    with jax.named_scope("weights_upward"):
        up_split = upward_weight.reshape(64, 4, 2, 2, 256).transpose(1, 2, 3, 0, 4)
        up_paired = jnp.concatenate([up_split, up_split[:, ::-1]], axis=-1)
        upward_pair = exchange(up_paired.reshape(16, 64, 512), FSDP).reshape(D, 512)

    with jax.named_scope("first"):
        inputs = gather(block_input)
        normal_first, inverse_first = normalize(inputs.astype(f32))
        normed_first = (normal_first * gain_first + shift_first).astype(bf16)
        heads_other = (dot(normed_first, project[:, 192:]) + bias_other).astype(bf16)
        heads_arrived = shift(heads_other, "xh", 1)
        heads_own = (dot(normed_first, project[:, :192]) + bias_own).astype(bf16)
        heads = jnp.concatenate([heads_own, heads_arrived], axis=0).reshape(16, ROWS, 192)

    place = np.arange(16)
    tab = (
        8 * ((place // 2 % 2) ^ xh) + 4 * ((place % 2) ^ c) + (place // 4 - y) % 4
    ).astype(jnp.int32)
    slope = jnp.exp2(-8.0 * (shard + 1).astype(f32) / HEADS)[None]

    with jax.named_scope("attention"):
        mixed, lse = attention_forward(tab, slope, heads)
        mixed_arrived = shift(mixed[8:], "xh", 1)
        mixed_pair = jnp.concatenate([mixed[:8], mixed_arrived], axis=-1).reshape(8 * ROWS, 128)
    with jax.named_scope("output"):
        branch_other = dot(mixed_pair[512:], output_pair).astype(bf16)
        branch_mine = dot(mixed_pair[:512], output_pair)
        branch = scatter(branch_mine, branch_other) + bias_output
        residual_mid = block_input.astype(f32) + branch
        normal_second, inverse_second = normalize(residual_mid)
        normed_second = (normal_second * gain_second + shift_second).astype(bf16)

    with jax.named_scope("feed"):
        cotangents = gather(cotangent)
        activated_grad = dot_nt(cotangents, downward_pair)
        seconds = gather(normed_second)
        upward = dot(seconds, upward_pair) + bias_upward
        activated, gelu_back = jax.vjp(gelu_tanh, upward)
        activated = activated.astype(bf16)
        upward_grad = gelu_back(activated_grad)[0].astype(bf16)
        second_other = dot_nt(upward_grad[512:], upward_pair).astype(bf16)
        second_mine = dot_nt(upward_grad[:512], upward_pair)
        second_in = scatter(second_mine, second_other)
        second_gain_grad = jnp.sum(second_in * normal_second, axis=0)
        second_shift_grad = jnp.sum(second_in, axis=0)
        wide_cotangent = cotangent.astype(f32)
        mid_grad = wide_cotangent + norm_back(
            second_in, gain_second, normal_second, inverse_second
        )
        branch_grad = mid_grad.astype(bf16)

    with jax.named_scope("mixed_back"):
        branch_grads = gather(branch_grad)
        mixed_grad = dot_nt(branch_grads, output_pair).astype(bf16)
        mixed_grad_arrived = shift(mixed_grad[:, HEAD:], "xh", 1)
        out_grad = jnp.concatenate([mixed_grad[:, :HEAD], mixed_grad_arrived], axis=0)
        out_grad = out_grad.reshape(16, ROWS, HEAD)

    with jax.named_scope("feed_out"):
        out_other = dot(activated[512:], downward_pair).astype(bf16)
        out_mine = dot(activated[:512], downward_pair)
        block_output = (residual_mid + scatter(out_mine, out_other) + bias_downward).astype(bf16)

    with jax.named_scope("feed_gradients"):
        downward_grad = dot_tn(activated, cotangents)
        output_grad = dot_tn(mixed_pair, branch_grads)
        rows_other = jnp.concatenate([output_grad[64:], downward_grad[256:]], axis=0).astype(bf16)
        rows_arrived = shift(rows_other, "xh", 1).astype(f32)
        output_sum = (output_grad[:64] + rows_arrived[:64]).astype(bf16).reshape(8, 8, D)
        downward_sum = (downward_grad[:256] + rows_arrived[64:]).astype(bf16).reshape(8, 32, D)
        rows_all = exchange(jnp.concatenate([output_sum, downward_sum], axis=1), SEQ)
        rows_total = jnp.sum(rows_all.astype(f32), axis=0).astype(bf16)

        upward_weight_grad = dot_tn(seconds, upward_grad).astype(bf16)
        upward_bias_grad = jnp.sum(upward_grad.astype(f32), axis=0).astype(bf16)
        quads = [
            second_gain_grad,
            second_shift_grad,
            jnp.sum(branch_grad.astype(f32), axis=0),
            jnp.sum(wide_cotangent, axis=0),
        ]
        quads = jnp.stack([q.astype(bf16).reshape(16, 64) for q in quads], axis=1)
        extra = jnp.concatenate(
            [
                quads.reshape(16, 2, 128),
                jnp.broadcast_to(upward_bias_grad.reshape(1, 4, 128), (16, 4, 128)),
                jnp.zeros((16, 2, 128), bf16),
            ],
            axis=1,
        )
        extra = jnp.broadcast_to(extra[:, None], (16, 8, 8, 128))
        shares = jnp.concatenate(
            [upward_weight_grad.reshape(16, 8, 8, 512), extra], axis=-1
        )
        shares = shares.transpose(1, 0, 2, 3).reshape(128, 8, 640)
        arrived_up = exchange(shares, ALL).reshape(8, 4, 2, 2, 8, 640).astype(f32)
        up_sum = jnp.sum(arrived_up[..., :512], axis=0)
        up_total = up_sum[..., :256] + up_sum[:, ::-1, :, :, 256:]
        up_total = up_total.transpose(3, 0, 1, 2, 4).reshape(8, FF).astype(bf16)
        small_sum = jnp.sum(arrived_up[..., 512:], axis=0)
        four_total = jnp.sum(small_sum[:, :, :, 0:2], axis=(0, 1, 2))
        bias_rows = small_sum.reshape(16, 8, 128)[:, 2:6].reshape(16, 512)
        bias_total = (
            lax.dynamic_index_in_dim(bias_rows, shard, 0, keepdims=False)[:256]
            + lax.dynamic_index_in_dim(bias_rows, shard ^ 2, 0, keepdims=False)[256:]
        )
        early = jnp.concatenate([rows_total, up_total.reshape(32, D)], axis=0)
        early_all = exchange(jnp.broadcast_to(early[None], (8, 72, D)), SEQ).astype(f32)
        output_weight_gradient = early_all[:, :8].reshape(64, D)
        downward_weight_gradient = early_all[:, 8:40].reshape(256, D)
        upward_weight_gradient = early_all[:, 40:].reshape(64, FF)

    with jax.named_scope("attention_back"):
        grads = attention_backward(tab, slope, heads, out_grad, lse)
        grads_arrived = shift(grads[8:], "xh", 1)
        joined = jnp.concatenate([grads[:8], grads_arrived], axis=-1).reshape(8 * ROWS, 384)
    with jax.named_scope("first_back"):
        first_other = dot_nt(joined[512:], project).astype(bf16)
        first_mine = dot_nt(joined[:512], project)
        first_in = scatter(first_mine, first_other)
        own_normal = normal_first[:ROWS]
        input_gradient = mid_grad + norm_back(
            first_in, gain_first, own_normal, inverse_first[:ROWS]
        )
    with jax.named_scope("attention_gradients"):
        weight_grad = dot_tn(normed_first, joined).astype(bf16)
        first_gain_part = jnp.sum(first_mine * normal_first[:512], axis=0) + jnp.sum(
            first_other.astype(f32) * normal_first[512:], axis=0
        )
        first_shift_part = jnp.sum(first_mine, axis=0) + jnp.sum(first_other.astype(f32), axis=0)
        token_sum = jnp.sum(grads.astype(f32), axis=(0, 1))
        pair_row = jnp.concatenate([token_sum[:64], token_sum[128:]]).astype(bf16)
        quads = jnp.concatenate(
            [
                first_gain_part.astype(bf16).reshape(16, 1, 64),
                first_shift_part.astype(bf16).reshape(16, 1, 64),
            ],
            axis=-1,
        )
        extra = jnp.concatenate(
            [
                quads,
                jnp.broadcast_to(pair_row[None, None], (16, 1, 128)),
                jnp.zeros((16, 6, 128), bf16),
            ],
            axis=1,
        )
        extra = jnp.broadcast_to(extra[:, None], (16, 8, 8, 128))
        shares = jnp.concatenate([weight_grad.reshape(16, 8, 8, 384), extra], axis=-1)
        shares = shares.transpose(1, 0, 2, 3).reshape(128, 8, 512)
        arrived_last = exchange(shares, ALL).reshape(8, 4, 2, 2, 8, 512).astype(f32)
        last_sum = jnp.sum(arrived_last, axis=0)
        last_total = last_sum[..., :192] + last_sum[:, ::-1, :, :, 192:384]
        last_total = last_total.reshape(16, 8, 3, HEAD).transpose(1, 2, 0, 3).reshape(8, 3 * D)
        late = last_total.astype(bf16).reshape(24, D)
        late_all = exchange(jnp.broadcast_to(late[None], (8, 24, D)), SEQ).astype(f32)
        attention_weight_gradient = late_all.reshape(64, 3 * D)
        last_small = last_sum[..., 384:].reshape(16, 8, 128)
        first_total = jnp.sum(last_small[:, 0], axis=0)
        bias_pair = lax.dynamic_index_in_dim(last_small[:, 1], shard, 0, keepdims=False)

    return (
        block_output,
        input_gradient,
        first_total[:64],
        first_total[64:],
        attention_weight_gradient,
        bias_pair[:64],
        bias_pair[64:],
        output_weight_gradient,
        four_total[1, :64],
        four_total[0, :64],
        four_total[0, 64:],
        upward_weight_gradient,
        bias_total,
        downward_weight_gradient,
        four_total[1, 64:],
    )


def solution(mesh):
    grid = Mesh(mesh.devices.reshape(4, 2, 4, 2, 2), ALL)
    tokens = P(ALL, None)
    rows = P(FSDP, None)
    line = P(FSDP)
    return jax.shard_map(
        on_device,
        mesh=grid,
        in_specs=(
            tokens, line, line, rows, line, line, rows, line, line, line, rows, line, rows, line,
            tokens,
        ),
        out_specs=(
            tokens, tokens, line, line, rows, line, line, rows, line, line, line, rows, line, rows,
            line,
        ),
        check_vma=False,
    )
```

```python
import jax
import jax.numpy as jnp
import numpy as np
from jax import lax
from jax.experimental import pallas as pl
from jax.experimental.pallas import tpu as pltpu
from jax.sharding import Mesh
from jax.sharding import PartitionSpec as P

D = 1024
HEADS = 16
HEAD = 64
FF = 4096

epsilon = 1e-05
score_scale = 0.125
bf16 = jnp.bfloat16
f32 = jnp.float32

SEQ = ("z", "xl")
FSDP = ("y", "xh", "c")
ALL = SEQ + FSDP
ROWS = 128
TILE = 256
TILES = 8
LENGTH = TILE * TILES

NT = (((1,), (1,)), ((), ()))


def dot(a, b):
    return jnp.dot(a, b, preferred_element_type=f32)


def dot_nt(a, b):
    return lax.dot_general(a, b, NT, preferred_element_type=f32)


def dot_tn(a, b):
    return lax.dot_general(a, b, (((0,), (0,)), ((), ())), preferred_element_type=f32)


def pack(narrow):
    return jnp.concatenate([narrow[0:64], narrow[64:128]], axis=1)


def unpack(wide):
    return jnp.concatenate([wide[:, 0:64], wide[:, 64:128]], axis=0)


smem = pl.BlockSpec(memory_space=pltpu.SMEM)
vmem = pl.BlockSpec(memory_space=pltpu.VMEM)


def call(kernel, name, outs, scratch, flops, moved, transcendentals, args, scalars=0):
    return pl.pallas_call(
        kernel,
        out_shape=tuple(jax.ShapeDtypeStruct(shape, kind) for shape, kind in outs),
        in_specs=[smem] * scalars + [vmem] * (len(args) - scalars),
        out_specs=(vmem,) * len(outs),
        scratch_shapes=[pltpu.VMEM(shape, kind) for shape, kind in scratch],
        compiler_params=pltpu.CompilerParams(vmem_limit_bytes=48 * 2**20),
        cost_estimate=pl.CostEstimate(
            flops=flops, bytes_accessed=moved, transcendentals=transcendentals
        ),
        name=name,
    )(*args)


def assemble(refs, out):
    for e in range(2):
        own, first, low, high, third = refs[5 * e : 5 * e + 5]
        base = 4 * ROWS * e
        out[base : base + ROWS, :] = own[...]
        out[base + ROWS : base + 2 * ROWS, :] = first[...]
        out[base + 2 * ROWS : base + 3 * ROWS, 0 : D // 2] = low[...]
        out[base + 2 * ROWS : base + 3 * ROWS, D // 2 : D] = high[...]
        out[base + 3 * ROWS : base + 4 * ROWS, :] = third[...]


def put_parts(refs, chunk, value):
    for b in range(2):
        ref = refs[2 * chunk + b]
        ref[...] = value[b * ROWS : (b + 1) * ROWS].astype(ref.dtype)


PARTS = [((ROWS, D), f32)] * 4 + [((ROWS, D), bf16)] * 4
ORDER = (2, 3, 0, 1)


def deal_kernel(weight_ref, small_ref, out_ref):
    small = small_ref[...]

    def piece(kind, head):
        start = kind * D + head * HEAD
        return weight_ref[:, start : start + HEAD]

    for y in range(4):
        for x in range(2):
            for c in range(2):
                shard = 4 * y + 2 * x + c
                twin = shard ^ 2
                out_ref[shard, 0:64, :] = jnp.concatenate(
                    [
                        piece(0, shard), piece(1, shard), piece(0, twin), piece(1, twin),
                        piece(2, shard), piece(2, twin),
                    ],
                    axis=1,
                )
                out_ref[shard, 64:80, :] = small


def first_kernel(shard_ref, *refs):
    pieces, arrived = refs[0:10], refs[10]
    own_ref, other_ref, normed_ref, normal_ref, project_ref, vector_ref, bias_ref = refs[11:18]
    inputs = refs[18]
    assemble(pieces, inputs)
    for r in range(16):
        project_ref[64 * r : 64 * r + 64, :] = arrived[r, 0:64, :]
    rows = [arrived[r, 64:80, :].astype(f32) for r in range(16)]
    for g in range(6):
        vector_ref[g : g + 1, :] = jnp.concatenate(
            [rows[r][0:1, 64 * g : 64 * g + 64] for r in range(16)], axis=1
        )
    shard = shard_ref[0]
    mine = arrived[shard, 64:80, :].astype(f32)[1:2]
    twin = arrived[shard ^ 2, 64:80, :].astype(f32)[1:2]
    bias_ref[0:1, :] = jnp.concatenate([mine[:, 128:], twin[:, 128:]], axis=1)
    zero = jnp.zeros((1, HEAD), f32)
    bias = jnp.concatenate(
        [mine[:, 0:64], zero, twin[:, 0:64], zero, mine[:, 64:128], twin[:, 64:128]], axis=1
    )
    gain = vector_ref[0:1, :]
    offset = vector_ref[1:2, :]
    for chunk in range(4):
        rows = slice(chunk * TILE, (chunk + 1) * TILE)
        normal, unused = normalize(inputs[rows, :].astype(f32))
        normal_ref[rows, :] = normal.astype(bf16)
        normed = (normal * gain + offset).astype(bf16)
        normed_ref[rows, :] = normed
        heads = (dot(normed, project_ref[...]) + bias).astype(bf16)
        for b in range(2):
            block = heads[b * ROWS : (b + 1) * ROWS]
            place = 2 * chunk + b
            own_ref[place, 0:ROWS, :] = block[:, 0:128]
            own_ref[place, ROWS:192, :] = pack(block[:, 256:320])
            other_ref[place, 0:ROWS, :] = block[:, 128:256]
            other_ref[place, ROWS:192, :] = pack(block[:, 320:384])


def first_heads(shard, pieces, arrived):
    return call(
        first_kernel, "first_heads",
        [
            ((8, 192, 128), bf16), ((8, 192, 128), bf16), ((1024, D), bf16), ((1024, D), bf16),
            ((D, 384), bf16), ((8, D), f32), ((8, 512), f32),
        ],
        [((1024, D), bf16)],
        8 * 10**8, 10**7, 10**4, (shard, *pieces, arrived), 1,
    )


def pick(table, a, own_ref, other_ref):
    return jnp.where((a // 2) % 2 == table[16], own_ref[table[a]], other_ref[table[a]])


def put(table, a, own_ref, other_ref, value):
    mine = (a // 2) % 2 == table[16]

    @pl.when(mine)
    def _():
        own_ref[table[a]] = value

    @pl.when(jnp.logical_not(mine))
    def _():
        other_ref[table[a]] = value


def stage_blocks(table, slope_ref, own_ref, other_ref, qa, ka, emit_rest):
    lane = lax.broadcasted_iota(jnp.int32, (ROWS, HEAD), 1)
    row = lax.broadcasted_iota(jnp.int32, (ROWS, HEAD), 0)
    ones = jnp.where(lane < 3, 1.0, 0.0).astype(bf16)
    slope = slope_ref[0]
    for a in range(HEADS):
        block = pick(table, a, own_ref, other_ref)
        rows = slice(a * ROWS, (a + 1) * ROWS)
        place = slope * (row + (a * ROWS - LENGTH // 2)).astype(f32)
        high = place.astype(bf16)
        rest = place - high.astype(f32)
        middle = rest.astype(bf16)
        low = (rest - middle.astype(f32)).astype(bf16)
        extra = jnp.where(
            lane == 0,
            high.astype(f32),
            jnp.where(
                lane == 1, middle.astype(f32), jnp.where(lane == 2, low.astype(f32), 0.0)
            ),
        ).astype(bf16)
        key = block[0:ROWS, HEAD : 2 * HEAD]
        scaled = (block[0:ROWS, 0:HEAD].astype(f32) * score_scale).astype(bf16)
        qa[rows, :] = jnp.concatenate([scaled, ones], axis=1)
        ka[rows, :] = jnp.concatenate([key, extra], axis=1)
        emit_rest(a, rows, key, unpack(block[ROWS:192]))


def fold(tile, op):
    parts = [tile[8 * g : 8 * g + 8] for g in range(TILE // 8)]
    while len(parts) > 1:
        parts = [op(parts[2 * g], parts[2 * g + 1]) for g in range(len(parts) // 2)]
    return parts[0]


def future():
    key = lax.broadcasted_iota(jnp.int32, (TILE, TILE), 0)
    query = lax.broadcasted_iota(jnp.int32, (TILE, TILE), 1)
    return key > query


def forward_kernel(
    table, slope_ref, own_ref, other_ref, out_own, out_other, lse_ref, qa, ka, vt, s_sc, p_sc
):
    def rest(a, rows, key, value):
        vt[:, rows] = value.astype(f32).T.astype(bf16)

    stage_blocks(table, slope_ref, own_ref, other_ref, qa, ka, rest)
    hidden = future()
    for i in range(TILES):
        q = qa[i * TILE : (i + 1) * TILE, :]
        peak = None
        for j in range(i + 1):
            s = dot_nt(ka[j * TILE : (j + 1) * TILE, :], q)
            if j == i:
                s = jnp.where(hidden, -1e30, s)
            s_sc[j * TILE : (j + 1) * TILE, :] = s
            top = fold(s, jnp.maximum)
            peak = top if peak is None else jnp.maximum(peak, top)
        peak = jnp.max(peak, axis=0, keepdims=True)
        total = None
        for j in range(i + 1):
            p = jnp.exp(s_sc[j * TILE : (j + 1) * TILE, :] - peak)
            p_sc[j * TILE : (j + 1) * TILE, :] = p.astype(bf16)
            part = fold(p, jnp.add)
            total = part if total is None else total + part
        total = jnp.sum(total, axis=0, keepdims=True)
        n = (i + 1) * TILE
        out = dot(vt[:, 0:n], p_sc[0:n, :]) / total
        out = out.T.astype(bf16)
        put(table, 2 * i, out_own, out_other, pack(out[0:ROWS]))
        put(table, 2 * i + 1, out_own, out_other, pack(out[ROWS:]))
        lse_ref[i] = peak + jnp.log(total)


def attention_forward(table, slope, own, other):
    return call(
        forward_kernel, "attention_forward",
        [((8, 64, 128), bf16), ((8, 64, 128), bf16), ((TILES, 1, TILE), f32)],
        [
            ((LENGTH, 2 * HEAD), bf16), ((LENGTH, 2 * HEAD), bf16), ((HEAD, LENGTH), bf16),
            ((LENGTH, TILE), f32), ((LENGTH, TILE), bf16),
        ],
        3 * 10**9, 2 * 10**6, 24 * 10**5, (table, slope, own, other), 2,
    )


def backward_kernel(
    table, slope_ref, own_ref, other_ref, grad_own, grad_other, lse_ref,
    out_own, out_other, sum_ref,
    qa, ka, va, kt, da, dq, dk, dv, p_sc, dp_sc, ds_sc,
):
    def rest(a, rows, key, value):
        va[rows, :] = value
        kt[:, rows] = key.astype(f32).T.astype(bf16)
        da[rows, :] = unpack(pick(table, a, grad_own, grad_other))

    stage_blocks(table, slope_ref, own_ref, other_ref, qa, ka, rest)
    hidden = future()
    for i in range(TILES):
        here = slice(i * TILE, (i + 1) * TILE)
        q = qa[here, :]
        q_plain = q[:, 0:HEAD]
        grad = da[here, :]
        lse = lse_ref[i]
        delta = None
        for j in range(i + 1):
            there = slice(j * TILE, (j + 1) * TILE)
            s = dot_nt(ka[there, :], q)
            if j == i:
                s = jnp.where(hidden, -1e30, s)
            p = jnp.exp(s - lse)
            dp = dot_nt(va[there, :], grad)
            p_sc[there, :] = p
            dp_sc[there, :] = dp
            part = fold(p * dp, jnp.add)
            delta = part if delta is None else delta + part
            value = dot(p.astype(bf16), grad)
            dv[there, :] = value if j == i else dv[there, :] + value
        delta = jnp.sum(delta, axis=0, keepdims=True)
        for j in range(i + 1):
            there = slice(j * TILE, (j + 1) * TILE)
            ds = (p_sc[there, :] * (dp_sc[there, :] - delta)).astype(bf16)
            ds_sc[there, :] = ds
            key = dot(ds, q_plain)
            dk[there, :] = key if j == i else dk[there, :] + key
        n = (i + 1) * TILE
        dq[here, :] = (dot(kt[:, 0:n], ds_sc[0:n, :]) * score_scale).T
    total = None
    for a in range(HEADS):
        rows = slice(a * ROWS, (a + 1) * ROWS)
        query = dq[rows, :].astype(bf16)
        value = dv[rows, :].astype(bf16)
        pair = jnp.concatenate([query, dk[rows, :].astype(bf16)], axis=1)
        put(table, a, out_own, out_other, jnp.concatenate([pair, pack(value)], axis=0))
        both = jnp.concatenate([query.astype(f32), value.astype(f32)], axis=1)
        both = jnp.sum(both, axis=0, keepdims=True)
        total = both if total is None else total + both
    sum_ref[0:1, :] = total


def attention_backward(table, slope, own, other, grad_own, grad_other, lse):
    narrow = ((LENGTH, HEAD), f32)
    return call(
        backward_kernel, "attention_backward",
        [((8, 192, 128), bf16), ((8, 192, 128), bf16), ((8, 128), f32)],
        [
            ((LENGTH, 2 * HEAD), bf16), ((LENGTH, 2 * HEAD), bf16), ((LENGTH, HEAD), bf16),
            ((HEAD, LENGTH), bf16), ((LENGTH, HEAD), bf16), narrow, narrow, narrow,
            ((LENGTH, TILE), f32), ((LENGTH, TILE), f32), ((LENGTH, TILE), bf16),
        ],
        6 * 10**9, 3 * 10**6, 24 * 10**5,
        (table, slope, own, other, grad_own, grad_other, lse), 2,
    )


def output_kernel(own_ref, other_ref, weight_ref, rows_ref, *refs):
    parts, mixed_ref = refs[0:8], refs[8]
    weight = jnp.concatenate([weight_ref[...], rows_ref[0:64, :]], axis=0)
    for chunk in ORDER:
        blocks = [
            jnp.concatenate([unpack(own_ref[b]), unpack(other_ref[b])], axis=1)
            for b in (2 * chunk, 2 * chunk + 1)
        ]
        mixed = jnp.concatenate(blocks, axis=0)
        mixed_ref[chunk * TILE : (chunk + 1) * TILE, :] = mixed
        put_parts(parts, chunk, dot(mixed, weight))


def output_parts(own, other, weight, rows):
    outs = call(
        output_kernel, "output_parts", PARTS + [((1024, 128), bf16)], [],
        27 * 10**7, 4 * 10**6, 0, (own, other, weight, rows),
    )
    return outs[0:8], outs[8]


def feed_kernel(*refs):
    pieces, cotangent_pieces = refs[0:10], refs[10:20]
    up_ref, down_ref, rows_ref, bias_ref = refs[20:24]
    parts, act_ref, grad_ref, second_ref, cotangent_ref = refs[24:32], *refs[32:36]
    assemble(pieces, second_ref)
    assemble(cotangent_pieces, cotangent_ref)
    bias = bias_ref[0:1, :]
    for chunk in ORDER:
        rows = slice(chunk * TILE, (chunk + 1) * TILE)
        cotangents = cotangent_ref[rows, :]
        back = jnp.concatenate(
            [dot_nt(cotangents, down_ref[...]), dot_nt(cotangents, rows_ref[64:320, :])], axis=1
        )
        up = dot(second_ref[rows, :], up_ref[...]) + bias
        square = up * up
        bend = jnp.tanh(0.7978845608028654 * (up + 0.044715 * square * up))
        half = 0.5 * (1.0 + bend)
        act_ref[rows, :] = (up * half).astype(bf16)
        slope = half + 0.5 * up * (1.0 - bend * bend) * (
            0.7978845608028654 * (1.0 + 0.134145 * square)
        )
        grad = (back * slope).astype(bf16)
        grad_ref[rows, :] = grad
        put_parts(parts, chunk, dot_nt(grad, up_ref[...]))


def feed_parts(pieces, cotangent_pieces, up, down, rows, bias):
    outs = call(
        feed_kernel, "feed_parts",
        PARTS + [((1024, 512), bf16)] * 2 + [((1024, D), bf16)] * 2, [],
        32 * 10**8, 2 * 10**7, 5 * 10**5, (*pieces, *cotangent_pieces, up, down, rows, bias),
    )
    return outs[0:8], outs[8], outs[9], outs[10], outs[11]


def out_kernel(act_ref, down_ref, rows_ref, *parts):
    for chunk in ORDER:
        act = act_ref[chunk * TILE : (chunk + 1) * TILE, :]
        value = dot(act[:, 0:256], down_ref[...]) + dot(act[:, 256:512], rows_ref[64:320, :])
        put_parts(parts, chunk, value)


def out_parts(act, down, rows):
    return call(out_kernel, "out_parts", PARTS, [], 11 * 10**8, 5 * 10**6, 0, (act, down, rows))


def mixed_kernel(*refs):
    pieces, weight_ref, rows_ref = refs[0:10], refs[10], refs[11]
    own_ref, other_ref, all_ref = refs[12:15]
    assemble(pieces, all_ref)
    weight = jnp.concatenate([weight_ref[...], rows_ref[0:64, :]], axis=0)
    for chunk in range(4):
        grads = dot_nt(all_ref[chunk * TILE : (chunk + 1) * TILE, :], weight).astype(bf16)
        for b in range(2):
            block = grads[b * ROWS : (b + 1) * ROWS]
            own_ref[2 * chunk + b] = pack(block[:, 0:64])
            other_ref[2 * chunk + b] = pack(block[:, 64:128])


def mixed_back(pieces, weight, rows):
    return call(
        mixed_kernel, "mixed_back",
        [((8, 64, 128), bf16), ((8, 64, 128), bf16), ((1024, D), bf16)], [],
        27 * 10**7, 4 * 10**6, 0, (*pieces, weight, rows),
    )


def last_kernel(own_ref, other_ref, project_ref, normal_ref, *refs):
    parts, joined_ref, sum_ref = refs[0:8], refs[8], refs[9]
    gain = None
    for chunk in ORDER:
        rows = slice(chunk * TILE, (chunk + 1) * TILE)
        blocks = []
        for b in (2 * chunk, 2 * chunk + 1):
            own, other = own_ref[b], other_ref[b]
            blocks.append(
                jnp.concatenate(
                    [own[0:ROWS], other[0:ROWS], unpack(own[ROWS:192]), unpack(other[ROWS:192])],
                    axis=1,
                )
            )
        joined = jnp.concatenate(blocks, axis=0)
        joined_ref[rows, :] = joined
        value = dot_nt(joined, project_ref[...])
        put_parts(parts, chunk, value)
        tilted = jnp.sum(value * normal_ref[rows, :].astype(f32), axis=0, keepdims=True)
        plain = jnp.sum(value, axis=0, keepdims=True)
        gain = tilted if gain is None else gain + tilted
        shift_sum = plain if chunk == ORDER[0] else shift_sum + plain
    sum_ref[0:1, :] = gain
    sum_ref[1:2, :] = shift_sum


def last_parts(own, other, project, normal):
    outs = call(
        last_kernel, "last_parts", PARTS + [((1024, 384), bf16), ((8, D), f32)], [],
        8 * 10**8, 7 * 10**6, 0, (own, other, project, normal),
    )
    return outs[0:8], outs[8], outs[9]


def landed(refs):
    mine, core, next_low, next_high, back_low, back_high = [ref[...].astype(f32) for ref in refs]
    near = jnp.concatenate([next_low, next_high], axis=1)
    back = jnp.concatenate([back_low, back_high], axis=1)
    return mine + core + near + back


def middle_kernel(*refs):
    input_ref, vector_ref, mid_ref, normal_ref, inverse_ref, normed_ref = refs[6:12]
    mid = input_ref[...].astype(f32) + (landed(refs[0:6]) + vector_ref[2:3, :])
    normal, inverse = normalize(mid)
    mid_ref[...] = mid
    normal_ref[...] = normal
    inverse_ref[...] = inverse
    normed_ref[...] = (normal * vector_ref[3:4, :] + vector_ref[4:5, :]).astype(bf16)


def middle(ends, inputs, vectors):
    return call(
        middle_kernel, "middle",
        [((ROWS, D), f32), ((ROWS, D), f32), ((ROWS, 1), f32), ((ROWS, D), bf16)], [],
        10**6, 3 * 10**6, 0, (*ends, inputs, vectors),
    )


def middle_back_kernel(*refs):
    cotangent_ref, vector_ref, normal_ref, inverse_ref, grad_ref, branch_ref, sum_ref = refs[6:13]
    second = landed(refs[0:6])
    normal = normal_ref[...]
    cotangent = cotangent_ref[...].astype(f32)
    grad = cotangent + norm_back(second, vector_ref[3:4, :], normal, inverse_ref[...])
    grad_ref[...] = grad
    branch = grad.astype(bf16)
    branch_ref[...] = branch
    sum_ref[0:1, :] = jnp.sum(second * normal, axis=0, keepdims=True)
    sum_ref[1:2, :] = jnp.sum(second, axis=0, keepdims=True)
    sum_ref[2:3, :] = jnp.sum(branch.astype(f32), axis=0, keepdims=True)
    sum_ref[3:4, :] = jnp.sum(cotangent, axis=0, keepdims=True)


def middle_back(ends, cotangent, vectors, normal, inverse):
    return call(
        middle_back_kernel, "middle_back",
        [((ROWS, D), f32), ((ROWS, D), bf16), ((8, D), f32)], [],
        10**6, 3 * 10**6, 0, (*ends, cotangent, vectors, normal, inverse),
    )


def block_kernel(*refs):
    mid_ref, vector_ref, out_ref = refs[6:9]
    out_ref[...] = (mid_ref[...] + landed(refs[0:6]) + vector_ref[5:6, :]).astype(bf16)


def block_end(ends, mid, vectors):
    return call(
        block_kernel, "block_end", [((ROWS, D), bf16)], [], 10**6, 2 * 10**6, 0,
        (*ends, mid, vectors),
    )[0]


def input_kernel(*refs):
    input_ref, vector_ref, grad_ref, out_ref = refs[6:10]
    normal, inverse = normalize(input_ref[...].astype(f32))
    out_ref[...] = grad_ref[...] + norm_back(
        landed(refs[0:6]), vector_ref[0:1, :], normal, inverse
    )


def input_end(ends, inputs, vectors, grad):
    return call(
        input_kernel, "input_end", [((ROWS, D), f32)], [], 10**6, 3 * 10**6, 0,
        (*ends, inputs, vectors, grad),
    )[0]


def shift(value, axis, step):
    size = lax.axis_size(axis)
    return lax.ppermute(value, axis, [(i, (i + step) % size) for i in range(size)])


def gather(own):
    half = own.shape[1] // 2
    third = shift(own, "y", 1)
    first = shift(own, "y", -1)
    low = shift(third[:, :half], "y", 1)
    high = shift(first[:, half:], "y", -1)
    mine = [own, first, low, high, third]
    return mine + [shift(block, "c", 1) for block in mine]


def scatter(parts):
    mine, other = parts[0:4], parts[4:8]
    half = D // 2
    core = [shift(block, "c", 1) for block in other]

    def join(d, columns, more=None):
        value = mine[d][:, columns] + core[d][:, columns].astype(f32)
        return (value if more is None else value + more.astype(f32)).astype(bf16)

    low, high = slice(0, half), slice(half, D)
    to_next = shift(join(2, low), "y", 1)
    to_last = shift(join(2, high), "y", -1)
    next_high = shift(join(1, high), "y", 1)
    back_low = shift(join(3, low), "y", -1)
    next_low = shift(join(1, low, to_next), "y", 1)
    back_high = shift(join(3, high, to_last), "y", -1)
    return (mine[0], core[0], next_low, next_high, back_low, back_high)


def exchange(value, axes):
    return lax.all_to_all(value, axes, split_axis=0, concat_axis=0, tiled=True)


def after(value, *others):
    return lax.optimization_barrier((value, *others))[0]


def normalize(values):
    centre = jnp.mean(values, axis=-1, keepdims=True)
    centred = values - centre
    spread = jnp.mean(centred * centred, axis=-1, keepdims=True)
    inverse = lax.rsqrt(spread + epsilon)
    return centred * inverse, inverse


def norm_back(grad, gain, normal, inverse):
    scaled = grad * gain
    return inverse * (
        scaled
        - jnp.mean(scaled, axis=-1, keepdims=True)
        - normal * jnp.mean(scaled * normal, axis=-1, keepdims=True)
    )


def on_device(
    block_input,
    first_gain,
    first_shift,
    attention_weight,
    query_bias,
    value_bias,
    output_weight,
    output_bias,
    second_gain,
    second_shift,
    upward_weight,
    upward_bias,
    downward_weight,
    downward_bias,
    cotangent,
):
    y = lax.axis_index("y")
    xh = lax.axis_index("xh")
    c = lax.axis_index("c")
    shard = 4 * y + 2 * xh + c
    place = np.arange(16)
    table = jnp.append(4 * ((place % 2) ^ c) + (place // 4 - y) % 4, xh).astype(jnp.int32)
    slope = jnp.exp2(-8.0 * (shard + 1).astype(f32) / HEADS)[None]

    with jax.named_scope("weights_attention"):
        small = jnp.concatenate(
            [
                first_gain, first_shift, output_bias, second_gain, second_shift, downward_bias,
                query_bias, value_bias, upward_bias,
            ]
        ).reshape(2, 384)
        small = jnp.pad(small, ((0, 14), (0, 0)))
        payload = call(
            deal_kernel, "deal", [((16, 80, 384), bf16)], [], 0, 2 * 10**6, 0,
            (attention_weight, small),
        )[0]
        arrived = exchange(payload, FSDP)

    with jax.named_scope("first"):
        inputs = gather(block_input)
        heads_own, heads_other, normed_first, normal_first, project, vectors, bias_up = first_heads(
            shard[None].astype(jnp.int32), inputs, arrived
        )
        heads_arrived = shift(heads_other, "xh", 1)
    with jax.named_scope("weights_upward"):
        up_split = after(upward_weight, arrived)
        up_split = up_split.reshape(64, 4, 2, 2, 256).transpose(1, 2, 3, 0, 4)
        up_paired = jnp.concatenate([up_split, up_split[:, ::-1]], axis=-1)
        upward_pair = exchange(up_paired.reshape(16, 64, 512), FSDP).reshape(D, 512)
    with jax.named_scope("weights_pair"):
        own_rows = jnp.concatenate([output_weight, downward_weight], axis=0)
        other_rows = shift(after(own_rows, heads_arrived), "xh", 1)
    with jax.named_scope("cotangents"):
        cotangents = gather(after(cotangent, arrived))

    with jax.named_scope("attention"):
        mixed_own, mixed_other, lse = attention_forward(table, slope, heads_own, heads_arrived)
        mixed_arrived = shift(mixed_other, "xh", 1)
    with jax.named_scope("output"):
        parts, mixed_pair = output_parts(mixed_own, mixed_arrived, output_weight, other_rows)
        residual_mid, normal_second, inverse_second, normed_second = middle(
            scatter(parts), block_input, vectors
        )

    with jax.named_scope("feed"):
        parts, activated, upward_grad, seconds, all_cotangents = feed_parts(
            gather(normed_second), cotangents, upward_pair, downward_weight, other_rows, bias_up
        )
        mid_grad, branch_grad, sums = middle_back(
            scatter(parts), cotangent, vectors, normal_second, inverse_second
        )

    with jax.named_scope("mixed_back"):
        grad_own, grad_other, branch_grads = mixed_back(
            gather(branch_grad), output_weight, other_rows
        )
        grad_arrived = shift(grad_other, "xh", 1)

    with jax.named_scope("feed_out"):
        block_output = block_end(
            scatter(out_parts(activated, downward_weight, other_rows)), residual_mid, vectors
        )

    with jax.named_scope("upward_gradients"):
        upward_weight_grad = dot_tn(seconds, upward_grad).astype(bf16)
        upward_bias_grad = jnp.sum(upward_grad.astype(f32), axis=0).astype(bf16)
        quads = sums[0:4].astype(bf16).reshape(4, 16, 64).transpose(1, 0, 2).reshape(16, 2, 128)
        extra = jnp.concatenate(
            [
                quads,
                jnp.broadcast_to(upward_bias_grad.reshape(1, 4, 128), (16, 4, 128)),
                jnp.zeros((16, 2, 128), bf16),
            ],
            axis=1,
        )
        extra = jnp.broadcast_to(extra[:, None], (16, 8, 8, 128)).reshape(1024, 128)
        shares = jnp.concatenate([upward_weight_grad, extra], axis=-1).reshape(128, 8, 640)
        arrived_up = exchange(shares, FSDP + SEQ)
        wide_up = arrived_up.reshape(4, 2, 2, 8, 8, 640).astype(f32)
        up_sum = jnp.sum(wide_up[..., :512], axis=3)
        up_total = up_sum[..., :256] + up_sum[:, ::-1, :, :, 256:]
        up_total = up_total.transpose(3, 0, 1, 2, 4).reshape(8, FF).astype(bf16)
        small_sum = jnp.sum(wide_up[..., 512:], axis=3)
        four_total = jnp.sum(small_sum[:, :, :, 0:2], axis=(0, 1, 2))
        bias_rows = small_sum.reshape(16, 8, 128)[:, 2:6].reshape(16, 512)
        bias_total = (
            lax.dynamic_index_in_dim(bias_rows, shard, 0, keepdims=False)[:256]
            + lax.dynamic_index_in_dim(bias_rows, shard ^ 2, 0, keepdims=False)[256:]
        )
    with jax.named_scope("row_gradients"):
        downward_grad = dot_tn(activated, all_cotangents)
        output_grad = dot_tn(mixed_pair, branch_grads)
        rows_other = jnp.concatenate([output_grad[64:], downward_grad[256:]], axis=0).astype(bf16)
        rows_arrived = shift(rows_other, "xh", 1)
        wide_rows = rows_arrived.astype(f32)
        output_sum = (output_grad[:64] + wide_rows[:64]).astype(bf16).reshape(8, 8, D)
        downward_sum = (downward_grad[:256] + wide_rows[64:]).astype(bf16).reshape(8, 32, D)
        rows_all = exchange(jnp.concatenate([output_sum, downward_sum], axis=1), SEQ)
        rows_total = jnp.sum(rows_all.astype(f32), axis=0).astype(bf16)
    with jax.named_scope("early_gradients"):
        early = jnp.concatenate([rows_total, up_total.reshape(32, D)], axis=0)
        early_all = exchange(jnp.broadcast_to(early[None], (8, 72, D)), SEQ)
        wide_early = early_all.astype(f32)
        output_weight_gradient = wide_early[:, :8].reshape(64, D)
        downward_weight_gradient = wide_early[:, 8:40].reshape(256, D)
        upward_weight_gradient = wide_early[:, 40:].reshape(64, FF)

    with jax.named_scope("attention_back"):
        back_own, back_other, token_sums = attention_backward(
            table, slope, heads_own, heads_arrived, grad_own, grad_arrived, lse
        )
        back_other = after(back_other, arrived_up, rows_arrived)
        back_arrived = shift(back_other, "xh", 1)
    with jax.named_scope("first_back"):
        back_arrived = after(back_arrived, rows_all)
        parts, joined, last_sums = last_parts(back_own, back_arrived, project, normal_first)
        input_gradient = input_end(scatter(parts), block_input, vectors, mid_grad)
    with jax.named_scope("attention_gradients"):
        weight_grad = dot_tn(normed_first, joined).astype(bf16)
        quads = last_sums[0:2].astype(bf16).reshape(2, 16, 64).transpose(1, 0, 2)
        extra = jnp.concatenate(
            [
                quads.reshape(16, 1, 128),
                jnp.broadcast_to(token_sums[None, 0:1].astype(bf16), (16, 1, 128)),
                jnp.zeros((16, 6, 128), bf16),
            ],
            axis=1,
        )
        extra = jnp.broadcast_to(extra[:, None], (16, 8, 8, 128)).reshape(1024, 128)
        shares = jnp.concatenate([weight_grad, extra], axis=-1).reshape(128, 8, 512)
        arrived_last = exchange(shares, FSDP + SEQ).reshape(4, 2, 2, 8, 8, 512).astype(f32)
        last_sum = jnp.sum(arrived_last, axis=3)
        twin_sum = last_sum[:, ::-1]
        pair_total = last_sum[..., 0:128] + twin_sum[..., 128:256]
        value_total = last_sum[..., 256:320] + twin_sum[..., 320:384]
        last_total = jnp.concatenate([pair_total, value_total], axis=-1)
        last_total = last_total.reshape(16, 8, 3, HEAD).transpose(1, 2, 0, 3).reshape(8, 3 * D)
        late = last_total.astype(bf16).reshape(24, D)
        late = after(late, early_all)
        late_all = exchange(jnp.broadcast_to(late[None], (8, 24, D)), SEQ).astype(f32)
        attention_weight_gradient = late_all.reshape(64, 3 * D)
        last_small = last_sum[..., 384:].reshape(16, 8, 128)
        first_total = jnp.sum(last_small[:, 0], axis=0)
        bias_pair = lax.dynamic_index_in_dim(last_small[:, 1], shard, 0, keepdims=False)

    return (
        block_output,
        input_gradient,
        first_total[:64],
        first_total[64:],
        attention_weight_gradient,
        bias_pair[:64],
        bias_pair[64:],
        output_weight_gradient,
        four_total[1, :64],
        four_total[0, :64],
        four_total[0, 64:],
        upward_weight_gradient,
        bias_total,
        downward_weight_gradient,
        four_total[1, 64:],
    )


def solution(mesh):
    grid = Mesh(mesh.devices.reshape(4, 2, 4, 2, 2), ALL)
    tokens = P(ALL, None)
    rows = P(FSDP, None)
    line = P(FSDP)
    return jax.shard_map(
        on_device,
        mesh=grid,
        in_specs=(
            tokens, line, line, rows, line, line, rows, line, line, line, rows, line, rows, line,
            tokens,
        ),
        out_specs=(
            tokens, tokens, line, line, rows, line, line, rows, line, line, line, rows, line, rows,
            line,
        ),
        check_vma=False,
    )
```

```python
import jax
import jax.numpy as jnp
import numpy as np
from jax import lax
from jax.experimental import pallas as pl
from jax.experimental.pallas import tpu as pltpu
from jax.sharding import Mesh
from jax.sharding import PartitionSpec as P

D = 1024
HEADS = 16
HEAD = 64
FF = 4096

epsilon = 1e-05
score_scale = 0.125
bf16 = jnp.bfloat16
f32 = jnp.float32

SEQ = ("z", "xl")
FSDP = ("y", "xh", "c")
ALL = SEQ + FSDP
ROWS = 128
TILE = 256
TILES = 8
LENGTH = TILE * TILES

NT = (((1,), (1,)), ((), ()))


def dot(a, b):
    return jnp.dot(a, b, preferred_element_type=f32)


def dot_nt(a, b):
    return lax.dot_general(a, b, NT, preferred_element_type=f32)


def dot_tn(a, b):
    return lax.dot_general(a, b, (((0,), (0,)), ((), ())), preferred_element_type=f32)


def pack(narrow):
    return jnp.concatenate([narrow[0:64], narrow[64:128]], axis=1)


def unpack(wide):
    return jnp.concatenate([wide[:, 0:64], wide[:, 64:128]], axis=0)


smem = pl.BlockSpec(memory_space=pltpu.SMEM)
vmem = pl.BlockSpec(memory_space=pltpu.VMEM)


def call(kernel, name, outs, scratch, flops, moved, transcendentals, args, scalars=0, pieces=0):
    rest = len(args) - scalars - pieces
    return pl.pallas_call(
        kernel,
        out_shape=tuple(jax.ShapeDtypeStruct(shape, kind) for shape, kind in outs),
        in_specs=[smem] * scalars + [pl.BlockSpec(memory_space=pl.ANY)] * pieces + [vmem] * rest,
        out_specs=(vmem,) * len(outs),
        scratch_shapes=[
            pltpu.VMEM(*item) if isinstance(item, tuple) else item for item in scratch
        ],
        compiler_params=pltpu.CompilerParams(vmem_limit_bytes=60 * 2**20),
        cost_estimate=pl.CostEstimate(
            flops=flops, bytes_accessed=moved, transcendentals=transcendentals
        ),
        name=name,
    )(*args)


def place(table, p):
    return pl.multiple_of(table[p] * ROWS, ROWS)


def assemble(table, refs, out, sems):
    copies = [
        pltpu.make_async_copy(refs[p], out.at[pl.ds(place(table, p), ROWS), :], sems.at[p])
        for p in range(8)
    ]
    for copy in copies:
        copy.start()
    return copies


def rows_of(table, ref, p):
    return jnp.concatenate(
        [ref[pl.ds(place(table, p + b), ROWS), :] for b in range(2)], axis=0
    )


def set_rows(table, ref, p, value):
    for b in range(2):
        ref[pl.ds(place(table, p + b), ROWS), :] = value[b * ROWS : (b + 1) * ROWS]


def put_parts(mine_ref, other_ref, chunk, value):
    ref = mine_ref if chunk < 2 else other_ref
    for b in range(2):
        ref[2 * (chunk % 2) + b] = value[b * ROWS : (b + 1) * ROWS].astype(ref.dtype)


PARTS = [((4, ROWS, D), f32), ((4, ROWS, D), bf16)]
ORDER = (2, 3, 0, 1)


def deal_kernel(weight_ref, small_ref, up_ref, out_ref, up_out):
    small = small_ref[...]

    def piece(kind, head):
        start = kind * D + head * HEAD
        return weight_ref[:, start : start + HEAD]

    for y in range(4):
        for x in range(2):
            for c in range(2):
                shard = 4 * y + 2 * x + c
                twin = shard ^ 2
                out_ref[shard, 0:64, :] = jnp.concatenate(
                    [
                        piece(0, shard), piece(1, shard), piece(0, twin), piece(1, twin),
                        piece(2, shard), piece(2, twin),
                    ],
                    axis=1,
                )
                out_ref[shard, 64:80, :] = small
                up_out[shard, :, 0:256] = up_ref[:, 256 * shard : 256 * shard + 256]
                up_out[shard, :, 256:512] = up_ref[:, 256 * twin : 256 * twin + 256]


def first_kernel(shard_ref, *refs):
    inputs, arrived = refs[0:2]
    own_ref, other_ref, normed_ref, normal_ref, project_ref, vector_ref, bias_ref = refs[2:9]
    for r in range(16):
        project_ref[64 * r : 64 * r + 64, :] = arrived[r, 0:64, :]
    rows = [arrived[r, 64:80, :].astype(f32) for r in range(16)]
    for g in range(6):
        vector_ref[g : g + 1, :] = jnp.concatenate(
            [rows[r][0:1, 64 * g : 64 * g + 64] for r in range(16)], axis=1
        )
    shard = shard_ref[0]
    mine = arrived[shard, 64:80, :].astype(f32)[1:2]
    twin = arrived[shard ^ 2, 64:80, :].astype(f32)[1:2]
    bias_ref[0:1, :] = jnp.concatenate([mine[:, 128:], twin[:, 128:]], axis=1)
    zero = jnp.zeros((1, HEAD), f32)
    bias = jnp.concatenate(
        [mine[:, 0:64], zero, twin[:, 0:64], zero, mine[:, 64:128], twin[:, 64:128]], axis=1
    )
    gain = vector_ref[0:1, :]
    offset = vector_ref[1:2, :]
    for chunk in range(4):
        rows = slice(chunk * TILE, (chunk + 1) * TILE)
        normal, unused = normalize(inputs[rows, :].astype(f32))
        normal_ref[rows, :] = normal.astype(bf16)
        normed = (normal * gain + offset).astype(bf16)
        normed_ref[rows, :] = normed
        heads = (dot(normed, project_ref[...]) + bias).astype(bf16)
        for b in range(2):
            block = heads[b * ROWS : (b + 1) * ROWS]
            k = 2 * chunk + b
            own_ref[k, 0:ROWS, :] = block[:, 0:128]
            own_ref[k, ROWS:192, :] = pack(block[:, 256:320])
            other_ref[k, 0:ROWS, :] = block[:, 128:256]
            other_ref[k, ROWS:192, :] = pack(block[:, 320:384])


def first_heads(shard, inputs, arrived):
    return call(
        first_kernel, "first_heads",
        [
            ((8, 192, 128), bf16), ((8, 192, 128), bf16), ((1024, D), bf16), ((1024, D), bf16),
            ((D, 384), bf16), ((8, D), f32), ((8, 512), f32),
        ],
        [], 8 * 10**8, 10**7, 10**4, (shard, inputs, arrived), 1,
    )


def block_of(a):
    return 2 * (a // 4) + a % 2


def pick(half, a, own_ref, other_ref):
    return jnp.where((a // 2) % 2 == half[0], own_ref[block_of(a)], other_ref[block_of(a)])


def put(half, a, own_ref, other_ref, value):
    mine = (a // 2) % 2 == half[0]
    own_ref[jnp.where(mine, block_of(a), 8)] = value
    other_ref[jnp.where(mine, 8, block_of(a))] = value


def stage_blocks(table, slope_ref, own_ref, other_ref, qa, ka, emit_rest):
    lane = lax.broadcasted_iota(jnp.int32, (ROWS, HEAD), 1)
    row = lax.broadcasted_iota(jnp.int32, (ROWS, HEAD), 0)
    ones = jnp.where(lane < 3, 1.0, 0.0).astype(bf16)
    slope = slope_ref[0]
    for a in range(HEADS):
        block = pick(table, a, own_ref, other_ref)
        rows = slice(a * ROWS, (a + 1) * ROWS)
        place = slope * (row + (a * ROWS - LENGTH // 2)).astype(f32)
        high = place.astype(bf16)
        rest = place - high.astype(f32)
        middle = rest.astype(bf16)
        low = (rest - middle.astype(f32)).astype(bf16)
        extra = jnp.where(
            lane == 0,
            high.astype(f32),
            jnp.where(
                lane == 1, middle.astype(f32), jnp.where(lane == 2, low.astype(f32), 0.0)
            ),
        ).astype(bf16)
        key = block[0:ROWS, HEAD : 2 * HEAD]
        scaled = (block[0:ROWS, 0:HEAD].astype(f32) * score_scale).astype(bf16)
        qa[rows, :] = jnp.concatenate([scaled, ones], axis=1)
        ka[rows, :] = jnp.concatenate([key, extra], axis=1)
        emit_rest(a, rows, key, unpack(block[ROWS:192]))


def fold(tile, op):
    parts = [tile[8 * g : 8 * g + 8] for g in range(TILE // 8)]
    while len(parts) > 1:
        parts = [op(parts[2 * g], parts[2 * g + 1]) for g in range(len(parts) // 2)]
    return parts[0]


def future():
    key = lax.broadcasted_iota(jnp.int32, (TILE, TILE), 0)
    query = lax.broadcasted_iota(jnp.int32, (TILE, TILE), 1)
    return key > query


def forward_kernel(
    table, slope_ref, own_ref, other_ref, out_own, out_other, lse_ref, qa, ka, vt, s_sc, p_sc
):
    def rest(a, rows, key, value):
        vt[:, rows] = value.astype(f32).T.astype(bf16)

    stage_blocks(table, slope_ref, own_ref, other_ref, qa, ka, rest)
    hidden = future()
    for i in range(TILES):
        q = qa[i * TILE : (i + 1) * TILE, :]
        peak = None
        for j in range(i + 1):
            s = dot_nt(ka[j * TILE : (j + 1) * TILE, :], q)
            if j == i:
                s = jnp.where(hidden, -1e30, s)
            s_sc[j * TILE : (j + 1) * TILE, :] = s
            top = fold(s, jnp.maximum)
            peak = top if peak is None else jnp.maximum(peak, top)
        peak = jnp.max(peak, axis=0, keepdims=True)
        total = None
        for j in range(i + 1):
            p = jnp.exp(s_sc[j * TILE : (j + 1) * TILE, :] - peak)
            p_sc[j * TILE : (j + 1) * TILE, :] = p.astype(bf16)
            part = fold(p, jnp.add)
            total = part if total is None else total + part
        total = jnp.sum(total, axis=0, keepdims=True)
        n = (i + 1) * TILE
        out = dot(vt[:, 0:n], p_sc[0:n, :]) / total
        out = out.T.astype(bf16)
        put(table, 2 * i, out_own, out_other, pack(out[0:ROWS]))
        put(table, 2 * i + 1, out_own, out_other, pack(out[ROWS:]))
        lse_ref[i] = peak + jnp.log(total)


def attention_forward(table, slope, own, other):
    return call(
        forward_kernel, "attention_forward",
        [((9, 64, 128), bf16), ((9, 64, 128), bf16), ((TILES, 1, TILE), f32)],
        [
            ((LENGTH, 2 * HEAD), bf16), ((LENGTH, 2 * HEAD), bf16), ((HEAD, LENGTH), bf16),
            ((LENGTH, TILE), f32), ((LENGTH, TILE), bf16),
        ],
        3 * 10**9, 2 * 10**6, 24 * 10**5, (table, slope, own, other), 2,
    )


def backward_kernel(
    table, slope_ref, own_ref, other_ref, grad_own, grad_other, lse_ref,
    out_own, out_other, sum_ref,
    qa, ka, va, kt, da, dq, dk, dv, p_sc, dp_sc, ds_sc,
):
    def rest(a, rows, key, value):
        va[rows, :] = value
        kt[:, rows] = key.astype(f32).T.astype(bf16)
        da[rows, :] = unpack(pick(table, a, grad_own, grad_other))

    stage_blocks(table, slope_ref, own_ref, other_ref, qa, ka, rest)
    hidden = future()
    for i in range(TILES):
        here = slice(i * TILE, (i + 1) * TILE)
        q = qa[here, :]
        q_plain = q[:, 0:HEAD]
        grad = da[here, :]
        lse = lse_ref[i]
        delta = None
        for j in range(i + 1):
            there = slice(j * TILE, (j + 1) * TILE)
            s = dot_nt(ka[there, :], q)
            if j == i:
                s = jnp.where(hidden, -1e30, s)
            p = jnp.exp(s - lse)
            dp = dot_nt(va[there, :], grad)
            p_sc[there, :] = p
            dp_sc[there, :] = dp
            part = fold(p * dp, jnp.add)
            delta = part if delta is None else delta + part
            value = dot(p.astype(bf16), grad)
            dv[there, :] = value if j == i else dv[there, :] + value
        delta = jnp.sum(delta, axis=0, keepdims=True)
        for j in range(i + 1):
            there = slice(j * TILE, (j + 1) * TILE)
            ds = (p_sc[there, :] * (dp_sc[there, :] - delta)).astype(bf16)
            ds_sc[there, :] = ds
            key = dot(ds, q_plain)
            dk[there, :] = key if j == i else dk[there, :] + key
        n = (i + 1) * TILE
        dq[here, :] = (dot(kt[:, 0:n], ds_sc[0:n, :]) * score_scale).T
    total = None
    for a in range(HEADS):
        rows = slice(a * ROWS, (a + 1) * ROWS)
        query = dq[rows, :].astype(bf16)
        value = dv[rows, :].astype(bf16)
        pair = jnp.concatenate([query, dk[rows, :].astype(bf16)], axis=1)
        put(table, a, out_own, out_other, jnp.concatenate([pair, pack(value)], axis=0))
        both = jnp.concatenate([query.astype(f32), value.astype(f32)], axis=1)
        both = jnp.sum(both, axis=0, keepdims=True)
        total = both if total is None else total + both
    sum_ref[0:1, :] = total


def attention_backward(table, slope, own, other, grad_own, grad_other, lse):
    narrow = ((LENGTH, HEAD), f32)
    return call(
        backward_kernel, "attention_backward",
        [((9, 192, 128), bf16), ((9, 192, 128), bf16), ((8, 128), f32)],
        [
            ((LENGTH, 2 * HEAD), bf16), ((LENGTH, 2 * HEAD), bf16), ((LENGTH, HEAD), bf16),
            ((HEAD, LENGTH), bf16), ((LENGTH, HEAD), bf16), narrow, narrow, narrow,
            ((LENGTH, TILE), f32), ((LENGTH, TILE), f32), ((LENGTH, TILE), bf16),
        ],
        6 * 10**9, 3 * 10**6, 24 * 10**5,
        (table, slope, own, other, grad_own, grad_other, lse), 2,
    )


def output_kernel(table, own_ref, other_ref, weight_ref, rows_ref, mine_part, other_part, mixed_ref):
    weight = jnp.concatenate([weight_ref[...], rows_ref[0:64, :]], axis=0)
    for chunk in ORDER:
        blocks = []
        for p in (2 * chunk, 2 * chunk + 1):
            k = table[p]
            block = jnp.concatenate([unpack(own_ref[k]), unpack(other_ref[k])], axis=1)
            mixed_ref[pl.ds(place(table, p), ROWS), :] = block
            blocks.append(block)
        put_parts(mine_part, other_part, chunk, dot(jnp.concatenate(blocks, axis=0), weight))


def output_parts(table, own, other, weight, rows):
    return call(
        output_kernel, "output_parts", PARTS + [((1024, 128), bf16)], [],
        27 * 10**7, 4 * 10**6, 0, (table, own, other, weight, rows), 1,
    )


def feed_kernel(table, *refs):
    pieces = refs[0:8]
    cotangent_ref, up_ref, down_ref, rows_ref, bias_ref = refs[8:13]
    mine_part, other_part, act_ref, grad_ref, second_ref, sems = refs[13:19]
    copies = assemble(table, pieces, second_ref, sems)
    bias = bias_ref[0:1, :]
    for chunk in ORDER:
        cotangents = rows_of(table, cotangent_ref, 2 * chunk)
        back = jnp.concatenate(
            [dot_nt(cotangents, down_ref[...]), dot_nt(cotangents, rows_ref[64:320, :])], axis=1
        )
        copies[2 * chunk].wait()
        copies[2 * chunk + 1].wait()
        up = dot(rows_of(table, second_ref, 2 * chunk), up_ref[...]) + bias
        square = up * up
        bend = jnp.tanh(0.7978845608028654 * (up + 0.044715 * square * up))
        half = 0.5 * (1.0 + bend)
        set_rows(table, act_ref, 2 * chunk, (up * half).astype(bf16))
        slope = half + 0.5 * up * (1.0 - bend * bend) * (
            0.7978845608028654 * (1.0 + 0.134145 * square)
        )
        grad = (back * slope).astype(bf16)
        set_rows(table, grad_ref, 2 * chunk, grad)
        put_parts(mine_part, other_part, chunk, dot_nt(grad, up_ref[...]))


def feed_parts(table, pieces, cotangents, up, down, rows, bias):
    return call(
        feed_kernel, "feed_parts", PARTS + [((1024, 512), bf16)] * 2 + [((1024, D), bf16)],
        [pltpu.SemaphoreType.DMA((8,))],
        32 * 10**8, 2 * 10**7, 5 * 10**5, (table, *pieces, cotangents, up, down, rows, bias), 1, 8,
    )


def out_kernel(act_ref, down_ref, rows_ref, out_ref):
    for chunk in range(4):
        rows = slice(chunk * TILE, (chunk + 1) * TILE)
        act = act_ref[rows, :]
        value = dot(act[:, 0:256], down_ref[...]) + dot(act[:, 256:512], rows_ref[64:320, :])
        out_ref[rows, :] = value.astype(bf16)


def out_part(act, down, rows):
    return call(
        out_kernel, "out_part", [((1024, D), bf16)], [], 11 * 10**8, 5 * 10**6, 0,
        (act, down, rows),
    )[0]


def mixed_kernel(table, *refs):
    pieces, weight_ref, rows_ref = refs[0:8], refs[8], refs[9]
    own_ref, other_ref, all_ref, sems = refs[10:14]
    copies = assemble(table, pieces, all_ref, sems)
    weight = jnp.concatenate([weight_ref[...], rows_ref[0:64, :]], axis=0)
    for chunk in range(4):
        copies[2 * chunk].wait()
        copies[2 * chunk + 1].wait()
        grads = dot_nt(rows_of(table, all_ref, 2 * chunk), weight).astype(bf16)
        for b in range(2):
            block = grads[b * ROWS : (b + 1) * ROWS]
            k = table[2 * chunk + b]
            own_ref[k] = pack(block[:, 0:64])
            other_ref[k] = pack(block[:, 64:128])


def mixed_back(table, pieces, weight, rows):
    return call(
        mixed_kernel, "mixed_back",
        [((8, 64, 128), bf16), ((8, 64, 128), bf16), ((1024, D), bf16)],
        [pltpu.SemaphoreType.DMA((8,))],
        27 * 10**7, 4 * 10**6, 0, (table, *pieces, weight, rows), 1, 8,
    )


def last_kernel(
    table, own_ref, other_ref, project_ref, normal_ref, mine_part, other_part, joined_ref, sum_ref
):
    gain = None
    for chunk in ORDER:
        blocks = []
        for p in (2 * chunk, 2 * chunk + 1):
            own, other = own_ref[table[p]], other_ref[table[p]]
            blocks.append(
                jnp.concatenate(
                    [own[0:ROWS], other[0:ROWS], unpack(own[ROWS:192]), unpack(other[ROWS:192])],
                    axis=1,
                )
            )
        joined = jnp.concatenate(blocks, axis=0)
        set_rows(table, joined_ref, 2 * chunk, joined)
        value = dot_nt(joined, project_ref[...])
        put_parts(mine_part, other_part, chunk, value)
        normal = rows_of(table, normal_ref, 2 * chunk).astype(f32)
        tilted = jnp.sum(value * normal, axis=0, keepdims=True)
        plain = jnp.sum(value, axis=0, keepdims=True)
        gain = tilted if gain is None else gain + tilted
        offset = plain if chunk == ORDER[0] else offset + plain
    sum_ref[0:1, :] = gain
    sum_ref[1:2, :] = offset


def last_parts(table, own, other, project, normal):
    return call(
        last_kernel, "last_parts", PARTS + [((1024, 384), bf16), ((8, D), f32)], [],
        8 * 10**8, 7 * 10**6, 0, (table, own, other, project, normal), 1,
    )


def join_kernel(mine_ref, core_ref, here_ref, near_ref, far_ref, back_ref):
    for d, ref in enumerate((here_ref, near_ref, far_ref, back_ref)):
        ref[...] = (mine_ref[d] + core_ref[d].astype(f32)).astype(ref.dtype)


def join(mine, core):
    return call(
        join_kernel, "join", [((ROWS, D), f32)] + [((ROWS, D), bf16)] * 3, [], 10**6, 4 * 10**6, 0,
        (mine, core),
    )


def landed(refs):
    here, near, far, back = [ref[...].astype(f32) for ref in refs]
    return here + near + far + back


def middle_kernel(*refs):
    input_ref, vector_ref, mid_ref, normal_ref, inverse_ref, normed_ref = refs[4:10]
    mid = input_ref[...].astype(f32) + (landed(refs[0:4]) + vector_ref[2:3, :])
    normal, inverse = normalize(mid)
    mid_ref[...] = mid
    normal_ref[...] = normal
    inverse_ref[...] = inverse
    normed_ref[...] = (normal * vector_ref[3:4, :] + vector_ref[4:5, :]).astype(bf16)


def middle(ends, inputs, vectors):
    return call(
        middle_kernel, "middle",
        [((ROWS, D), f32), ((ROWS, D), f32), ((ROWS, 1), f32), ((ROWS, D), bf16)], [],
        10**6, 3 * 10**6, 0, (*ends, inputs, vectors),
    )


def middle_back_kernel(*refs):
    cotangent_ref, vector_ref, normal_ref, inverse_ref, grad_ref, branch_ref, sum_ref = refs[4:11]
    second = landed(refs[0:4])
    normal = normal_ref[...]
    cotangent = cotangent_ref[...].astype(f32)
    grad = cotangent + norm_back(second, vector_ref[3:4, :], normal, inverse_ref[...])
    grad_ref[...] = grad
    branch = grad.astype(bf16)
    branch_ref[...] = branch
    sum_ref[0:1, :] = jnp.sum(second * normal, axis=0, keepdims=True)
    sum_ref[1:2, :] = jnp.sum(second, axis=0, keepdims=True)
    sum_ref[2:3, :] = jnp.sum(branch.astype(f32), axis=0, keepdims=True)
    sum_ref[3:4, :] = jnp.sum(cotangent, axis=0, keepdims=True)


def middle_back(ends, cotangent, vectors, normal, inverse):
    return call(
        middle_back_kernel, "middle_back",
        [((ROWS, D), f32), ((ROWS, D), bf16), ((8, D), f32)], [],
        10**6, 3 * 10**6, 0, (*ends, cotangent, vectors, normal, inverse),
    )


def block_kernel(part_ref, mid_ref, vector_ref, out_ref):
    out_ref[...] = (mid_ref[...] + part_ref[...].astype(f32) + vector_ref[5:6, :]).astype(bf16)


def block_end(part, mid, vectors):
    return call(
        block_kernel, "block_end", [((ROWS, D), bf16)], [], 10**6, 2 * 10**6, 0,
        (part, mid, vectors),
    )[0]


def input_kernel(*refs):
    input_ref, vector_ref, grad_ref, out_ref = refs[4:8]
    normal, inverse = normalize(input_ref[...].astype(f32))
    out_ref[...] = grad_ref[...] + norm_back(
        landed(refs[0:4]), vector_ref[0:1, :], normal, inverse
    )


def input_end(ends, inputs, vectors, grad):
    return call(
        input_kernel, "input_end", [((ROWS, D), f32)], [], 10**6, 3 * 10**6, 0,
        (*ends, inputs, vectors, grad),
    )[0]


def shift(value, axis, step):
    size = lax.axis_size(axis)
    return lax.ppermute(value, axis, [(i, (i + step) % size) for i in range(size)])


def gather(own):
    mine = [own] + [shift(own, "y", -step) for step in (1, 2, 3)]
    return mine + [shift(block, "c", 1) for block in mine]


def scatter(mine, other):
    here, near, far, back = join(mine, shift(other, "c", 1))
    return here, shift(near, "y", 1), shift(far, "y", 2), shift(back, "y", 3)


def exchange(value, axes):
    return lax.all_to_all(value, axes, split_axis=0, concat_axis=0, tiled=True)


def after(value, *others):
    return lax.optimization_barrier((value, *others))[0]


def normalize(values):
    centre = jnp.mean(values, axis=-1, keepdims=True)
    centred = values - centre
    spread = jnp.mean(centred * centred, axis=-1, keepdims=True)
    inverse = lax.rsqrt(spread + epsilon)
    return centred * inverse, inverse


def norm_back(grad, gain, normal, inverse):
    scaled = grad * gain
    return inverse * (
        scaled
        - jnp.mean(scaled, axis=-1, keepdims=True)
        - normal * jnp.mean(scaled * normal, axis=-1, keepdims=True)
    )


def on_device(
    block_input,
    first_gain,
    first_shift,
    attention_weight,
    query_bias,
    value_bias,
    output_weight,
    output_bias,
    second_gain,
    second_shift,
    upward_weight,
    upward_bias,
    downward_weight,
    downward_bias,
    cotangent,
):
    y = lax.axis_index("y")
    xh = lax.axis_index("xh")
    c = lax.axis_index("c")
    shard = 4 * y + 2 * xh + c
    piece = np.arange(8)
    table = (2 * ((y + piece % 4) % 4) + (c ^ (piece // 4))).astype(jnp.int32)
    half = xh[None].astype(jnp.int32)
    slope = jnp.exp2(-8.0 * (shard + 1).astype(f32) / HEADS)[None]

    with jax.named_scope("weights_attention"):
        vectors_own = jnp.concatenate(
            [first_gain, first_shift, output_bias, second_gain, second_shift, downward_bias]
        )
        biases_own = jnp.concatenate([query_bias, value_bias, upward_bias])
        small = jnp.pad(vectors_own[None], ((0, 15), (0, 0))) + jnp.pad(
            biases_own[None], ((1, 14), (0, 0))
        )
        payload, up_payload = call(
            deal_kernel, "deal", [((16, 80, 384), bf16), ((16, 64, 512), bf16)], [],
            0, 4 * 10**6, 0, (attention_weight, small, upward_weight),
        )
        arrived = exchange(payload, FSDP)

    with jax.named_scope("first"):
        inputs = lax.all_gather(block_input, ("y", "c"), axis=0, tiled=True)
        heads_own, heads_other, normed_first, normal_first, project, vectors, bias_up = first_heads(
            shard[None].astype(jnp.int32), inputs, arrived
        )
        heads_arrived = shift(heads_other, "xh", 1)
    with jax.named_scope("weights_upward"):
        upward_pair = exchange(after(up_payload, arrived), FSDP).reshape(D, 512)
    with jax.named_scope("weights_pair"):
        own_rows = jnp.concatenate([output_weight, downward_weight], axis=0)
        other_rows = shift(after(own_rows, heads_arrived), "xh", 1)
    with jax.named_scope("cotangents"):
        cotangents = lax.all_gather(after(cotangent, inputs), ("y", "c"), axis=0, tiled=True)

    with jax.named_scope("attention"):
        mixed_own, mixed_other, lse = attention_forward(half, slope, heads_own, heads_arrived)
        mixed_arrived = shift(mixed_other, "xh", 1)
    with jax.named_scope("output"):
        mine, other, mixed_pair = output_parts(
            table, mixed_own, mixed_arrived, output_weight, other_rows
        )
        residual_mid, normal_second, inverse_second, normed_second = middle(
            scatter(mine, other), block_input, vectors
        )

    with jax.named_scope("feed"):
        mine, other, activated, upward_grad, seconds = feed_parts(
            table, gather(normed_second), cotangents, upward_pair, downward_weight, other_rows,
            bias_up,
        )
        mid_grad, branch_grad, sums = middle_back(
            scatter(mine, other), cotangent, vectors, normal_second, inverse_second
        )

    with jax.named_scope("mixed_back"):
        grad_own, grad_other, branch_grads = mixed_back(
            table, gather(branch_grad), output_weight, other_rows
        )
        grad_arrived = shift(grad_other, "xh", 1)

    with jax.named_scope("feed_out"):
        out = lax.psum_scatter(
            out_part(activated, downward_weight, other_rows), ("y", "c"), scatter_dimension=0,
            tiled=True,
        )
        block_output = block_end(out, residual_mid, vectors)

    with jax.named_scope("upward_gradients"):
        upward_weight_grad = dot_tn(seconds, upward_grad).astype(bf16)
        upward_bias_grad = jnp.sum(upward_grad.astype(f32), axis=0).astype(bf16)
        quads = sums[0:4].astype(bf16).reshape(4, 16, 64).transpose(1, 0, 2).reshape(16, 2, 128)
        extra = jnp.concatenate(
            [
                quads,
                jnp.broadcast_to(upward_bias_grad.reshape(1, 4, 128), (16, 4, 128)),
                jnp.zeros((16, 2, 128), bf16),
            ],
            axis=1,
        )
        extra = jnp.broadcast_to(extra[:, None], (16, 8, 8, 128)).reshape(1024, 128)
        shares = jnp.concatenate([upward_weight_grad, extra], axis=-1).reshape(128, 8, 640)
        arrived_up = exchange(shares, FSDP + SEQ)
        wide_up = arrived_up.reshape(4, 2, 2, 8, 8, 640).astype(f32)
        up_sum = jnp.sum(wide_up[..., :512], axis=3)
        up_total = up_sum[..., :256] + up_sum[:, ::-1, :, :, 256:]
        up_total = up_total.transpose(3, 0, 1, 2, 4).reshape(8, FF).astype(bf16)
        small_sum = jnp.sum(wide_up[..., 512:], axis=3)
        four_total = jnp.sum(small_sum[:, :, :, 0:2], axis=(0, 1, 2))
        bias_rows = small_sum.reshape(16, 8, 128)[:, 2:6].reshape(16, 512)
        bias_total = (
            lax.dynamic_index_in_dim(bias_rows, shard, 0, keepdims=False)[:256]
            + lax.dynamic_index_in_dim(bias_rows, shard ^ 2, 0, keepdims=False)[256:]
        )
    with jax.named_scope("row_gradients"):
        downward_grad = dot_tn(activated, cotangents)
        output_grad = dot_tn(mixed_pair, branch_grads)
        rows_other = jnp.concatenate([output_grad[64:], downward_grad[256:]], axis=0).astype(bf16)
        rows_arrived = shift(rows_other, "xh", 1)
        wide_rows = rows_arrived.astype(f32)
        output_sum = (output_grad[:64] + wide_rows[:64]).astype(bf16).reshape(8, 8, D)
        downward_sum = (downward_grad[:256] + wide_rows[64:]).astype(bf16).reshape(8, 32, D)
        rows_all = exchange(jnp.concatenate([output_sum, downward_sum], axis=1), SEQ)
        rows_total = jnp.sum(rows_all.astype(f32), axis=0).astype(bf16)
    with jax.named_scope("early_gradients"):
        early = jnp.concatenate([rows_total, up_total.reshape(32, D)], axis=0)
        early_all = exchange(jnp.broadcast_to(early[None], (8, 72, D)), SEQ)
        wide_early = early_all.astype(f32)
        output_weight_gradient = wide_early[:, :8].reshape(64, D)
        downward_weight_gradient = wide_early[:, 8:40].reshape(256, D)
        upward_weight_gradient = wide_early[:, 40:].reshape(64, FF)

    with jax.named_scope("attention_back"):
        back_own, back_other, token_sums = attention_backward(
            half, slope, heads_own, heads_arrived, grad_own, grad_arrived, lse
        )
        back_other = after(back_other, arrived_up, rows_arrived)
        back_arrived = shift(back_other, "xh", 1)
    with jax.named_scope("first_back"):
        back_arrived = after(back_arrived, rows_all)
        mine, other, joined, last_sums = last_parts(
            table, back_own, back_arrived, project, normal_first
        )
        input_gradient = input_end(scatter(mine, other), block_input, vectors, mid_grad)
    with jax.named_scope("attention_gradients"):
        weight_grad = dot_tn(normed_first, joined).astype(bf16)
        quads = last_sums[0:2].astype(bf16).reshape(2, 16, 64).transpose(1, 0, 2)
        extra = jnp.concatenate(
            [
                quads.reshape(16, 1, 128),
                jnp.broadcast_to(token_sums[None, 0:1].astype(bf16), (16, 1, 128)),
                jnp.zeros((16, 6, 128), bf16),
            ],
            axis=1,
        )
        extra = jnp.broadcast_to(extra[:, None], (16, 8, 8, 128)).reshape(1024, 128)
        shares = jnp.concatenate([weight_grad, extra], axis=-1).reshape(128, 8, 512)
        arrived_last = exchange(shares, FSDP + SEQ).reshape(4, 2, 2, 8, 8, 512).astype(f32)
        last_sum = jnp.sum(arrived_last, axis=3)
        twin_sum = last_sum[:, ::-1]
        pair_total = last_sum[..., 0:128] + twin_sum[..., 128:256]
        value_total = last_sum[..., 256:320] + twin_sum[..., 320:384]
        last_total = jnp.concatenate([pair_total, value_total], axis=-1)
        last_total = last_total.reshape(16, 8, 3, HEAD).transpose(1, 2, 0, 3).reshape(8, 3 * D)
        late = last_total.astype(bf16).reshape(24, D)
        late = after(late, early_all)
        late_all = exchange(jnp.broadcast_to(late[None], (8, 24, D)), SEQ).astype(f32)
        attention_weight_gradient = late_all.reshape(64, 3 * D)
        last_small = last_sum[..., 384:].reshape(16, 8, 128)
        first_total = jnp.sum(last_small[:, 0], axis=0)
        bias_pair = lax.dynamic_index_in_dim(last_small[:, 1], shard, 0, keepdims=False)

    return (
        block_output,
        input_gradient,
        first_total[:64],
        first_total[64:],
        attention_weight_gradient,
        bias_pair[:64],
        bias_pair[64:],
        output_weight_gradient,
        four_total[1, :64],
        four_total[0, :64],
        four_total[0, 64:],
        upward_weight_gradient,
        bias_total,
        downward_weight_gradient,
        four_total[1, 64:],
    )


def solution(mesh):
    grid = Mesh(mesh.devices.reshape(4, 2, 4, 2, 2), ALL)
    tokens = P(ALL, None)
    rows = P(FSDP, None)
    line = P(FSDP)
    return jax.shard_map(
        on_device,
        mesh=grid,
        in_specs=(
            tokens, line, line, rows, line, line, rows, line, line, line, rows, line, rows, line,
            tokens,
        ),
        out_specs=(
            tokens, tokens, line, line, rows, line, line, rows, line, line, line, rows, line, rows,
            line,
        ),
        check_vma=False,
    )
```

```python
import jax
import jax.numpy as jnp
import numpy as np
from jax import lax
from jax.experimental import pallas as pl
from jax.experimental.pallas import tpu as pltpu
from jax.sharding import Mesh
from jax.sharding import PartitionSpec as P

D = 1024
HEADS = 16
HEAD = 64
FF = 4096

epsilon = 1e-05
score_scale = 0.125
bf16 = jnp.bfloat16
f32 = jnp.float32

SEQ = ("z", "xl")
FSDP = ("y", "xh", "c")
ALL = SEQ + FSDP
ROWS = 128
TILE = 256
TILES = 8
LENGTH = TILE * TILES

NT = (((1,), (1,)), ((), ()))


def dot(a, b):
    return jnp.dot(a, b, preferred_element_type=f32)


def dot_nt(a, b):
    return lax.dot_general(a, b, NT, preferred_element_type=f32)


def dot_tn(a, b):
    return lax.dot_general(a, b, (((0,), (0,)), ((), ())), preferred_element_type=f32)


smem = pl.BlockSpec(memory_space=pltpu.SMEM)
vmem = pl.BlockSpec(memory_space=pltpu.VMEM)


def call(kernel, name, outs, scratch, flops, moved, transcendentals, args, scalars=0, pieces=0):
    rest = len(args) - scalars - pieces
    return pl.pallas_call(
        kernel,
        out_shape=tuple(jax.ShapeDtypeStruct(shape, kind) for shape, kind in outs),
        in_specs=[smem] * scalars + [pl.BlockSpec(memory_space=pl.ANY)] * pieces + [vmem] * rest,
        out_specs=(vmem,) * len(outs),
        scratch_shapes=[
            pltpu.VMEM(*item) if isinstance(item, tuple) else item for item in scratch
        ],
        compiler_params=pltpu.CompilerParams(vmem_limit_bytes=60 * 2**20),
        cost_estimate=pl.CostEstimate(
            flops=flops, bytes_accessed=moved, transcendentals=transcendentals
        ),
        name=name,
    )(*args)


def place(table, p):
    return pl.multiple_of(table[p] * ROWS, ROWS)


def assemble(table, refs, out, sems):
    copies = [
        pltpu.make_async_copy(refs[p], out.at[pl.ds(place(table, p), ROWS), :], sems.at[p])
        for p in range(8)
    ]
    for copy in copies:
        copy.start()
    return copies


def rows_of(table, ref, p):
    return jnp.concatenate(
        [ref[pl.ds(place(table, p + b), ROWS), :] for b in range(2)], axis=0
    )


def set_rows(table, ref, p, value):
    for b in range(2):
        ref[pl.ds(place(table, p + b), ROWS), :] = value[b * ROWS : (b + 1) * ROWS]


def put_parts(mine_ref, other_ref, chunk, value):
    ref = mine_ref if chunk < 2 else other_ref
    for b in range(2):
        ref[2 * (chunk % 2) + b] = value[b * ROWS : (b + 1) * ROWS].astype(ref.dtype)


PARTS = [((4, ROWS, D), bf16), ((4, ROWS, D), bf16)]
ORDER = (2, 3, 0, 1)


def deal_kernel(weight_ref, small_ref, up_ref, out_ref, up_out):
    small = small_ref[...]

    def piece(kind, head):
        start = kind * D + head * HEAD
        return weight_ref[:, start : start + HEAD]

    for y in range(4):
        for x in range(2):
            for c in range(2):
                shard = 4 * y + 2 * x + c
                twin = shard ^ 2
                out_ref[shard, 0:64, :] = jnp.concatenate(
                    [
                        piece(kind, head) for kind in range(3) for head in (shard, twin)
                    ],
                    axis=1,
                )
                out_ref[shard, 64:80, :] = small
                up_out[shard, :, 0:256] = up_ref[:, 256 * shard : 256 * shard + 256]
                up_out[shard, :, 256:512] = up_ref[:, 256 * twin : 256 * twin + 256]


def swap(pairs):
    return jnp.concatenate(
        [pairs[:, 64:128], pairs[:, 0:64], pairs[:, 192:256], pairs[:, 128:192]], axis=1
    )


def first_kernel(shard_ref, *refs):
    inputs, arrived = refs[0:2]
    query_ref, kv_ref, send_ref, normed_ref, normal_ref, project_ref, vector_ref, bias_ref = refs[2:]
    for r in range(16):
        project_ref[64 * r : 64 * r + 64, :] = arrived[r, 0:64, :]
    rows = [arrived[r, 64:80, :].astype(f32) for r in range(16)]
    for g in range(6):
        vector_ref[g : g + 1, :] = jnp.concatenate(
            [rows[r][0:1, 64 * g : 64 * g + 64] for r in range(16)], axis=1
        )
    shard = shard_ref[0]
    mine = arrived[shard, 64:80, :].astype(f32)[1:2]
    twin = arrived[shard ^ 2, 64:80, :].astype(f32)[1:2]
    bias_ref[0:1, :] = jnp.concatenate([mine[:, 128:], twin[:, 128:]], axis=1)
    zero = jnp.zeros((1, 2 * HEAD), f32)
    bias = jnp.concatenate(
        [mine[:, 0:64], twin[:, 0:64], zero, mine[:, 64:128], twin[:, 64:128]], axis=1
    )
    gain = vector_ref[0:1, :]
    offset = vector_ref[1:2, :]
    for chunk in range(4):
        rows = slice(chunk * TILE, (chunk + 1) * TILE)
        normal, unused = normalize(inputs[rows, :].astype(f32))
        normal_ref[rows, :] = normal.astype(bf16)
        normed = (normal * gain + offset).astype(bf16)
        normed_ref[rows, :] = normed
        heads = (dot(normed, project_ref[...]) + bias).astype(bf16)
        query_ref[rows, :] = heads[:, 0:128]
        kv_ref[rows, :] = heads[:, 128:384]
        send_ref[rows, :] = swap(heads[:, 128:384])


def first_heads(shard, inputs, arrived):
    return call(
        first_kernel, "first_heads",
        [
            ((1024, 128), bf16), ((1024, 256), bf16), ((1024, 256), bf16), ((1024, D), bf16),
            ((1024, D), bf16), ((D, 384), bf16), ((8, D), f32), ((8, 512), f32),
        ],
        [], 8 * 10**8, 10**7, 10**4, (shard, inputs, arrived), 1,
    )


def in_head(shape, head):
    lane = lax.broadcasted_iota(jnp.int32, shape, 1)
    return (lane < HEAD) if head == 0 else (lane >= HEAD)


def stage_queries(query, head):
    lane = lax.broadcasted_iota(jnp.int32, query.shape, 1) - (HEAD if head == 0 else 0)
    ones = jnp.where((lane >= 0) & (lane < 3), 1.0, 0.0)
    scaled = query.astype(f32) * score_scale
    return jnp.where(in_head(query.shape, head), scaled, ones).astype(bf16)


def stage_keys(key, head, slope, first):
    shape = key.shape
    lane = lax.broadcasted_iota(jnp.int32, shape, 1) - (HEAD if head == 0 else 0)
    row = lax.broadcasted_iota(jnp.int32, shape, 0)
    place = slope * (row + first).astype(f32)
    high = place.astype(bf16).astype(f32)
    rest = place - high
    middle = rest.astype(bf16).astype(f32)
    low = rest - middle
    extra = jnp.where(
        lane == 0, high, jnp.where(lane == 1, middle, jnp.where(lane == 2, low, 0.0))
    )
    return jnp.where(in_head(shape, head), key.astype(f32), extra).astype(bf16)


def fold(tile, op):
    parts = [tile[8 * g : 8 * g + 8] for g in range(TILE // 8)]
    while len(parts) > 1:
        parts = [op(parts[2 * g], parts[2 * g + 1]) for g in range(len(parts) // 2)]
    return parts[0]


def future():
    key = lax.broadcasted_iota(jnp.int32, (TILE, TILE), 0)
    query = lax.broadcasted_iota(jnp.int32, (TILE, TILE), 1)
    return key > query


def tile_rows(t):
    return slice(t * TILE, (t + 1) * TILE)


def stage(half, slopes, own_ref, other_ref, ka, emit_rest):
    for t in range(4):
        for side, ref in enumerate((own_ref, other_ref)):
            slot = tile_rows(2 * t + side)
            pair = ref[tile_rows(t), :]
            first = TILE * (2 * t + (half[0] if side == 0 else 1 - half[0])) - LENGTH // 2
            for head in range(2):
                ka[head, slot, :] = stage_keys(pair[:, 0:128], head, slopes[head], first)
            emit_rest(slot, pair)


def masked(s, t, slot, hidden, ahead):
    if slot == 2 * t:
        return jnp.where(hidden, -1e30, s)
    return s + ahead if slot == 2 * t + 1 else s


def forward_kernel(half, slopes, q_ref, own_ref, other_ref, out_ref, lse_ref, ka, vt, s_sc, p_sc):
    def rest(slot, pair):
        vt[:, slot] = pair[:, 128:256].astype(f32).T.astype(bf16)

    stage(half, slopes, own_ref, other_ref, ka, rest)
    hidden = future()
    ahead = jnp.where(half[0] == 1, 0.0, -1e30)
    for t in range(4):
        query = q_ref[tile_rows(t), :]
        n = (2 * t + 2) * TILE
        outs = []
        for head in range(2):
            q = stage_queries(query, head)
            peak = None
            for slot in range(2 * t + 2):
                rows = tile_rows(slot)
                s = masked(dot_nt(ka[head, rows, :], q), t, slot, hidden, ahead)
                s_sc[head, rows, :] = s
                top = fold(s, jnp.maximum)
                peak = top if peak is None else jnp.maximum(peak, top)
            peak = jnp.max(peak, axis=0, keepdims=True)
            total = None
            for slot in range(2 * t + 2):
                rows = tile_rows(slot)
                p = jnp.exp(s_sc[head, rows, :] - peak)
                p_sc[head, rows, :] = p.astype(bf16)
                part = fold(p, jnp.add)
                total = part if total is None else total + part
            total = jnp.sum(total, axis=0, keepdims=True)
            outs.append(dot(vt[head * HEAD : (head + 1) * HEAD, 0:n], p_sc[head, 0:n, :]) / total)
            lse_ref[2 * t + head] = peak + jnp.log(total)
        out_ref[tile_rows(t), :] = jnp.concatenate(outs, axis=0).T.astype(bf16)


def attention_forward(half, slopes, query, own, other):
    return call(
        forward_kernel, "attention_forward",
        [((1024, 128), bf16), ((8, 1, TILE), f32)],
        [
            ((2, LENGTH, 128), bf16), ((128, LENGTH), bf16), ((2, LENGTH, TILE), f32),
            ((2, LENGTH, TILE), bf16),
        ],
        3 * 10**9, 2 * 10**6, 24 * 10**5, (half, slopes, query, own, other), 2,
    )


def backward_kernel(
    half, slopes, q_ref, own_ref, other_ref, grad_ref, lse_ref,
    dq_ref, down_ref, send_ref,
    ka, kt, va, dk, dv, p_sc, dp_sc, ds_sc,
):
    def rest(slot, pair):
        va[slot, :] = pair[:, 128:256]
        kt[:, slot] = pair[:, 0:128].astype(f32).T.astype(bf16)

    stage(half, slopes, own_ref, other_ref, ka, rest)
    hidden = future()
    ahead = jnp.where(half[0] == 1, 0.0, -1e30)
    for t in range(4):
        query = q_ref[tile_rows(t), :]
        grad = grad_ref[tile_rows(t), :]
        n = (2 * t + 2) * TILE
        grads = [
            jnp.where(in_head(grad.shape, head), grad.astype(f32), 0.0).astype(bf16)
            for head in range(2)
        ]
        plain = [
            jnp.where(in_head(query.shape, head), query.astype(f32) * score_scale, 0.0).astype(bf16)
            for head in range(2)
        ]
        queries = [stage_queries(query, head) for head in range(2)]
        grad_rows = jnp.concatenate(grads, axis=0)
        plain_rows = jnp.concatenate(plain, axis=0)
        delta = [None, None]
        for slot in range(2 * t + 2):
            rows = tile_rows(slot)
            low = []
            for head in range(2):
                s = masked(dot_nt(ka[head, rows, :], queries[head]), t, slot, hidden, ahead)
                p = jnp.exp(s - lse_ref[2 * t + head])
                dp = dot_nt(va[rows, :], grads[head])
                p_sc[head, rows, :] = p
                dp_sc[head, rows, :] = dp
                part = fold(p * dp, jnp.add)
                delta[head] = part if delta[head] is None else delta[head] + part
                low.append(p.astype(bf16))
            value = dot(jnp.concatenate(low, axis=1), grad_rows)
            dv[rows, :] = value if slot >= 2 * t else dv[rows, :] + value
        delta = [jnp.sum(item, axis=0, keepdims=True) for item in delta]
        for slot in range(2 * t + 2):
            rows = tile_rows(slot)
            low = []
            for head in range(2):
                ds = (p_sc[head, rows, :] * (dp_sc[head, rows, :] - delta[head])).astype(bf16)
                ds_sc[head, rows, :] = ds
                low.append(ds)
            key = dot(jnp.concatenate(low, axis=1), plain_rows)
            dk[rows, :] = key if slot >= 2 * t else dk[rows, :] + key
        outs = [
            dot(kt[head * HEAD : (head + 1) * HEAD, 0:n], ds_sc[head, 0:n, :]) for head in range(2)
        ]
        dq_ref[tile_rows(t), :] = (jnp.concatenate(outs, axis=0) * score_scale).T.astype(bf16)
    for t in range(4):
        rows = tile_rows(t)
        down_ref[rows, 0:128] = dk[tile_rows(2 * t), :]
        down_ref[rows, 128:256] = dv[tile_rows(2 * t), :]
        pair = jnp.concatenate([dk[tile_rows(2 * t + 1), :], dv[tile_rows(2 * t + 1), :]], axis=1)
        send_ref[rows, :] = swap(pair.astype(bf16))


def attention_backward(half, slopes, query, own, other, grad, lse):
    return call(
        backward_kernel, "attention_backward",
        [((1024, 128), bf16), ((1024, 256), f32), ((1024, 256), bf16)],
        [
            ((2, LENGTH, 128), bf16), ((128, LENGTH), bf16), ((LENGTH, 128), bf16),
            ((LENGTH, 128), f32), ((LENGTH, 128), f32), ((2, LENGTH, TILE), f32),
            ((2, LENGTH, TILE), f32), ((2, LENGTH, TILE), bf16),
        ],
        6 * 10**9, 3 * 10**6, 24 * 10**5, (half, slopes, query, own, other, grad, lse), 2,
    )


def output_kernel(table, mixed_ref, weight_ref, rows_ref, mine_part, other_part):
    weight = jnp.concatenate([weight_ref[...], rows_ref[...]], axis=0)
    for chunk in ORDER:
        put_parts(mine_part, other_part, chunk, dot(rows_of(table, mixed_ref, 2 * chunk), weight))


def output_parts(table, mixed, weight, rows):
    return call(
        output_kernel, "output_parts", PARTS, [], 27 * 10**7, 4 * 10**6, 0,
        (table, mixed, weight, rows), 1,
    )


def feed_kernel(table, *refs):
    pieces = refs[0:8]
    cotangent_ref, up_ref, down_ref, rows_ref, bias_ref = refs[8:13]
    mine_part, other_part, act_ref, grad_ref, second_ref, sems = refs[13:19]
    copies = assemble(table, pieces, second_ref, sems)
    bias = bias_ref[0:1, :]
    for chunk in ORDER:
        cotangents = rows_of(table, cotangent_ref, 2 * chunk)
        back = jnp.concatenate(
            [dot_nt(cotangents, down_ref[...]), dot_nt(cotangents, rows_ref[...])], axis=1
        )
        copies[2 * chunk].wait()
        copies[2 * chunk + 1].wait()
        up = dot(rows_of(table, second_ref, 2 * chunk), up_ref[...]) + bias
        square = up * up
        bend = jnp.tanh(0.7978845608028654 * (up + 0.044715 * square * up))
        half = 0.5 * (1.0 + bend)
        set_rows(table, act_ref, 2 * chunk, (up * half).astype(bf16))
        slope = half + 0.5 * up * (1.0 - bend * bend) * (
            0.7978845608028654 * (1.0 + 0.134145 * square)
        )
        grad = (back * slope).astype(bf16)
        set_rows(table, grad_ref, 2 * chunk, grad)
        put_parts(mine_part, other_part, chunk, dot_nt(grad, up_ref[...]))


def feed_parts(table, pieces, cotangents, up, down, rows, bias):
    return call(
        feed_kernel, "feed_parts", PARTS + [((1024, 512), bf16)] * 2 + [((1024, D), bf16)],
        [pltpu.SemaphoreType.DMA((8,))],
        32 * 10**8, 2 * 10**7, 5 * 10**5, (table, *pieces, cotangents, up, down, rows, bias), 1, 8,
    )


def out_kernel(act_ref, down_ref, rows_ref, out_ref):
    for chunk in range(4):
        rows = slice(chunk * TILE, (chunk + 1) * TILE)
        act = act_ref[rows, :]
        value = dot(act[:, 0:256], down_ref[...]) + dot(act[:, 256:512], rows_ref[...])
        out_ref[rows, :] = value.astype(bf16)


def out_part(act, down, rows):
    return call(
        out_kernel, "out_part", [((1024, D), bf16)], [], 11 * 10**8, 5 * 10**6, 0,
        (act, down, rows),
    )[0]


def mixed_kernel(table, *refs):
    pieces, weight_ref, rows_ref = refs[0:8], refs[8], refs[9]
    grad_ref, all_ref, sems = refs[10:13]
    copies = assemble(table, pieces, all_ref, sems)
    weight = jnp.concatenate([weight_ref[...], rows_ref[...]], axis=0)
    for chunk in range(4):
        copies[2 * chunk].wait()
        copies[2 * chunk + 1].wait()
        grads = dot_nt(rows_of(table, all_ref, 2 * chunk), weight).astype(bf16)
        set_rows(table, grad_ref, 2 * chunk, grads)


def mixed_back(table, pieces, weight, rows):
    return call(
        mixed_kernel, "mixed_back",
        [((1024, 128), bf16), ((1024, D), bf16)],
        [pltpu.SemaphoreType.DMA((8,))],
        27 * 10**7, 4 * 10**6, 0, (table, *pieces, weight, rows), 1, 8,
    )


def last_kernel(
    table, query_ref, own_ref, other_ref, project_ref, normal_ref,
    mine_part, other_part, joined_ref, sum_ref,
):
    gain = None
    for chunk in ORDER:
        own = rows_of(table, own_ref, 2 * chunk)
        other = rows_of(table, other_ref, 2 * chunk).astype(f32)
        joined = jnp.concatenate(
            [rows_of(table, query_ref, 2 * chunk), (own + other).astype(bf16)], axis=1
        )
        set_rows(table, joined_ref, 2 * chunk, joined)
        bias = jnp.sum(joined.astype(f32), axis=0, keepdims=True)
        biases = bias if chunk == ORDER[0] else biases + bias
        value = dot_nt(joined, project_ref[...])
        put_parts(mine_part, other_part, chunk, value)
        normal = rows_of(table, normal_ref, 2 * chunk).astype(f32)
        tilted = jnp.sum(value * normal, axis=0, keepdims=True)
        plain = jnp.sum(value, axis=0, keepdims=True)
        gain = tilted if gain is None else gain + tilted
        offset = plain if chunk == ORDER[0] else offset + plain
    sum_ref[0:1, :] = gain
    sum_ref[1:2, :] = offset
    sum_ref[2:3, 0:384] = biases


def last_parts(table, query, own, other, project, normal):
    return call(
        last_kernel, "last_parts", PARTS + [((1024, 384), bf16), ((8, D), f32)], [],
        8 * 10**8, 7 * 10**6, 0, (table, query, own, other, project, normal), 1,
    )


def join_kernel(mine_ref, core_ref, here_ref, near_ref, far_ref, back_ref):
    for d, ref in enumerate((here_ref, near_ref, far_ref, back_ref)):
        ref[...] = (mine_ref[d] + core_ref[d].astype(f32)).astype(ref.dtype)


def join(mine, core):
    return call(
        join_kernel, "join", [((ROWS, D), f32)] + [((ROWS, D), bf16)] * 3, [], 10**6, 4 * 10**6, 0,
        (mine, core),
    )


def landed(refs):
    here, near, far, back = [ref[...].astype(f32) for ref in refs]
    return here + near + far + back


def middle_kernel(*refs):
    input_ref, vector_ref, mid_ref, normal_ref, inverse_ref, normed_ref = refs[4:10]
    mid = input_ref[...].astype(f32) + (landed(refs[0:4]) + vector_ref[2:3, :])
    normal, inverse = normalize(mid)
    mid_ref[...] = mid
    normal_ref[...] = normal
    inverse_ref[...] = inverse
    normed_ref[...] = (normal * vector_ref[3:4, :] + vector_ref[4:5, :]).astype(bf16)


def middle(ends, inputs, vectors):
    return call(
        middle_kernel, "middle",
        [((ROWS, D), f32), ((ROWS, D), f32), ((ROWS, 1), f32), ((ROWS, D), bf16)], [],
        10**6, 3 * 10**6, 0, (*ends, inputs, vectors),
    )


def middle_back_kernel(*refs):
    cotangent_ref, vector_ref, normal_ref, inverse_ref, grad_ref, branch_ref, sum_ref = refs[4:11]
    second = landed(refs[0:4])
    normal = normal_ref[...]
    cotangent = cotangent_ref[...].astype(f32)
    grad = cotangent + norm_back(second, vector_ref[3:4, :], normal, inverse_ref[...])
    grad_ref[...] = grad
    branch = grad.astype(bf16)
    branch_ref[...] = branch
    sum_ref[0:1, :] = jnp.sum(second * normal, axis=0, keepdims=True)
    sum_ref[1:2, :] = jnp.sum(second, axis=0, keepdims=True)
    sum_ref[2:3, :] = jnp.sum(branch.astype(f32), axis=0, keepdims=True)
    sum_ref[3:4, :] = jnp.sum(cotangent, axis=0, keepdims=True)


def middle_back(ends, cotangent, vectors, normal, inverse):
    return call(
        middle_back_kernel, "middle_back",
        [((ROWS, D), f32), ((ROWS, D), bf16), ((8, D), f32)], [],
        10**6, 3 * 10**6, 0, (*ends, cotangent, vectors, normal, inverse),
    )


def block_kernel(part_ref, mid_ref, vector_ref, out_ref):
    out_ref[...] = (mid_ref[...] + part_ref[...].astype(f32) + vector_ref[5:6, :]).astype(bf16)


def block_end(part, mid, vectors):
    return call(
        block_kernel, "block_end", [((ROWS, D), bf16)], [], 10**6, 2 * 10**6, 0,
        (part, mid, vectors),
    )[0]


def input_kernel(*refs):
    input_ref, vector_ref, grad_ref, out_ref = refs[4:8]
    normal, inverse = normalize(input_ref[...].astype(f32))
    out_ref[...] = grad_ref[...] + norm_back(
        landed(refs[0:4]), vector_ref[0:1, :], normal, inverse
    )


def input_end(ends, inputs, vectors, grad):
    return call(
        input_kernel, "input_end", [((ROWS, D), f32)], [], 10**6, 3 * 10**6, 0,
        (*ends, inputs, vectors, grad),
    )[0]


def shift(value, axis, step):
    size = lax.axis_size(axis)
    return lax.ppermute(value, axis, [(i, (i + step) % size) for i in range(size)])


def gather(own):
    mine = [own] + [shift(own, "y", -step) for step in (1, 2, 3)]
    return mine + [shift(block, "c", 1) for block in mine]


def scatter(mine, other):
    here, near, far, back = join(mine, shift(other, "c", 1))
    return here, shift(near, "y", 1), shift(far, "y", 2), shift(back, "y", 3)


def exchange(value, axes):
    return lax.all_to_all(value, axes, split_axis=0, concat_axis=0, tiled=True)


def after(value, *others):
    return lax.optimization_barrier((value, *others))[0]


def normalize(values):
    centre = jnp.mean(values, axis=-1, keepdims=True)
    centred = values - centre
    spread = jnp.mean(centred * centred, axis=-1, keepdims=True)
    inverse = lax.rsqrt(spread + epsilon)
    return centred * inverse, inverse


def norm_back(grad, gain, normal, inverse):
    scaled = grad * gain
    return inverse * (
        scaled
        - jnp.mean(scaled, axis=-1, keepdims=True)
        - normal * jnp.mean(scaled * normal, axis=-1, keepdims=True)
    )


def on_device(
    block_input,
    first_gain,
    first_shift,
    attention_weight,
    query_bias,
    value_bias,
    output_weight,
    output_bias,
    second_gain,
    second_shift,
    upward_weight,
    upward_bias,
    downward_weight,
    downward_bias,
    cotangent,
):
    y = lax.axis_index("y")
    xh = lax.axis_index("xh")
    c = lax.axis_index("c")
    shard = 4 * y + 2 * xh + c
    piece = np.arange(8)
    table = (2 * ((y + piece % 4) % 4) + (c ^ (piece // 4))).astype(jnp.int32)
    half = xh[None].astype(jnp.int32)
    slopes = jnp.exp2(-8.0 * (jnp.stack([shard, shard ^ 2]) + 1).astype(f32) / HEADS)

    with jax.named_scope("weights_attention"):
        vectors_own = [
            first_gain, first_shift, output_bias, second_gain, second_shift, downward_bias
        ]
        small = sum(
            jnp.pad(item[None], ((0, 15), (64 * g, 320 - 64 * g)))
            for g, item in enumerate(vectors_own)
        )
        small = small + jnp.pad(query_bias[None], ((1, 14), (0, 320)))
        small = small + jnp.pad(value_bias[None], ((1, 14), (64, 256)))
        small = small + jnp.pad(upward_bias[None], ((1, 14), (128, 0)))
        payload, up_payload = call(
            deal_kernel, "deal", [((16, 80, 384), bf16), ((16, 64, 512), bf16)], [],
            0, 4 * 10**6, 0, (attention_weight, small, upward_weight),
        )
        arrived = exchange(payload, FSDP)

    with jax.named_scope("first"):
        inputs = lax.all_gather(block_input, ("y", "c"), axis=0, tiled=True)
        query, heads_own, heads_send, normed_first, normal_first, project, vectors, bias_up = (
            first_heads(shard[None].astype(jnp.int32), inputs, arrived)
        )
        heads_arrived = shift(heads_send, "xh", 1)
    with jax.named_scope("weights_upward"):
        upward_pair = exchange(after(up_payload, arrived), FSDP).reshape(D, 512)
    with jax.named_scope("weights_pair"):
        output_rows = shift(after(output_weight, arrived), "xh", 1)
        downward_rows = shift(after(downward_weight, heads_arrived), "xh", 1)
    with jax.named_scope("cotangents"):
        cotangents = lax.all_gather(after(cotangent, inputs), ("y", "c"), axis=0, tiled=True)

    with jax.named_scope("attention"):
        mixed, lse = attention_forward(half, slopes, query, heads_own, heads_arrived)
    with jax.named_scope("output"):
        mixed = after(mixed, upward_pair)
        mine, other = output_parts(table, mixed, output_weight, output_rows)
        residual_mid, normal_second, inverse_second, normed_second = middle(
            scatter(mine, other), block_input, vectors
        )

    with jax.named_scope("feed"):
        mine, other, activated, upward_grad, seconds = feed_parts(
            table, gather(normed_second), cotangents, upward_pair, downward_weight,
            downward_rows, bias_up,
        )
        ends = scatter(mine, other)

    with jax.named_scope("upward_gradients"):
        upward_weight_grad = dot_tn(seconds, upward_grad).astype(bf16)
        upward_bias_grad = jnp.sum(upward_grad.astype(f32), axis=0).astype(bf16)
        downward_grad = dot_tn(activated, cotangents)
        downward_other = downward_grad[256:].astype(bf16)
    with jax.named_scope("feed"):
        ends = lax.optimization_barrier((*ends, upward_weight_grad, downward_other))[0:4]
        mid_grad, branch_grad, sums = middle_back(
            ends, cotangent, vectors, normal_second, inverse_second
        )
    with jax.named_scope("feed_out"):
        out_all = out_part(activated, downward_weight, downward_rows)
        out = lax.psum_scatter(out_all, ("y", "c"), scatter_dimension=0, tiled=True)
        block_output = block_end(out, residual_mid, vectors)
    with jax.named_scope("mixed_back"):
        pieces = gather(branch_grad)
        pieces = lax.optimization_barrier((*pieces, out_all))[0:8]
        mixed_grad, branch_grads = mixed_back(table, pieces, output_weight, output_rows)

    with jax.named_scope("upward_gradients"):
        quads = sums[0:4].astype(bf16).reshape(4, 16, 64).transpose(1, 0, 2).reshape(16, 2, 128)
        extra = jnp.concatenate(
            [
                quads,
                jnp.broadcast_to(upward_bias_grad.reshape(1, 4, 128), (16, 4, 128)),
                jnp.zeros((16, 2, 128), bf16),
            ],
            axis=1,
        )
        extra = jnp.broadcast_to(extra[:, None], (16, 8, 8, 128)).reshape(1024, 128)
        shares = jnp.concatenate([upward_weight_grad, extra], axis=-1).reshape(128, 8, 640)
        arrived_up = exchange(shares, FSDP + SEQ)
        wide_up = arrived_up.reshape(4, 2, 2, 8, 8, 640).astype(f32)
        up_sum = jnp.sum(wide_up[..., :512], axis=3)
        up_total = up_sum[..., :256] + up_sum[:, ::-1, :, :, 256:]
        up_total = up_total.transpose(3, 0, 1, 2, 4).reshape(8, FF).astype(bf16)
        small_sum = jnp.sum(wide_up[..., 512:], axis=3)
        four_total = jnp.sum(small_sum[:, :, :, 0:2], axis=(0, 1, 2))
        bias_rows = small_sum.reshape(16, 8, 128)[:, 2:6].reshape(16, 512)
        bias_total = (
            lax.dynamic_index_in_dim(bias_rows, shard, 0, keepdims=False)[:256]
            + lax.dynamic_index_in_dim(bias_rows, shard ^ 2, 0, keepdims=False)[256:]
        )
    with jax.named_scope("row_gradients"):
        downward_arrived = shift(downward_other, "xh", 1)
        downward_sum = (downward_grad[:256] + downward_arrived.astype(f32)).astype(bf16)
        output_grad = dot_tn(mixed, branch_grads)
        output_arrived = shift(output_grad[64:].astype(bf16), "xh", 1)
        output_sum = (output_grad[:64] + output_arrived.astype(f32)).astype(bf16)
        rows_all = exchange(
            jnp.concatenate(
                [output_sum.reshape(8, 8, D), downward_sum.reshape(8, 32, D)], axis=1
            ),
            SEQ,
        )
        rows_total = jnp.sum(rows_all.astype(f32), axis=0).astype(bf16)
    with jax.named_scope("early_gradients"):
        early = jnp.concatenate([rows_total, up_total.reshape(32, D)], axis=0)
        early_all = exchange(jnp.broadcast_to(early[None], (8, 72, D)), SEQ)
        wide_early = early_all.astype(f32)
        output_weight_gradient = wide_early[:, :8].reshape(64, D)
        downward_weight_gradient = wide_early[:, 8:40].reshape(256, D)
        upward_weight_gradient = wide_early[:, 40:].reshape(64, FF)

    with jax.named_scope("attention_back"):
        query_grad, back_own, back_send = attention_backward(
            half, slopes, query, heads_own, heads_arrived, mixed_grad, lse
        )
        back_arrived = shift(back_send, "xh", 1)
    with jax.named_scope("first_back"):
        back_arrived = after(back_arrived, rows_all, arrived_up)
        mine, other, joined, last_sums = last_parts(
            table, query_grad, back_own, back_arrived, project, normal_first
        )
        ends = scatter(mine, other)
        input_gradient = input_end(ends, block_input, vectors, mid_grad)
    with jax.named_scope("attention_gradients"):
        weight_grad = dot_tn(normed_first, joined).astype(bf16)
        low_sums = last_sums.astype(bf16)
        quads = low_sums[0:2].reshape(2, 16, 64).transpose(1, 0, 2)
        biases = jnp.stack([low_sums[2, 0:128], low_sums[2, 256:384]])
        extra = jnp.concatenate(
            [
                quads.reshape(16, 1, 128),
                jnp.broadcast_to(biases[None], (16, 2, 128)),
                jnp.zeros((16, 5, 128), bf16),
            ],
            axis=1,
        )
        extra = jnp.broadcast_to(extra[:, None], (16, 8, 8, 128)).reshape(1024, 128)
        shares = jnp.concatenate([weight_grad, extra], axis=-1).reshape(128, 8, 512)
        shares = after(shares, ends[0])
        arrived_last = exchange(shares, FSDP + SEQ).reshape(4, 2, 2, 8, 8, 512).astype(f32)
        last_sum = jnp.sum(arrived_last, axis=3)
        pairs = last_sum[..., :384].reshape(4, 2, 2, 8, 3, 2, HEAD)
        last_total = pairs[..., 0, :] + pairs[:, ::-1, :, :, :, 1]
        last_total = last_total.reshape(16, 8, 3, HEAD).transpose(1, 2, 0, 3).reshape(8, 3 * D)
        late = last_total.astype(bf16).reshape(24, D)
        late = after(late, early_all)
        late_all = exchange(jnp.broadcast_to(late[None], (8, 24, D)), SEQ).astype(f32)
        attention_weight_gradient = late_all.reshape(64, 3 * D)
        last_small = last_sum[..., 384:].reshape(16, 8, 128)
        first_total = jnp.sum(last_small[:, 0], axis=0)
        bias_mine = lax.dynamic_index_in_dim(last_small, shard, 0, keepdims=False)
        bias_twin = lax.dynamic_index_in_dim(last_small, shard ^ 2, 0, keepdims=False)
        bias_pair = bias_mine[1:3, :64] + bias_twin[1:3, 64:]

    return (
        block_output,
        input_gradient,
        first_total[:64],
        first_total[64:],
        attention_weight_gradient,
        bias_pair[0],
        bias_pair[1],
        output_weight_gradient,
        four_total[1, :64],
        four_total[0, :64],
        four_total[0, 64:],
        upward_weight_gradient,
        bias_total,
        downward_weight_gradient,
        four_total[1, 64:],
    )


def solution(mesh):
    grid = Mesh(mesh.devices.reshape(4, 2, 4, 2, 2), ALL)
    tokens = P(ALL, None)
    rows = P(FSDP, None)
    line = P(FSDP)
    return jax.shard_map(
        on_device,
        mesh=grid,
        in_specs=(
            tokens, line, line, rows, line, line, rows, line, line, line, rows, line, rows, line,
            tokens,
        ),
        out_specs=(
            tokens, tokens, line, line, rows, line, line, rows, line, line, line, rows, line, rows,
            line,
        ),
        check_vma=False,
    )
```

```python
import jax
import jax.numpy as jnp
import numpy as np
from jax import lax
from jax.experimental import pallas as pl
from jax.experimental.pallas import tpu as pltpu
from jax.sharding import Mesh
from jax.sharding import PartitionSpec as P

D = 1024
HEADS = 16
HEAD = 64
FF = 4096

epsilon = 1e-05
score_scale = 0.125
bf16 = jnp.bfloat16
f32 = jnp.float32

SEQ = ("z", "xl")
FSDP = ("y", "xh", "c")
ALL = SEQ + FSDP
ROWS = 128
TILE = 256
TILES = 8
LENGTH = TILE * TILES

NT = (((1,), (1,)), ((), ()))


def dot(a, b):
    return jnp.dot(a, b, preferred_element_type=f32)


def dot_nt(a, b):
    return lax.dot_general(a, b, NT, preferred_element_type=f32)


def dot_tn(a, b):
    return lax.dot_general(a, b, (((0,), (0,)), ((), ())), preferred_element_type=f32)


smem = pl.BlockSpec(memory_space=pltpu.SMEM)
vmem = pl.BlockSpec(memory_space=pltpu.VMEM)


def call(kernel, name, outs, scratch, flops, moved, transcendentals, args, scalars=0, pieces=0):
    rest = len(args) - scalars - pieces
    return pl.pallas_call(
        kernel,
        out_shape=tuple(jax.ShapeDtypeStruct(shape, kind) for shape, kind in outs),
        in_specs=[smem] * scalars + [pl.BlockSpec(memory_space=pl.ANY)] * pieces + [vmem] * rest,
        out_specs=(vmem,) * len(outs),
        scratch_shapes=[
            pltpu.VMEM(*item) if isinstance(item, tuple) else item for item in scratch
        ],
        compiler_params=pltpu.CompilerParams(vmem_limit_bytes=60 * 2**20),
        cost_estimate=pl.CostEstimate(
            flops=flops, bytes_accessed=moved, transcendentals=transcendentals
        ),
        name=name,
    )(*args)


def place(table, p):
    return pl.multiple_of(table[p] * ROWS, ROWS)


def assemble(table, refs, out, sems):
    copies = [
        pltpu.make_async_copy(refs[p], out.at[pl.ds(place(table, p), ROWS), :], sems.at[p])
        for p in range(8)
    ]
    for copy in copies:
        copy.start()
    return copies


def rows_of(table, ref, p):
    return jnp.concatenate(
        [ref[pl.ds(place(table, p + b), ROWS), :] for b in range(2)], axis=0
    )


def set_rows(table, ref, p, value):
    for b in range(2):
        ref[pl.ds(place(table, p + b), ROWS), :] = value[b * ROWS : (b + 1) * ROWS]


def put_parts(mine_ref, other_ref, chunk, value):
    ref = mine_ref if chunk < 2 else other_ref
    for b in range(2):
        ref[2 * (chunk % 2) + b] = value[b * ROWS : (b + 1) * ROWS].astype(ref.dtype)


PARTS = [((4, ROWS, D), bf16), ((4, ROWS, D), bf16)]
ORDER = (2, 3, 0, 1)


def deal_kernel(weight_ref, small_ref, up_ref, out_ref, up_out):
    small = small_ref[...]

    def piece(kind, head):
        start = kind * D + head * HEAD
        return weight_ref[:, start : start + HEAD]

    for y in range(4):
        for x in range(2):
            for c in range(2):
                shard = 4 * y + 2 * x + c
                twin = shard ^ 2
                out_ref[shard, 0:64, :] = jnp.concatenate(
                    [
                        piece(kind, head) for kind in range(3) for head in (shard, twin)
                    ],
                    axis=1,
                )
                out_ref[shard, 64:80, :] = small
                up_out[shard, :, 0:256] = up_ref[:, 256 * shard : 256 * shard + 256]
                up_out[shard, :, 256:512] = up_ref[:, 256 * twin : 256 * twin + 256]


def swap(pairs):
    return jnp.concatenate(
        [pairs[:, 64:128], pairs[:, 0:64], pairs[:, 192:256], pairs[:, 128:192]], axis=1
    )


def first_kernel(table, shard_ref, *refs):
    pieces, arrived = refs[0:8], refs[8]
    kv_ref, send_ref, normed_ref, normal_ref, project_ref, vector_ref, bias_ref = refs[9:16]
    inputs, sems = refs[16:18]
    copies = assemble(table, pieces, inputs, sems)
    for r in range(16):
        project_ref[64 * r : 64 * r + 64, :] = arrived[r, 0:64, :]
    rows = [arrived[r, 64:80, :].astype(f32) for r in range(16)]
    for g in range(6):
        vector_ref[g : g + 1, :] = jnp.concatenate(
            [rows[r][0:1, 64 * g : 64 * g + 64] for r in range(16)], axis=1
        )
    shard = shard_ref[0]
    mine = arrived[shard, 64:80, :].astype(f32)[1:2]
    twin = arrived[shard ^ 2, 64:80, :].astype(f32)[1:2]
    bias_ref[0:1, :] = jnp.concatenate([mine[:, 128:], twin[:, 128:]], axis=1)
    bias_ref[1:2, 0:128] = jnp.concatenate([mine[:, 0:64], twin[:, 0:64]], axis=1)
    bias = jnp.concatenate(
        [jnp.zeros((1, 2 * HEAD), f32), mine[:, 64:128], twin[:, 64:128]], axis=1
    )
    gain = vector_ref[0:1, :]
    offset = vector_ref[1:2, :]
    for copy in copies:
        copy.wait()
    for chunk in range(4):
        rows = slice(chunk * TILE, (chunk + 1) * TILE)
        normal, unused = normalize(inputs[rows, :].astype(f32))
        normal_ref[rows, :] = normal.astype(bf16)
        normed = (normal * gain + offset).astype(bf16)
        normed_ref[rows, :] = normed
        heads = (dot(normed, project_ref[:, 128:384]) + bias).astype(bf16)
        kv_ref[rows, :] = heads
        send_ref[rows, :] = swap(heads)


def query_kernel(normed_ref, project_ref, bias_ref, query_ref):
    bias = bias_ref[1:2, 0:128]
    for chunk in range(4):
        rows = slice(chunk * TILE, (chunk + 1) * TILE)
        value = dot(normed_ref[rows, :], project_ref[:, 0:128]) + bias
        query_ref[rows, :] = value.astype(bf16)


def queries(normed, project, bias):
    return call(
        query_kernel, "queries", [((1024, 128), bf16)], [], 27 * 10**7, 3 * 10**6, 0,
        (normed, project, bias),
    )[0]


def first_heads(table, shard, pieces, arrived):
    return call(
        first_kernel, "first_heads",
        [
            ((1024, 256), bf16), ((1024, 256), bf16), ((1024, D), bf16), ((1024, D), bf16),
            ((D, 384), bf16), ((8, D), f32), ((8, 512), f32),
        ],
        [((1024, D), bf16), pltpu.SemaphoreType.DMA((8,))],
        8 * 10**8, 10**7, 10**4, (table, shard, *pieces, arrived), 2, 8,
    )


def in_head(shape, head):
    lane = lax.broadcasted_iota(jnp.int32, shape, 1)
    return (lane < HEAD) if head == 0 else (lane >= HEAD)


def stage_queries(query, head):
    lane = lax.broadcasted_iota(jnp.int32, query.shape, 1) - (HEAD if head == 0 else 0)
    ones = jnp.where((lane >= 0) & (lane < 3), 1.0, 0.0)
    scaled = query.astype(f32) * score_scale
    return jnp.where(in_head(query.shape, head), scaled, ones).astype(bf16)


def stage_keys(key, head, slope, first):
    shape = key.shape
    lane = lax.broadcasted_iota(jnp.int32, shape, 1) - (HEAD if head == 0 else 0)
    row = lax.broadcasted_iota(jnp.int32, shape, 0)
    place = slope * (row + first).astype(f32)
    high = place.astype(bf16).astype(f32)
    rest = place - high
    middle = rest.astype(bf16).astype(f32)
    low = rest - middle
    extra = jnp.where(
        lane == 0, high, jnp.where(lane == 1, middle, jnp.where(lane == 2, low, 0.0))
    )
    return jnp.where(in_head(shape, head), key.astype(f32), extra).astype(bf16)


def fold(tile, op):
    parts = [tile[8 * g : 8 * g + 8] for g in range(TILE // 8)]
    while len(parts) > 1:
        parts = [op(parts[2 * g], parts[2 * g + 1]) for g in range(len(parts) // 2)]
    return parts[0]


def future():
    key = lax.broadcasted_iota(jnp.int32, (TILE, TILE), 0)
    query = lax.broadcasted_iota(jnp.int32, (TILE, TILE), 1)
    return key > query


def tile_rows(t):
    return slice(t * TILE, (t + 1) * TILE)


def stage(half, slopes, own_ref, other_ref, ka, emit_rest):
    for t in range(4):
        for side, ref in enumerate((own_ref, other_ref)):
            slot = tile_rows(2 * t + side)
            pair = ref[tile_rows(t), :]
            first = TILE * (2 * t + (half[0] if side == 0 else 1 - half[0])) - LENGTH // 2
            for head in range(2):
                ka[head, slot, :] = stage_keys(pair[:, 0:128], head, slopes[head], first)
            emit_rest(slot, pair)


def masked(s, t, slot, hidden, ahead):
    if slot == 2 * t:
        return jnp.where(hidden, -1e30, s)
    return s + ahead if slot == 2 * t + 1 else s


def forward_kernel(half, slopes, q_ref, own_ref, other_ref, out_ref, lse_ref, ka, vt, s_sc, p_sc):
    def rest(slot, pair):
        vt[:, slot] = pair[:, 128:256].astype(f32).T.astype(bf16)

    stage(half, slopes, own_ref, other_ref, ka, rest)
    hidden = future()
    ahead = jnp.where(half[0] == 1, 0.0, -1e30)
    for t in range(4):
        query = q_ref[tile_rows(t), :]
        n = (2 * t + 2) * TILE
        outs = []
        for head in range(2):
            q = stage_queries(query, head)
            peak = None
            for slot in range(2 * t + 2):
                rows = tile_rows(slot)
                s = masked(dot_nt(ka[head, rows, :], q), t, slot, hidden, ahead)
                s_sc[head, rows, :] = s
                top = fold(s, jnp.maximum)
                peak = top if peak is None else jnp.maximum(peak, top)
            peak = jnp.max(peak, axis=0, keepdims=True)
            total = None
            for slot in range(2 * t + 2):
                rows = tile_rows(slot)
                p = jnp.exp(s_sc[head, rows, :] - peak)
                p_sc[head, rows, :] = p.astype(bf16)
                part = fold(p, jnp.add)
                total = part if total is None else total + part
            total = jnp.sum(total, axis=0, keepdims=True)
            outs.append(dot(vt[head * HEAD : (head + 1) * HEAD, 0:n], p_sc[head, 0:n, :]) / total)
            lse_ref[2 * t + head] = peak + jnp.log(total)
        out_ref[tile_rows(t), :] = jnp.concatenate(outs, axis=0).T.astype(bf16)


def attention_forward(half, slopes, query, own, other):
    return call(
        forward_kernel, "attention_forward",
        [((1024, 128), bf16), ((8, 1, TILE), f32)],
        [
            ((2, LENGTH, 128), bf16), ((128, LENGTH), bf16), ((2, LENGTH, TILE), f32),
            ((2, LENGTH, TILE), bf16),
        ],
        3 * 10**9, 2 * 10**6, 24 * 10**5, (half, slopes, query, own, other), 2,
    )


def backward_kernel(
    half, slopes, q_ref, own_ref, other_ref, grad_ref, lse_ref,
    dq_ref, down_ref, send_ref,
    ka, kt, va, dk, dv, p_sc, dp_sc, ds_sc,
):
    def rest(slot, pair):
        va[slot, :] = pair[:, 128:256]
        kt[:, slot] = pair[:, 0:128].astype(f32).T.astype(bf16)

    stage(half, slopes, own_ref, other_ref, ka, rest)
    hidden = future()
    ahead = jnp.where(half[0] == 1, 0.0, -1e30)
    for t in range(4):
        query = q_ref[tile_rows(t), :]
        grad = grad_ref[tile_rows(t), :]
        n = (2 * t + 2) * TILE
        grads = [
            jnp.where(in_head(grad.shape, head), grad.astype(f32), 0.0).astype(bf16)
            for head in range(2)
        ]
        plain = [
            jnp.where(in_head(query.shape, head), query.astype(f32) * score_scale, 0.0).astype(bf16)
            for head in range(2)
        ]
        queries = [stage_queries(query, head) for head in range(2)]
        grad_rows = jnp.concatenate(grads, axis=0)
        plain_rows = jnp.concatenate(plain, axis=0)
        delta = [None, None]
        for slot in range(2 * t + 2):
            rows = tile_rows(slot)
            low = []
            for head in range(2):
                s = masked(dot_nt(ka[head, rows, :], queries[head]), t, slot, hidden, ahead)
                p = jnp.exp(s - lse_ref[2 * t + head])
                dp = dot_nt(va[rows, :], grads[head])
                p_sc[head, rows, :] = p
                dp_sc[head, rows, :] = dp
                part = fold(p * dp, jnp.add)
                delta[head] = part if delta[head] is None else delta[head] + part
                low.append(p.astype(bf16))
            value = dot(jnp.concatenate(low, axis=1), grad_rows)
            dv[rows, :] = value if slot >= 2 * t else dv[rows, :] + value
        delta = [jnp.sum(item, axis=0, keepdims=True) for item in delta]
        for slot in range(2 * t + 2):
            rows = tile_rows(slot)
            low = []
            for head in range(2):
                ds = (p_sc[head, rows, :] * (dp_sc[head, rows, :] - delta[head])).astype(bf16)
                ds_sc[head, rows, :] = ds
                low.append(ds)
            key = dot(jnp.concatenate(low, axis=1), plain_rows)
            dk[rows, :] = key if slot >= 2 * t else dk[rows, :] + key
        outs = [
            dot(kt[head * HEAD : (head + 1) * HEAD, 0:n], ds_sc[head, 0:n, :]) for head in range(2)
        ]
        dq_ref[tile_rows(t), :] = (jnp.concatenate(outs, axis=0) * score_scale).T.astype(bf16)
    for t in range(4):
        rows = tile_rows(t)
        down_ref[rows, 0:128] = dk[tile_rows(2 * t), :]
        down_ref[rows, 128:256] = dv[tile_rows(2 * t), :]
        pair = jnp.concatenate([dk[tile_rows(2 * t + 1), :], dv[tile_rows(2 * t + 1), :]], axis=1)
        send_ref[rows, :] = swap(pair.astype(bf16))


def attention_backward(half, slopes, query, own, other, grad, lse):
    return call(
        backward_kernel, "attention_backward",
        [((1024, 128), bf16), ((1024, 256), f32), ((1024, 256), bf16)],
        [
            ((2, LENGTH, 128), bf16), ((128, LENGTH), bf16), ((LENGTH, 128), bf16),
            ((LENGTH, 128), f32), ((LENGTH, 128), f32), ((2, LENGTH, TILE), f32),
            ((2, LENGTH, TILE), f32), ((2, LENGTH, TILE), bf16),
        ],
        6 * 10**9, 3 * 10**6, 24 * 10**5, (half, slopes, query, own, other, grad, lse), 2,
    )


def output_kernel(table, mixed_ref, weight_ref, rows_ref, mine_part, other_part):
    weight = jnp.concatenate([weight_ref[...], rows_ref[...]], axis=0)
    for chunk in ORDER:
        put_parts(mine_part, other_part, chunk, dot(rows_of(table, mixed_ref, 2 * chunk), weight))


def output_parts(table, mixed, weight, rows):
    return call(
        output_kernel, "output_parts", PARTS, [], 27 * 10**7, 4 * 10**6, 0,
        (table, mixed, weight, rows), 1,
    )


def feed_kernel(table, *refs):
    up_ref, down_ref, rows_ref, bias_ref = refs[16:20]
    mine_part, other_part, act_ref, grad_ref, second_ref, cotangent_ref, sum_ref = refs[20:27]
    sems, more = refs[27:29]
    copies = assemble(table, refs[0:8], second_ref, sems)
    cotangent_copies = assemble(table, refs[8:16], cotangent_ref, more)
    bias = bias_ref[0:1, :]
    for chunk in ORDER:
        cotangent_copies[2 * chunk].wait()
        cotangent_copies[2 * chunk + 1].wait()
        cotangents = rows_of(table, cotangent_ref, 2 * chunk)
        back = jnp.concatenate(
            [dot_nt(cotangents, down_ref[...]), dot_nt(cotangents, rows_ref[...])], axis=1
        )
        copies[2 * chunk].wait()
        copies[2 * chunk + 1].wait()
        up = dot(rows_of(table, second_ref, 2 * chunk), up_ref[...]) + bias
        square = up * up
        bend = jnp.tanh(0.7978845608028654 * (up + 0.044715 * square * up))
        half = 0.5 * (1.0 + bend)
        set_rows(table, act_ref, 2 * chunk, (up * half).astype(bf16))
        slope = half + 0.5 * up * (1.0 - bend * bend) * (
            0.7978845608028654 * (1.0 + 0.134145 * square)
        )
        grad = (back * slope).astype(bf16)
        set_rows(table, grad_ref, 2 * chunk, grad)
        part = jnp.sum(grad.astype(f32), axis=0, keepdims=True)
        total = part if chunk == ORDER[0] else total + part
        put_parts(mine_part, other_part, chunk, dot_nt(grad, up_ref[...]))
    sum_ref[0:1, :] = total


def feed_parts(table, pieces, cotangents, up, down, rows, bias):
    return call(
        feed_kernel, "feed_parts", PARTS + [((1024, 512), bf16)] * 2 + [((1024, D), bf16)] * 2 + [((8, 512), f32)],
        [pltpu.SemaphoreType.DMA((8,)), pltpu.SemaphoreType.DMA((8,))],
        32 * 10**8, 2 * 10**7, 5 * 10**5, (table, *pieces, *cotangents, up, down, rows, bias), 1,
        16,
    )


def out_kernel(table, act_ref, down_ref, rows_ref, mine_part, other_part):
    for chunk in ORDER:
        act = rows_of(table, act_ref, 2 * chunk)
        value = dot(act[:, 0:256], down_ref[...]) + dot(act[:, 256:512], rows_ref[...])
        put_parts(mine_part, other_part, chunk, value)


def out_parts(table, act, down, rows):
    return call(
        out_kernel, "out_parts", PARTS, [], 11 * 10**8, 5 * 10**6, 0, (table, act, down, rows), 1
    )


def mixed_kernel(table, *refs):
    pieces, weight_ref, rows_ref = refs[0:8], refs[8], refs[9]
    grad_ref, all_ref, sems = refs[10:13]
    copies = assemble(table, pieces, all_ref, sems)
    weight = jnp.concatenate([weight_ref[...], rows_ref[...]], axis=0)
    for chunk in range(4):
        copies[2 * chunk].wait()
        copies[2 * chunk + 1].wait()
        grads = dot_nt(rows_of(table, all_ref, 2 * chunk), weight).astype(bf16)
        set_rows(table, grad_ref, 2 * chunk, grads)


def mixed_back(table, pieces, weight, rows):
    return call(
        mixed_kernel, "mixed_back",
        [((1024, 128), bf16), ((1024, D), bf16)],
        [pltpu.SemaphoreType.DMA((8,))],
        27 * 10**7, 4 * 10**6, 0, (table, *pieces, weight, rows), 1, 8,
    )


def last_kernel(
    table, query_ref, own_ref, other_ref, project_ref, normal_ref,
    mine_part, other_part, joined_ref, extra_ref,
):
    gain = None
    for chunk in ORDER:
        own = rows_of(table, own_ref, 2 * chunk)
        other = rows_of(table, other_ref, 2 * chunk).astype(f32)
        joined = jnp.concatenate(
            [rows_of(table, query_ref, 2 * chunk), (own + other).astype(bf16)], axis=1
        )
        set_rows(table, joined_ref, 2 * chunk, joined)
        bias = jnp.sum(joined.astype(f32), axis=0, keepdims=True)
        biases = bias if chunk == ORDER[0] else biases + bias
        value = dot_nt(joined, project_ref[...])
        put_parts(mine_part, other_part, chunk, value)
        normal = rows_of(table, normal_ref, 2 * chunk).astype(f32)
        tilted = jnp.sum(value * normal, axis=0, keepdims=True)
        plain = jnp.sum(value, axis=0, keepdims=True)
        gain = tilted if gain is None else gain + tilted
        offset = plain if chunk == ORDER[0] else offset + plain
    extra_rows(extra_ref, [(gain, offset)], [biases[:, 0:128], biases[:, 256:384]])


def last_parts(table, query, own, other, project, normal):
    return call(
        last_kernel, "last_parts", PARTS + [((1024, 384), bf16), ((1024, 128), bf16)], [],
        8 * 10**8, 7 * 10**6, 0, (table, query, own, other, project, normal), 1,
    )


def extra_rows(out_ref, pairs, lines):
    row = lax.broadcasted_iota(jnp.int32, (64, 128), 0) % 8
    for shard in range(16):
        columns = slice(64 * shard, 64 * shard + 64)
        block = jnp.zeros((64, 128), f32)
        for r, (left, right) in enumerate(pairs):
            line = jnp.concatenate([left[:, columns], right[:, columns]], axis=1)
            block = jnp.where(row == r, line, block)
        for r, line in enumerate(lines):
            block = jnp.where(row == len(pairs) + r, line, block)
        out_ref[64 * shard : 64 * shard + 64, :] = block.astype(bf16)


def join_kernel(mine_ref, core_ref, here_ref, near_ref, far_ref, back_ref):
    for d, ref in enumerate((here_ref, near_ref, far_ref, back_ref)):
        ref[...] = (mine_ref[d] + core_ref[d].astype(f32)).astype(ref.dtype)


def join(mine, core):
    return call(
        join_kernel, "join", [((ROWS, D), f32)] + [((ROWS, D), bf16)] * 3, [], 10**6, 4 * 10**6, 0,
        (mine, core),
    )


def landed(refs):
    here, near, far, back = [ref[...].astype(f32) for ref in refs]
    return here + near + far + back


def middle_kernel(*refs):
    input_ref, vector_ref, mid_ref, normal_ref, inverse_ref, normed_ref = refs[4:10]
    mid = input_ref[...].astype(f32) + (landed(refs[0:4]) + vector_ref[2:3, :])
    normal, inverse = normalize(mid)
    mid_ref[...] = mid
    normal_ref[...] = normal
    inverse_ref[...] = inverse
    normed_ref[...] = (normal * vector_ref[3:4, :] + vector_ref[4:5, :]).astype(bf16)


def middle(ends, inputs, vectors):
    return call(
        middle_kernel, "middle",
        [((ROWS, D), f32), ((ROWS, D), f32), ((ROWS, 1), f32), ((ROWS, D), bf16)], [],
        10**6, 3 * 10**6, 0, (*ends, inputs, vectors),
    )


def middle_back_kernel(*refs):
    cotangent_ref, vector_ref, normal_ref, inverse_ref, bias_ref = refs[4:9]
    grad_ref, branch_ref, extra_ref = refs[9:12]
    second = landed(refs[0:4])
    normal = normal_ref[...]
    cotangent = cotangent_ref[...].astype(f32)
    grad = cotangent + norm_back(second, vector_ref[3:4, :], normal, inverse_ref[...])
    grad_ref[...] = grad
    branch = grad.astype(bf16)
    branch_ref[...] = branch
    pairs = [
        (jnp.sum(second * normal, axis=0, keepdims=True), jnp.sum(second, axis=0, keepdims=True)),
        (
            jnp.sum(branch.astype(f32), axis=0, keepdims=True),
            jnp.sum(cotangent, axis=0, keepdims=True),
        ),
    ]
    extra_rows(extra_ref, pairs, [bias_ref[0:1, 128 * g : 128 * g + 128] for g in range(4)])


def middle_back(ends, cotangent, vectors, normal, inverse, sums):
    return call(
        middle_back_kernel, "middle_back",
        [((ROWS, D), f32), ((ROWS, D), bf16), ((1024, 128), bf16)], [],
        10**6, 3 * 10**6, 0, (*ends, cotangent, vectors, normal, inverse, sums),
    )


def block_kernel(*refs):
    mid_ref, vector_ref, out_ref = refs[4:7]
    out_ref[...] = (mid_ref[...] + landed(refs[0:4]) + vector_ref[5:6, :]).astype(bf16)


def block_end(ends, mid, vectors):
    return call(
        block_kernel, "block_end", [((ROWS, D), bf16)], [], 10**6, 2 * 10**6, 0,
        (*ends, mid, vectors),
    )[0]


def input_kernel(*refs):
    input_ref, vector_ref, grad_ref, out_ref = refs[4:8]
    normal, inverse = normalize(input_ref[...].astype(f32))
    out_ref[...] = grad_ref[...] + norm_back(
        landed(refs[0:4]), vector_ref[0:1, :], normal, inverse
    )


def input_end(ends, inputs, vectors, grad):
    return call(
        input_kernel, "input_end", [((ROWS, D), f32)], [], 10**6, 3 * 10**6, 0,
        (*ends, inputs, vectors, grad),
    )[0]


def totals_kernel(whose, rows_ref, up_ref, last_ref, total_ref, small_ref, up_small, last_small):
    def over_seq(ref, shard, columns):
        value = ref[8 * shard, :, columns].astype(f32)
        for q in range(1, 8):
            value = value + ref[8 * shard + q, :, columns].astype(f32)
        return value

    rows = rows_ref[0].astype(f32)
    for q in range(1, 8):
        rows = rows + rows_ref[q].astype(f32)
    ups, lasts = [], []
    for shard in range(16):
        up_small[shard] = over_seq(up_ref, shard, slice(512, 640))
        last_small[shard] = over_seq(last_ref, shard, slice(384, 512))
        lasts.append(over_seq(last_ref, shard, slice(0, 384)))
        ups.append(over_seq(up_ref, shard, slice(0, 512)))
    pieces = [rows]
    for block in range(4):
        pieces.append(
            jnp.concatenate(
                [
                    ups[shard][:, 0:256] + ups[shard ^ 2][:, 256:512]
                    for shard in range(4 * block, 4 * block + 4)
                ],
                axis=1,
            )
        )
    for kind in range(3):
        start = 128 * kind
        pieces.append(
            jnp.concatenate(
                [
                    lasts[shard][:, start : start + 64]
                    + lasts[shard ^ 2][:, start + 64 : start + 128]
                    for shard in range(16)
                ],
                axis=1,
            )
        )
    total = jnp.concatenate(pieces, axis=0).astype(bf16)
    for q in range(8):
        total_ref[q] = total
    up_sum, last_sum = up_small[0], last_small[0]
    for shard in range(1, 16):
        up_sum = up_sum + up_small[shard]
        last_sum = last_sum + last_small[shard]
    mine, twin = last_small[whose[0]], last_small[whose[0] ^ 2]
    up_mine, up_twin = up_small[whose[0]], up_small[whose[0] ^ 2]
    small_ref[0:1, 0:128] = last_sum[0:1]
    small_ref[1:3, 0:128] = up_sum[0:2]
    small_ref[3:4, 0:128] = jnp.concatenate(
        [mine[1:2, 0:64] + twin[1:2, 64:128], mine[2:3, 0:64] + twin[2:3, 64:128]], axis=1
    )
    small_ref[4:5, :] = jnp.concatenate(
        [up_mine[2:3] + up_twin[4:5], up_mine[3:4] + up_twin[5:6]], axis=1
    )


def totals(whose, rows, up, last):
    return call(
        totals_kernel, "totals", [((8, 96, D), bf16), ((8, 256), f32)],
        [((16, 8, 128), f32), ((16, 8, 128), f32)],
        2 * 10**6, 6 * 10**6, 0, (whose, rows, up, last), 1,
    )


def deal_out_kernel(total_ref, output_ref, down_ref, up_ref, attention_ref):
    for q in range(8):
        total = total_ref[q].astype(f32)
        output_ref[8 * q : 8 * q + 8, :] = total[0:8]
        down_ref[32 * q : 32 * q + 32, :] = total[8:40]
        for block in range(4):
            up_ref[8 * q : 8 * q + 8, D * block : D * block + D] = total[
                40 + 8 * block : 48 + 8 * block
            ]
        for kind in range(3):
            attention_ref[8 * q : 8 * q + 8, D * kind : D * kind + D] = total[
                72 + 8 * kind : 80 + 8 * kind
            ]


def deal_out(total):
    return call(
        deal_out_kernel, "deal_out",
        [((64, D), f32), ((256, D), f32), ((64, FF), f32), ((64, 3 * D), f32)], [],
        10**6, 5 * 10**6, 0, (total,),
    )


def shift(value, axis, step):
    size = lax.axis_size(axis)
    return lax.ppermute(value, axis, [(i, (i + step) % size) for i in range(size)])


def gather(own, *first):
    mine = [shift(own, "y", -step) for step in (1, 2, 3)]
    if first:
        mine = list(lax.optimization_barrier((*mine, *first))[0:3])
    mine = [own, *mine]
    return mine + [shift(block, "c", 1) for block in mine]


def joined(mine, other, *first):
    core = shift(other, "c", 1)
    return join(mine, after(core, *first) if first else core)


def spread(here, near, far, back):
    return here, shift(near, "y", 1), shift(far, "y", 2), shift(back, "y", 3)


def scatter(mine, other, *first):
    return spread(*joined(mine, other, *first))


def exchange(value, axes):
    return lax.all_to_all(value, axes, split_axis=0, concat_axis=0, tiled=True)


def after(value, *others):
    return lax.optimization_barrier((value, *others))[0]


def normalize(values):
    centre = jnp.mean(values, axis=-1, keepdims=True)
    centred = values - centre
    spread = jnp.mean(centred * centred, axis=-1, keepdims=True)
    inverse = lax.rsqrt(spread + epsilon)
    return centred * inverse, inverse


def norm_back(grad, gain, normal, inverse):
    scaled = grad * gain
    return inverse * (
        scaled
        - jnp.mean(scaled, axis=-1, keepdims=True)
        - normal * jnp.mean(scaled * normal, axis=-1, keepdims=True)
    )


def on_device(
    block_input,
    first_gain,
    first_shift,
    attention_weight,
    query_bias,
    value_bias,
    output_weight,
    output_bias,
    second_gain,
    second_shift,
    upward_weight,
    upward_bias,
    downward_weight,
    downward_bias,
    cotangent,
):
    y = lax.axis_index("y")
    xh = lax.axis_index("xh")
    c = lax.axis_index("c")
    shard = 4 * y + 2 * xh + c
    piece = np.arange(8)
    table = (2 * ((y + piece % 4) % 4) + (c ^ (piece // 4))).astype(jnp.int32)
    half = xh[None].astype(jnp.int32)
    whose = shard[None].astype(jnp.int32)
    slopes = jnp.exp2(-8.0 * (jnp.stack([shard, shard ^ 2]) + 1).astype(f32) / HEADS)

    with jax.named_scope("weights_attention"):
        vectors_own = [
            first_gain, first_shift, output_bias, second_gain, second_shift, downward_bias
        ]
        small = sum(
            jnp.pad(item[None], ((0, 15), (64 * g, 320 - 64 * g)))
            for g, item in enumerate(vectors_own)
        )
        small = small + jnp.pad(query_bias[None], ((1, 14), (0, 320)))
        small = small + jnp.pad(value_bias[None], ((1, 14), (64, 256)))
        small = small + jnp.pad(upward_bias[None], ((1, 14), (128, 0)))
        payload, up_payload = call(
            deal_kernel, "deal", [((16, 80, 384), bf16), ((16, 64, 512), bf16)], [],
            0, 4 * 10**6, 0, (attention_weight, small, upward_weight),
        )
        arrived = exchange(payload, FSDP)

    with jax.named_scope("first"):
        inputs = gather(block_input)
        cotangents = gather(after(cotangent, *inputs[1:4]))
        heads_own, heads_send, normed_first, normal_first, project, vectors, bias_up = (
            first_heads(table, whose, inputs, after(arrived, *cotangents[1:4]))
        )
        query = queries(normed_first, project, bias_up)
        heads_arrived = shift(heads_send, "xh", 1)
    with jax.named_scope("weights_upward"):
        upward_pair = exchange(after(up_payload, query), FSDP).reshape(D, 512)
    with jax.named_scope("weights_pair"):
        output_rows = shift(after(output_weight, arrived), "xh", 1)
        downward_rows = shift(after(downward_weight, heads_arrived), "xh", 1)
    with jax.named_scope("attention"):
        heads_arrived = after(heads_arrived, *cotangents)
        mixed, lse = attention_forward(half, slopes, query, heads_own, heads_arrived)
    with jax.named_scope("output"):
        mixed = after(mixed, upward_pair)
        mine, other = output_parts(table, mixed, output_weight, output_rows)
        residual_mid, normal_second, inverse_second, normed_second = middle(
            scatter(mine, other), block_input, vectors
        )

    with jax.named_scope("feed"):
        mine, other, activated, upward_grad, seconds, all_cotangents, bias_sums = feed_parts(
            table, gather(normed_second), cotangents, upward_pair, downward_weight,
            downward_rows, bias_up,
        )
        sums_near = joined(mine, other)
        ends = spread(*sums_near)

    with jax.named_scope("upward_gradients"):
        late_grad, late_act = lax.optimization_barrier((upward_grad, activated, sums_near[0]))[0:2]
        upward_weight_grad = dot_tn(seconds, late_grad).astype(bf16)
        downward_grad = dot_tn(late_act, all_cotangents)
        downward_other = downward_grad[256:].astype(bf16)
    with jax.named_scope("feed"):
        ends = lax.optimization_barrier(
            (*ends, upward_weight_grad, downward_other)
        )[0:4]
        mid_grad, branch_grad, extra = middle_back(
            ends, cotangent, vectors, normal_second, inverse_second, bias_sums
        )

    with jax.named_scope("upward_gradients"):
        shares = jnp.concatenate([upward_weight_grad, extra], axis=-1).reshape(128, 8, 640)
    with jax.named_scope("feed_out"):
        out_mine, out_other = out_parts(table, activated, downward_weight, downward_rows)
    with jax.named_scope("mixed_back"):
        mixed_grad, branch_grads = mixed_back(
            table, gather(branch_grad, shares, out_mine), output_weight, output_rows
        )
    with jax.named_scope("attention_back"):
        query_grad, back_own, back_send = attention_backward(
            half, slopes, query, heads_own, heads_arrived, mixed_grad, lse
        )
        back_arrived = shift(back_send, "xh", 1)
    with jax.named_scope("feed_out"):
        out_near = joined(out_mine, after(out_other, back_send))
        out_ends = spread(*out_near)
        block_output = block_end(out_ends, residual_mid, vectors)
    with jax.named_scope("upward_sums"):
        arrived_up = exchange(shares, FSDP + SEQ)
    with jax.named_scope("row_gradients"):
        downward_arrived = shift(after(downward_other, branch_grad), "xh", 1)
        downward_sum = (downward_grad[:256] + downward_arrived.astype(f32)).astype(bf16)
        output_grad = dot_tn(mixed, after(branch_grads, back_send))
        output_arrived = shift(output_grad[64:].astype(bf16), "xh", 1)
        output_sum = (output_grad[:64] + output_arrived.astype(f32)).astype(bf16)
        rows_sent = jnp.concatenate(
            [output_sum.reshape(8, 8, D), downward_sum.reshape(8, 32, D)], axis=1
        )
        rows_all = exchange(after(rows_sent, arrived_up), SEQ)
    with jax.named_scope("first_back"):
        mine, other, head_grads, extra = last_parts(
            table, query_grad, back_own, back_arrived, project, normal_first
        )
        last_near = joined(mine, other)
        ends = spread(*last_near)
        input_gradient = input_end(ends, block_input, vectors, mid_grad)
    with jax.named_scope("attention_gradients"):
        weight_grad = dot_tn(normed_first, head_grads).astype(bf16)
        shares = jnp.concatenate([weight_grad, extra], axis=-1).reshape(128, 8, 512)
        arrived_last = exchange(after(shares, rows_all), FSDP + SEQ)
    with jax.named_scope("totals"):
        total, small_total = totals(
            whose, rows_all, arrived_up, after(arrived_last, out_near[0], last_near[0])
        )
        (
            output_weight_gradient, downward_weight_gradient, upward_weight_gradient,
            attention_weight_gradient,
        ) = deal_out(exchange(total, SEQ))

    return (
        block_output,
        input_gradient,
        small_total[0, 0:64],
        small_total[0, 64:128],
        attention_weight_gradient,
        small_total[3, 0:64],
        small_total[3, 64:128],
        output_weight_gradient,
        small_total[2, 0:64],
        small_total[1, 0:64],
        small_total[1, 64:128],
        upward_weight_gradient,
        small_total[4],
        downward_weight_gradient,
        small_total[2, 64:128],
    )


def solution(mesh):
    grid = Mesh(mesh.devices.reshape(4, 2, 4, 2, 2), ALL)
    tokens = P(ALL, None)
    rows = P(FSDP, None)
    line = P(FSDP)
    return jax.shard_map(
        on_device,
        mesh=grid,
        in_specs=(
            tokens, line, line, rows, line, line, rows, line, line, line, rows, line, rows, line,
            tokens,
        ),
        out_specs=(
            tokens, tokens, line, line, rows, line, line, rows, line, line, line, rows, line, rows,
            line,
        ),
        check_vma=False,
    )
```

```python
import jax
import jax.numpy as jnp
import numpy as np
from jax import lax
from jax.experimental import pallas as pl
from jax.experimental.pallas import tpu as pltpu
from jax.sharding import Mesh
from jax.sharding import PartitionSpec as P

D = 1024
HEADS = 16
HEAD = 64
FF = 4096

epsilon = 1e-05
score_scale = 0.125
bf16 = jnp.bfloat16
f32 = jnp.float32

SEQ = ("z", "xl")
FSDP = ("y", "xh", "c")
ALL = SEQ + FSDP
ROWS = 128
TILE = 256
TILES = 8
LENGTH = TILE * TILES

NT = (((1,), (1,)), ((), ()))


def dot(a, b):
    return jnp.dot(a, b, preferred_element_type=f32)


def dot_nt(a, b):
    return lax.dot_general(a, b, NT, preferred_element_type=f32)


def dot_tn(a, b):
    return lax.dot_general(a, b, (((0,), (0,)), ((), ())), preferred_element_type=f32)


smem = pl.BlockSpec(memory_space=pltpu.SMEM)
vmem = pl.BlockSpec(memory_space=pltpu.VMEM)


def call(kernel, name, outs, scratch, flops, moved, transcendentals, args, scalars=0, pieces=0):
    rest = len(args) - scalars - pieces
    return pl.pallas_call(
        kernel,
        out_shape=tuple(jax.ShapeDtypeStruct(shape, kind) for shape, kind in outs),
        in_specs=[smem] * scalars + [pl.BlockSpec(memory_space=pl.ANY)] * pieces + [vmem] * rest,
        out_specs=(vmem,) * len(outs),
        scratch_shapes=[
            pltpu.VMEM(*item) if isinstance(item, tuple) else item for item in scratch
        ],
        compiler_params=pltpu.CompilerParams(vmem_limit_bytes=60 * 2**20),
        cost_estimate=pl.CostEstimate(
            flops=flops, bytes_accessed=moved, transcendentals=transcendentals
        ),
        name=name,
    )(*args)


def place(table, p):
    return pl.multiple_of(table[p] * ROWS, ROWS)


def assemble(table, refs, out, sems):
    copies = [
        pltpu.make_async_copy(refs[p], out.at[pl.ds(place(table, p), ROWS), :], sems.at[p])
        for p in range(8)
    ]
    for copy in copies:
        copy.start()
    return copies


def rows_of(table, ref, p):
    return jnp.concatenate(
        [ref[pl.ds(place(table, p + b), ROWS), :] for b in range(2)], axis=0
    )


def set_rows(table, ref, p, value):
    for b in range(2):
        ref[pl.ds(place(table, p + b), ROWS), :] = value[b * ROWS : (b + 1) * ROWS]


def put_parts(mine_ref, other_ref, chunk, value):
    ref = mine_ref if chunk < 2 else other_ref
    for b in range(2):
        ref[2 * (chunk % 2) + b] = value[b * ROWS : (b + 1) * ROWS].astype(ref.dtype)


PARTS = [((4, ROWS, D), bf16), ((4, ROWS, D), bf16)]
ORDER = (2, 3, 0, 1)


def extra_rows(out_ref, pairs, lines):
    row = lax.broadcasted_iota(jnp.int32, (64, 128), 0) % 8
    for shard in range(16):
        columns = slice(64 * shard, 64 * shard + 64)
        block = jnp.zeros((64, 128), f32)
        for r, (left, right) in enumerate(pairs):
            line = jnp.concatenate([left[:, columns], right[:, columns]], axis=1)
            block = jnp.where(row == r, line, block)
        for r, line in enumerate(lines):
            block = jnp.where(row == len(pairs) + r, line, block)
        out_ref[64 * shard : 64 * shard + 64, :] = block.astype(bf16)


def deal_kernel(weight_ref, small_ref, up_ref, out_ref, up_out):
    small = small_ref[...]

    def piece(kind, head):
        start = kind * D + head * HEAD
        return weight_ref[:, start : start + HEAD]

    for y in range(4):
        for x in range(2):
            for c in range(2):
                shard = 4 * y + 2 * x + c
                twin = shard ^ 2
                out_ref[shard, 0:64, :] = jnp.concatenate(
                    [
                        piece(kind, head) for kind in range(3) for head in (shard, twin)
                    ],
                    axis=1,
                )
                out_ref[shard, 64:80, :] = small
                up_out[shard, :, 0:256] = up_ref[:, 256 * shard : 256 * shard + 256]
                up_out[shard, :, 256:512] = up_ref[:, 256 * twin : 256 * twin + 256]


def swap(pairs):
    return jnp.concatenate(
        [pairs[:, 64:128], pairs[:, 0:64], pairs[:, 192:256], pairs[:, 128:192]], axis=1
    )


def first_kernel(table, shard_ref, *refs):
    pieces, arrived = refs[0:8], refs[8]
    kv_ref, send_ref, normed_ref, normal_ref, project_ref, vector_ref, bias_ref = refs[9:16]
    inputs, sems = refs[16:18]
    copies = assemble(table, pieces, inputs, sems)
    for r in range(16):
        project_ref[64 * r : 64 * r + 64, :] = arrived[r, 0:64, :]
    rows = [arrived[r, 64:80, :].astype(f32) for r in range(16)]
    for g in range(6):
        vector_ref[g : g + 1, :] = jnp.concatenate(
            [rows[r][0:1, 64 * g : 64 * g + 64] for r in range(16)], axis=1
        )
    shard = shard_ref[0]
    mine = arrived[shard, 64:80, :].astype(f32)[1:2]
    twin = arrived[shard ^ 2, 64:80, :].astype(f32)[1:2]
    bias_ref[0:1, :] = jnp.concatenate([mine[:, 128:], twin[:, 128:]], axis=1)
    bias_ref[1:2, 0:128] = jnp.concatenate([mine[:, 0:64], twin[:, 0:64]], axis=1)
    bias = jnp.concatenate(
        [jnp.zeros((1, 2 * HEAD), f32), mine[:, 64:128], twin[:, 64:128]], axis=1
    )
    gain = vector_ref[0:1, :]
    offset = vector_ref[1:2, :]
    for copy in copies:
        copy.wait()
    for chunk in range(4):
        rows = slice(chunk * TILE, (chunk + 1) * TILE)
        normal, unused = normalize(inputs[rows, :].astype(f32))
        normal_ref[rows, :] = normal.astype(bf16)
        normed = (normal * gain + offset).astype(bf16)
        normed_ref[rows, :] = normed
        heads = (dot(normed, project_ref[:, 128:384]) + bias).astype(bf16)
        kv_ref[rows, :] = heads
        send_ref[rows, :] = swap(heads)


def query_kernel(normed_ref, project_ref, bias_ref, query_ref):
    bias = bias_ref[1:2, 0:128]
    for chunk in range(4):
        rows = slice(chunk * TILE, (chunk + 1) * TILE)
        value = dot(normed_ref[rows, :], project_ref[:, 0:128]) + bias
        query_ref[rows, :] = value.astype(bf16)


def queries(normed, project, bias):
    return call(
        query_kernel, "queries", [((1024, 128), bf16)], [], 27 * 10**7, 3 * 10**6, 0,
        (normed, project, bias),
    )[0]


def first_heads(table, shard, pieces, arrived):
    return call(
        first_kernel, "first_heads",
        [
            ((1024, 256), bf16), ((1024, 256), bf16), ((1024, D), bf16), ((1024, D), bf16),
            ((D, 384), bf16), ((8, D), f32), ((8, 512), f32),
        ],
        [((1024, D), bf16), pltpu.SemaphoreType.DMA((8,))],
        8 * 10**8, 10**7, 10**4, (table, shard, *pieces, arrived), 2, 8,
    )


def in_head(shape, head):
    lane = lax.broadcasted_iota(jnp.int32, shape, 1)
    return (lane < HEAD) if head == 0 else (lane >= HEAD)


def stage_queries(query, head):
    lane = lax.broadcasted_iota(jnp.int32, query.shape, 1) - (HEAD if head == 0 else 0)
    ones = jnp.where((lane >= 0) & (lane < 3), 1.0, 0.0)
    scaled = query.astype(f32) * score_scale
    return jnp.where(in_head(query.shape, head), scaled, ones).astype(bf16)


def stage_keys(key, head, slope, first):
    shape = key.shape
    lane = lax.broadcasted_iota(jnp.int32, shape, 1) - (HEAD if head == 0 else 0)
    row = lax.broadcasted_iota(jnp.int32, shape, 0)
    place = slope * (row + first).astype(f32)
    high = place.astype(bf16).astype(f32)
    rest = place - high
    middle = rest.astype(bf16).astype(f32)
    low = rest - middle
    extra = jnp.where(
        lane == 0, high, jnp.where(lane == 1, middle, jnp.where(lane == 2, low, 0.0))
    )
    return jnp.where(in_head(shape, head), key.astype(f32), extra).astype(bf16)


def fold(tile, op):
    parts = [tile[8 * g : 8 * g + 8] for g in range(TILE // 8)]
    while len(parts) > 1:
        parts = [op(parts[2 * g], parts[2 * g + 1]) for g in range(len(parts) // 2)]
    return parts[0]


def future():
    key = lax.broadcasted_iota(jnp.int32, (TILE, TILE), 0)
    query = lax.broadcasted_iota(jnp.int32, (TILE, TILE), 1)
    return key > query


def tile_rows(t):
    return slice(t * TILE, (t + 1) * TILE)


def stage(half, slopes, own_ref, other_ref, ka, emit_rest):
    for t in range(4):
        for side, ref in enumerate((own_ref, other_ref)):
            slot = tile_rows(2 * t + side)
            pair = ref[tile_rows(t), :]
            first = TILE * (2 * t + (half[0] if side == 0 else 1 - half[0])) - LENGTH // 2
            for head in range(2):
                ka[head, slot, :] = stage_keys(pair[:, 0:128], head, slopes[head], first)
            emit_rest(slot, pair)


def masked(s, t, slot, hidden, ahead):
    if slot == 2 * t:
        return jnp.where(hidden, -1e30, s)
    return s + ahead if slot == 2 * t + 1 else s


def forward_kernel(half, slopes, q_ref, own_ref, other_ref, out_ref, lse_ref, ka, vt, s_sc, p_sc):
    def rest(slot, pair):
        vt[:, slot] = pair[:, 128:256].astype(f32).T.astype(bf16)

    stage(half, slopes, own_ref, other_ref, ka, rest)
    hidden = future()
    ahead = jnp.where(half[0] == 1, 0.0, -1e30)
    for t in range(4):
        query = q_ref[tile_rows(t), :]
        n = (2 * t + 2) * TILE
        outs = []
        for head in range(2):
            q = stage_queries(query, head)
            peak = None
            for slot in range(2 * t + 2):
                rows = tile_rows(slot)
                s = masked(dot_nt(ka[head, rows, :], q), t, slot, hidden, ahead)
                s_sc[head, rows, :] = s
                top = fold(s, jnp.maximum)
                peak = top if peak is None else jnp.maximum(peak, top)
            peak = jnp.max(peak, axis=0, keepdims=True)
            total = None
            for slot in range(2 * t + 2):
                rows = tile_rows(slot)
                p = jnp.exp(s_sc[head, rows, :] - peak)
                p_sc[head, rows, :] = p.astype(bf16)
                part = fold(p, jnp.add)
                total = part if total is None else total + part
            total = jnp.sum(total, axis=0, keepdims=True)
            outs.append(dot(vt[head * HEAD : (head + 1) * HEAD, 0:n], p_sc[head, 0:n, :]) / total)
            lse_ref[2 * t + head] = peak + jnp.log(total)
        out_ref[tile_rows(t), :] = jnp.concatenate(outs, axis=0).T.astype(bf16)


def attention_forward(half, slopes, query, own, other):
    return call(
        forward_kernel, "attention_forward",
        [((1024, 128), bf16), ((8, 1, TILE), f32)],
        [
            ((2, LENGTH, 128), bf16), ((128, LENGTH), bf16), ((2, LENGTH, TILE), f32),
            ((2, LENGTH, TILE), bf16),
        ],
        3 * 10**9, 2 * 10**6, 24 * 10**5, (half, slopes, query, own, other), 2,
    )


def backward_kernel(
    half, slopes, q_ref, own_ref, other_ref, grad_ref, lse_ref,
    dq_ref, down_ref, send_ref,
    ka, kt, va, dk, dv, p_sc, dp_sc, ds_sc,
):
    def rest(slot, pair):
        va[slot, :] = pair[:, 128:256]
        kt[:, slot] = pair[:, 0:128].astype(f32).T.astype(bf16)

    stage(half, slopes, own_ref, other_ref, ka, rest)
    hidden = future()
    ahead = jnp.where(half[0] == 1, 0.0, -1e30)
    for t in range(4):
        query = q_ref[tile_rows(t), :]
        grad = grad_ref[tile_rows(t), :]
        n = (2 * t + 2) * TILE
        grads = [
            jnp.where(in_head(grad.shape, head), grad.astype(f32), 0.0).astype(bf16)
            for head in range(2)
        ]
        plain = [
            jnp.where(in_head(query.shape, head), query.astype(f32) * score_scale, 0.0).astype(bf16)
            for head in range(2)
        ]
        queries = [stage_queries(query, head) for head in range(2)]
        grad_rows = jnp.concatenate(grads, axis=0)
        plain_rows = jnp.concatenate(plain, axis=0)
        delta = [None, None]
        for slot in range(2 * t + 2):
            rows = tile_rows(slot)
            low = []
            for head in range(2):
                s = masked(dot_nt(ka[head, rows, :], queries[head]), t, slot, hidden, ahead)
                p = jnp.exp(s - lse_ref[2 * t + head])
                dp = dot_nt(va[rows, :], grads[head])
                p_sc[head, rows, :] = p
                dp_sc[head, rows, :] = dp
                part = fold(p * dp, jnp.add)
                delta[head] = part if delta[head] is None else delta[head] + part
                low.append(p.astype(bf16))
            value = dot(jnp.concatenate(low, axis=1), grad_rows)
            dv[rows, :] = value if slot >= 2 * t else dv[rows, :] + value
        delta = [jnp.sum(item, axis=0, keepdims=True) for item in delta]
        for slot in range(2 * t + 2):
            rows = tile_rows(slot)
            low = []
            for head in range(2):
                ds = (p_sc[head, rows, :] * (dp_sc[head, rows, :] - delta[head])).astype(bf16)
                ds_sc[head, rows, :] = ds
                low.append(ds)
            key = dot(jnp.concatenate(low, axis=1), plain_rows)
            dk[rows, :] = key if slot >= 2 * t else dk[rows, :] + key
        outs = [
            dot(kt[head * HEAD : (head + 1) * HEAD, 0:n], ds_sc[head, 0:n, :]) for head in range(2)
        ]
        dq_ref[tile_rows(t), :] = (jnp.concatenate(outs, axis=0) * score_scale).T.astype(bf16)
    for t in range(4):
        rows = tile_rows(t)
        down_ref[rows, 0:128] = dk[tile_rows(2 * t), :]
        down_ref[rows, 128:256] = dv[tile_rows(2 * t), :]
        pair = jnp.concatenate([dk[tile_rows(2 * t + 1), :], dv[tile_rows(2 * t + 1), :]], axis=1)
        send_ref[rows, :] = swap(pair.astype(bf16))


def attention_backward(half, slopes, query, own, other, grad, lse):
    return call(
        backward_kernel, "attention_backward",
        [((1024, 128), bf16), ((1024, 256), f32), ((1024, 256), bf16)],
        [
            ((2, LENGTH, 128), bf16), ((128, LENGTH), bf16), ((LENGTH, 128), bf16),
            ((LENGTH, 128), f32), ((LENGTH, 128), f32), ((2, LENGTH, TILE), f32),
            ((2, LENGTH, TILE), f32), ((2, LENGTH, TILE), bf16),
        ],
        6 * 10**9, 3 * 10**6, 24 * 10**5, (half, slopes, query, own, other, grad, lse), 2,
    )


def output_kernel(table, mixed_ref, weight_ref, rows_ref, mine_part, other_part):
    weight = jnp.concatenate([weight_ref[...], rows_ref[...]], axis=0)
    for chunk in ORDER:
        put_parts(mine_part, other_part, chunk, dot(rows_of(table, mixed_ref, 2 * chunk), weight))


def output_parts(table, mixed, weight, rows):
    return call(
        output_kernel, "output_parts", PARTS, [], 27 * 10**7, 4 * 10**6, 0,
        (table, mixed, weight, rows), 1,
    )


def feed_kernel(table, *refs):
    up_ref, down_ref, rows_ref, bias_ref = refs[16:20]
    mine_part, other_part, act_ref, grad_ref, second_ref, cotangent_ref, extra_ref = refs[20:27]
    sems, more = refs[27:29]
    copies = assemble(table, refs[0:8], second_ref, sems)
    cotangent_copies = assemble(table, refs[8:16], cotangent_ref, more)
    bias = bias_ref[0:1, :]
    for chunk in ORDER:
        cotangent_copies[2 * chunk].wait()
        cotangent_copies[2 * chunk + 1].wait()
        cotangents = rows_of(table, cotangent_ref, 2 * chunk)
        back = jnp.concatenate(
            [dot_nt(cotangents, down_ref[...]), dot_nt(cotangents, rows_ref[...])], axis=1
        )
        copies[2 * chunk].wait()
        copies[2 * chunk + 1].wait()
        up = dot(rows_of(table, second_ref, 2 * chunk), up_ref[...]) + bias
        square = up * up
        bend = jnp.tanh(0.7978845608028654 * (up + 0.044715 * square * up))
        half = 0.5 * (1.0 + bend)
        set_rows(table, act_ref, 2 * chunk, (up * half).astype(bf16))
        slope = half + 0.5 * up * (1.0 - bend * bend) * (
            0.7978845608028654 * (1.0 + 0.134145 * square)
        )
        grad = (back * slope).astype(bf16)
        set_rows(table, grad_ref, 2 * chunk, grad)
        part = jnp.sum(grad.astype(f32), axis=0, keepdims=True)
        total = part if chunk == ORDER[0] else total + part
        put_parts(mine_part, other_part, chunk, dot_nt(grad, up_ref[...]))
    extra_rows(extra_ref, [], [total[:, 128 * g : 128 * g + 128] for g in range(4)])


def feed_parts(table, pieces, cotangents, up, down, rows, bias):
    return call(
        feed_kernel, "feed_parts", PARTS + [((1024, 512), bf16)] * 2 + [((1024, D), bf16)] * 2 + [((1024, 128), bf16)],
        [pltpu.SemaphoreType.DMA((8,)), pltpu.SemaphoreType.DMA((8,))],
        32 * 10**8, 2 * 10**7, 5 * 10**5, (table, *pieces, *cotangents, up, down, rows, bias), 1,
        16,
    )


def out_kernel(table, act_ref, down_ref, rows_ref, mine_part, other_part):
    for chunk in ORDER:
        act = rows_of(table, act_ref, 2 * chunk)
        value = dot(act[:, 0:256], down_ref[...]) + dot(act[:, 256:512], rows_ref[...])
        put_parts(mine_part, other_part, chunk, value)


def out_parts(table, act, down, rows):
    return call(
        out_kernel, "out_parts", PARTS, [], 11 * 10**8, 5 * 10**6, 0, (table, act, down, rows), 1
    )


def mixed_kernel(table, *refs):
    pieces, weight_ref, rows_ref = refs[0:8], refs[8], refs[9]
    grad_ref, all_ref, sems = refs[10:13]
    copies = assemble(table, pieces, all_ref, sems)
    weight = jnp.concatenate([weight_ref[...], rows_ref[...]], axis=0)
    for chunk in range(4):
        copies[2 * chunk].wait()
        copies[2 * chunk + 1].wait()
        grads = dot_nt(rows_of(table, all_ref, 2 * chunk), weight).astype(bf16)
        set_rows(table, grad_ref, 2 * chunk, grads)


def mixed_back(table, pieces, weight, rows):
    return call(
        mixed_kernel, "mixed_back",
        [((1024, 128), bf16), ((1024, D), bf16)],
        [pltpu.SemaphoreType.DMA((8,))],
        27 * 10**7, 4 * 10**6, 0, (table, *pieces, weight, rows), 1, 8,
    )


def last_kernel(
    table, query_ref, own_ref, other_ref, project_ref, normal_ref, middle_ref,
    mine_part, other_part, joined_ref, extra_ref,
):
    gain = None
    for chunk in ORDER:
        own = rows_of(table, own_ref, 2 * chunk)
        other = rows_of(table, other_ref, 2 * chunk).astype(f32)
        joined = jnp.concatenate(
            [rows_of(table, query_ref, 2 * chunk), (own + other).astype(bf16)], axis=1
        )
        set_rows(table, joined_ref, 2 * chunk, joined)
        bias = jnp.sum(joined.astype(f32), axis=0, keepdims=True)
        biases = bias if chunk == ORDER[0] else biases + bias
        value = dot_nt(joined, project_ref[...])
        put_parts(mine_part, other_part, chunk, value)
        normal = rows_of(table, normal_ref, 2 * chunk).astype(f32)
        tilted = jnp.sum(value * normal, axis=0, keepdims=True)
        plain = jnp.sum(value, axis=0, keepdims=True)
        gain = tilted if gain is None else gain + tilted
        offset = plain if chunk == ORDER[0] else offset + plain
    pairs = [
        (gain, offset), (middle_ref[0:1, :], middle_ref[1:2, :]),
        (middle_ref[2:3, :], middle_ref[3:4, :]),
    ]
    extra_rows(extra_ref, pairs, [biases[:, 0:128], biases[:, 256:384]])


def last_parts(table, query, own, other, project, normal, sums):
    return call(
        last_kernel, "last_parts", PARTS + [((1024, 384), bf16), ((1024, 128), bf16)], [],
        8 * 10**8, 7 * 10**6, 0, (table, query, own, other, project, normal, sums), 1,
    )


def join_kernel(mine_ref, core_ref, here_ref, near_ref, far_ref, back_ref):
    for d, ref in enumerate((here_ref, near_ref, far_ref, back_ref)):
        ref[...] = (mine_ref[d] + core_ref[d].astype(f32)).astype(ref.dtype)


def join(mine, core):
    return call(
        join_kernel, "join", [((ROWS, D), f32)] + [((ROWS, D), bf16)] * 3, [], 10**6, 4 * 10**6, 0,
        (mine, core),
    )


def landed(refs):
    here, near, far, back = [ref[...].astype(f32) for ref in refs]
    return here + near + far + back


def middle_kernel(*refs):
    input_ref, vector_ref, mid_ref, normal_ref, inverse_ref, normed_ref = refs[4:10]
    mid = input_ref[...].astype(f32) + (landed(refs[0:4]) + vector_ref[2:3, :])
    normal, inverse = normalize(mid)
    mid_ref[...] = mid
    normal_ref[...] = normal
    inverse_ref[...] = inverse
    normed_ref[...] = (normal * vector_ref[3:4, :] + vector_ref[4:5, :]).astype(bf16)


def middle(ends, inputs, vectors):
    return call(
        middle_kernel, "middle",
        [((ROWS, D), f32), ((ROWS, D), f32), ((ROWS, 1), f32), ((ROWS, D), bf16)], [],
        10**6, 3 * 10**6, 0, (*ends, inputs, vectors),
    )


def middle_back_kernel(*refs):
    cotangent_ref, vector_ref, normal_ref, inverse_ref, grad_ref, branch_ref, sum_ref = refs[4:11]
    second = landed(refs[0:4])
    normal = normal_ref[...]
    cotangent = cotangent_ref[...].astype(f32)
    grad = cotangent + norm_back(second, vector_ref[3:4, :], normal, inverse_ref[...])
    grad_ref[...] = grad
    branch = grad.astype(bf16)
    branch_ref[...] = branch
    sum_ref[0:1, :] = jnp.sum(second * normal, axis=0, keepdims=True)
    sum_ref[1:2, :] = jnp.sum(second, axis=0, keepdims=True)
    sum_ref[2:3, :] = jnp.sum(branch.astype(f32), axis=0, keepdims=True)
    sum_ref[3:4, :] = jnp.sum(cotangent, axis=0, keepdims=True)


def middle_back(ends, cotangent, vectors, normal, inverse):
    return call(
        middle_back_kernel, "middle_back",
        [((ROWS, D), f32), ((ROWS, D), bf16), ((8, D), f32)], [],
        10**6, 3 * 10**6, 0, (*ends, cotangent, vectors, normal, inverse),
    )


def block_kernel(*refs):
    mid_ref, vector_ref, out_ref = refs[4:7]
    out_ref[...] = (mid_ref[...] + landed(refs[0:4]) + vector_ref[5:6, :]).astype(bf16)


def block_end(ends, mid, vectors):
    return call(
        block_kernel, "block_end", [((ROWS, D), bf16)], [], 10**6, 2 * 10**6, 0,
        (*ends, mid, vectors),
    )[0]


def input_kernel(*refs):
    input_ref, vector_ref, grad_ref, out_ref = refs[4:8]
    normal, inverse = normalize(input_ref[...].astype(f32))
    out_ref[...] = grad_ref[...] + norm_back(
        landed(refs[0:4]), vector_ref[0:1, :], normal, inverse
    )


def input_end(ends, inputs, vectors, grad):
    return call(
        input_kernel, "input_end", [((ROWS, D), f32)], [], 10**6, 3 * 10**6, 0,
        (*ends, inputs, vectors, grad),
    )[0]


def totals_kernel(whose, rows_ref, up_ref, last_ref, total_ref, small_ref, up_small, last_small):
    def over_seq(ref, shard, columns):
        value = ref[8 * shard, :, columns].astype(f32)
        for q in range(1, 8):
            value = value + ref[8 * shard + q, :, columns].astype(f32)
        return value

    rows = rows_ref[0].astype(f32)
    for q in range(1, 8):
        rows = rows + rows_ref[q].astype(f32)
    ups, lasts = [], []
    for shard in range(16):
        up_small[shard] = over_seq(up_ref, shard, slice(512, 640))
        last_small[shard] = over_seq(last_ref, shard, slice(384, 512))
        lasts.append(over_seq(last_ref, shard, slice(0, 384)))
        ups.append(over_seq(up_ref, shard, slice(0, 512)))
    pieces = [rows]
    for block in range(4):
        pieces.append(
            jnp.concatenate(
                [
                    ups[shard][:, 0:256] + ups[shard ^ 2][:, 256:512]
                    for shard in range(4 * block, 4 * block + 4)
                ],
                axis=1,
            )
        )
    for kind in range(3):
        start = 128 * kind
        pieces.append(
            jnp.concatenate(
                [
                    lasts[shard][:, start : start + 64]
                    + lasts[shard ^ 2][:, start + 64 : start + 128]
                    for shard in range(16)
                ],
                axis=1,
            )
        )
    total = jnp.concatenate(pieces, axis=0).astype(bf16)
    for q in range(8):
        total_ref[q] = total
    last_sum = last_small[0]
    for shard in range(1, 16):
        last_sum = last_sum + last_small[shard]
    mine, twin = last_small[whose[0]], last_small[whose[0] ^ 2]
    up_mine, up_twin = up_small[whose[0]], up_small[whose[0] ^ 2]
    small_ref[0:3, 0:128] = last_sum[0:3]
    small_ref[3:4, 0:128] = jnp.concatenate(
        [mine[3:4, 0:64] + twin[3:4, 64:128], mine[4:5, 0:64] + twin[4:5, 64:128]], axis=1
    )
    small_ref[4:5, :] = jnp.concatenate(
        [up_mine[0:1] + up_twin[2:3], up_mine[1:2] + up_twin[3:4]], axis=1
    )


def totals(whose, rows, up, last):
    return call(
        totals_kernel, "totals", [((8, 96, D), bf16), ((8, 256), f32)],
        [((16, 8, 128), f32), ((16, 8, 128), f32)],
        2 * 10**6, 6 * 10**6, 0, (whose, rows, up, last), 1,
    )


def deal_out_kernel(total_ref, output_ref, down_ref, up_ref, attention_ref):
    for q in range(8):
        total = total_ref[q].astype(f32)
        output_ref[8 * q : 8 * q + 8, :] = total[0:8]
        down_ref[32 * q : 32 * q + 32, :] = total[8:40]
        for block in range(4):
            up_ref[8 * q : 8 * q + 8, D * block : D * block + D] = total[
                40 + 8 * block : 48 + 8 * block
            ]
        for kind in range(3):
            attention_ref[8 * q : 8 * q + 8, D * kind : D * kind + D] = total[
                72 + 8 * kind : 80 + 8 * kind
            ]


def deal_out(total):
    return call(
        deal_out_kernel, "deal_out",
        [((64, D), f32), ((256, D), f32), ((64, FF), f32), ((64, 3 * D), f32)], [],
        10**6, 5 * 10**6, 0, (total,),
    )


def shift(value, axis, step):
    size = lax.axis_size(axis)
    return lax.ppermute(value, axis, [(i, (i + step) % size) for i in range(size)])


def gather(own, *first):
    mine = [shift(own, "y", -step) for step in (1, 2, 3)]
    if first:
        mine = list(lax.optimization_barrier((*mine, *first))[0:3])
    mine = [own, *mine]
    return mine + [shift(block, "c", 1) for block in mine]


def joined(mine, other, *first):
    core = shift(other, "c", 1)
    return join(mine, after(core, *first) if first else core)


def spread(here, near, far, back):
    return here, shift(near, "y", 1), shift(far, "y", 2), shift(back, "y", 3)


def scatter(mine, other, *first):
    return spread(*joined(mine, other, *first))


def exchange(value, axes):
    return lax.all_to_all(value, axes, split_axis=0, concat_axis=0, tiled=True)


def after(value, *others):
    return lax.optimization_barrier((value, *others))[0]


def normalize(values):
    centre = jnp.mean(values, axis=-1, keepdims=True)
    centred = values - centre
    spread = jnp.mean(centred * centred, axis=-1, keepdims=True)
    inverse = lax.rsqrt(spread + epsilon)
    return centred * inverse, inverse


def norm_back(grad, gain, normal, inverse):
    scaled = grad * gain
    return inverse * (
        scaled
        - jnp.mean(scaled, axis=-1, keepdims=True)
        - normal * jnp.mean(scaled * normal, axis=-1, keepdims=True)
    )


def on_device(
    block_input,
    first_gain,
    first_shift,
    attention_weight,
    query_bias,
    value_bias,
    output_weight,
    output_bias,
    second_gain,
    second_shift,
    upward_weight,
    upward_bias,
    downward_weight,
    downward_bias,
    cotangent,
):
    y = lax.axis_index("y")
    xh = lax.axis_index("xh")
    c = lax.axis_index("c")
    shard = 4 * y + 2 * xh + c
    piece = np.arange(8)
    table = (2 * ((y + piece % 4) % 4) + (c ^ (piece // 4))).astype(jnp.int32)
    half = xh[None].astype(jnp.int32)
    whose = shard[None].astype(jnp.int32)
    slopes = jnp.exp2(-8.0 * (jnp.stack([shard, shard ^ 2]) + 1).astype(f32) / HEADS)

    with jax.named_scope("weights_attention"):
        vectors_own = [
            first_gain, first_shift, output_bias, second_gain, second_shift, downward_bias
        ]
        small = sum(
            jnp.pad(item[None], ((0, 15), (64 * g, 320 - 64 * g)))
            for g, item in enumerate(vectors_own)
        )
        small = small + jnp.pad(query_bias[None], ((1, 14), (0, 320)))
        small = small + jnp.pad(value_bias[None], ((1, 14), (64, 256)))
        small = small + jnp.pad(upward_bias[None], ((1, 14), (128, 0)))
        payload, up_payload = call(
            deal_kernel, "deal", [((16, 80, 384), bf16), ((16, 64, 512), bf16)], [],
            0, 4 * 10**6, 0, (attention_weight, small, upward_weight),
        )
        arrived = exchange(payload, FSDP)

    with jax.named_scope("first"):
        inputs = gather(block_input)
        heads_own, heads_send, normed_first, normal_first, project, vectors, bias_up = (
            first_heads(table, whose, inputs, arrived)
        )
        query = queries(normed_first, project, bias_up)
        heads_arrived = shift(heads_send, "xh", 1)
        cotangents = gather(after(cotangent, heads_send))
    with jax.named_scope("weights_upward"):
        upward_pair = exchange(after(up_payload, arrived), FSDP).reshape(D, 512)
    with jax.named_scope("weights_pair"):
        output_rows = shift(after(output_weight, arrived), "xh", 1)
        downward_rows = shift(after(downward_weight, heads_arrived), "xh", 1)
    with jax.named_scope("attention"):
        mixed, lse = attention_forward(half, slopes, query, heads_own, heads_arrived)
    with jax.named_scope("output"):
        mixed = after(mixed, upward_pair, *cotangents)
        mine, other = output_parts(table, mixed, output_weight, output_rows)
        residual_mid, normal_second, inverse_second, normed_second = middle(
            scatter(mine, other), block_input, vectors
        )

    with jax.named_scope("feed"):
        mine, other, activated, upward_grad, seconds, all_cotangents, extra = feed_parts(
            table, gather(normed_second), cotangents, upward_pair, downward_weight,
            downward_rows, bias_up,
        )
        sums_near = joined(mine, other)
        ends = spread(*sums_near)

    with jax.named_scope("upward_gradients"):
        late_grad, late_act = lax.optimization_barrier((upward_grad, activated, sums_near[0]))[0:2]
        upward_weight_grad = dot_tn(seconds, late_grad).astype(bf16)
        downward_grad = dot_tn(late_act, all_cotangents)
        downward_other = downward_grad[256:].astype(bf16)
        out_mine, out_other = out_parts(table, late_act, downward_weight, downward_rows)
    with jax.named_scope("feed"):
        ends = lax.optimization_barrier(
            (*ends, upward_weight_grad, downward_other, out_mine)
        )[0:4]
        mid_grad, branch_grad, sums = middle_back(
            ends, cotangent, vectors, normal_second, inverse_second
        )

    with jax.named_scope("upward_gradients"):
        shares = jnp.concatenate([upward_weight_grad, extra], axis=-1).reshape(128, 8, 640)
    with jax.named_scope("mixed_back"):
        mixed_grad, branch_grads = mixed_back(
            table, gather(branch_grad, shares), output_weight, output_rows
        )
        output_grad = dot_tn(mixed, branch_grads)
        output_other = output_grad[64:].astype(bf16)
        mixed_grad = after(mixed_grad, output_other)
    with jax.named_scope("upward_sums"):
        arrived_up = exchange(shares, FSDP + SEQ)
    with jax.named_scope("attention_back"):
        output_arrived = shift(output_other, "xh", 1)
        query_grad, back_own, back_send = attention_backward(
            half, slopes, query, heads_own, heads_arrived, mixed_grad, lse
        )
        back_send = after(back_send, arrived_up, output_arrived)
        back_arrived = shift(back_send, "xh", 1)
    with jax.named_scope("feed_out"):
        out_near = joined(out_mine, after(out_other, back_send))
        out_ends = spread(*out_near)
        block_output = block_end(out_ends, residual_mid, vectors)
    with jax.named_scope("row_gradients"):
        downward_arrived = shift(after(downward_other, branch_grad), "xh", 1)
        downward_sum = (downward_grad[:256] + downward_arrived.astype(f32)).astype(bf16)
        output_sum = (output_grad[:64] + output_arrived.astype(f32)).astype(bf16)
        rows_sent = jnp.concatenate(
            [output_sum.reshape(8, 8, D), downward_sum.reshape(8, 32, D)], axis=1
        )
        rows_all = exchange(after(rows_sent, arrived_up), SEQ)
    with jax.named_scope("first_back"):
        back_arrived = after(back_arrived, out_near[0])
        mine, other, head_grads, last_extra = last_parts(
            table, query_grad, back_own, back_arrived, project, normal_first, sums
        )
        last_near = joined(mine, other)
        ends = spread(*last_near)
        input_gradient = input_end(ends, block_input, vectors, mid_grad)
    with jax.named_scope("attention_gradients"):
        weight_grad = dot_tn(normed_first, head_grads).astype(bf16)
        shares = jnp.concatenate([weight_grad, last_extra], axis=-1).reshape(128, 8, 512)
        arrived_last = exchange(after(shares, rows_all), FSDP + SEQ)
    with jax.named_scope("totals"):
        total, small_total = totals(
            whose, rows_all, arrived_up, after(arrived_last, block_output, last_near[0])
        )
        (
            output_weight_gradient, downward_weight_gradient, upward_weight_gradient,
            attention_weight_gradient,
        ) = deal_out(exchange(total, SEQ))

    return (
        block_output,
        input_gradient,
        small_total[0, 0:64],
        small_total[0, 64:128],
        attention_weight_gradient,
        small_total[3, 0:64],
        small_total[3, 64:128],
        output_weight_gradient,
        small_total[2, 0:64],
        small_total[1, 0:64],
        small_total[1, 64:128],
        upward_weight_gradient,
        small_total[4],
        downward_weight_gradient,
        small_total[2, 64:128],
    )


def solution(mesh):
    grid = Mesh(mesh.devices.reshape(4, 2, 4, 2, 2), ALL)
    tokens = P(ALL, None)
    rows = P(FSDP, None)
    line = P(FSDP)
    return jax.shard_map(
        on_device,
        mesh=grid,
        in_specs=(
            tokens, line, line, rows, line, line, rows, line, line, line, rows, line, rows, line,
            tokens,
        ),
        out_specs=(
            tokens, tokens, line, line, rows, line, line, rows, line, line, line, rows, line, rows,
            line,
        ),
        check_vma=False,
    )
```

```python
import jax
import jax.numpy as jnp
import numpy as np
from jax import lax
from jax.experimental import pallas as pl
from jax.experimental.pallas import tpu as pltpu
from jax.sharding import Mesh
from jax.sharding import PartitionSpec as P

D = 1024
HEADS = 16
HEAD = 64
FF = 4096

epsilon = 1e-05
score_scale = 0.125
bf16 = jnp.bfloat16
f32 = jnp.float32

SEQ = ("z", "xl")
FSDP = ("y", "xh", "c")
ALL = SEQ + FSDP
ROWS = 128
TILE = 256
TILES = 8
LENGTH = TILE * TILES

NT = (((1,), (1,)), ((), ()))


def dot(a, b):
    return jnp.dot(a, b, preferred_element_type=f32)


def dot_nt(a, b):
    return lax.dot_general(a, b, NT, preferred_element_type=f32)


def dot_tn(a, b):
    return lax.dot_general(a, b, (((0,), (0,)), ((), ())), preferred_element_type=f32)


smem = pl.BlockSpec(memory_space=pltpu.SMEM)
vmem = pl.BlockSpec(memory_space=pltpu.VMEM)


def call(kernel, name, outs, scratch, flops, moved, transcendentals, args, scalars=0, pieces=0):
    rest = len(args) - scalars - pieces
    return pl.pallas_call(
        kernel,
        out_shape=tuple(jax.ShapeDtypeStruct(shape, kind) for shape, kind in outs),
        in_specs=[smem] * scalars + [pl.BlockSpec(memory_space=pl.ANY)] * pieces + [vmem] * rest,
        out_specs=(vmem,) * len(outs),
        scratch_shapes=[
            pltpu.VMEM(*item) if isinstance(item, tuple) else item for item in scratch
        ],
        compiler_params=pltpu.CompilerParams(vmem_limit_bytes=60 * 2**20),
        cost_estimate=pl.CostEstimate(
            flops=flops, bytes_accessed=moved, transcendentals=transcendentals
        ),
        name=name,
    )(*args)


def first_row(table, p):
    return pl.multiple_of(table[p] * ROWS, ROWS)


def assemble(table, refs, out, sems):
    copies = [
        pltpu.make_async_copy(refs[p], out.at[pl.ds(first_row(table, p), ROWS), :], sems.at[p])
        for p in range(8)
    ]
    for copy in copies:
        copy.start()
    return copies


def rows_of(table, ref, p):
    return jnp.concatenate(
        [ref[pl.ds(first_row(table, p + b), ROWS), :] for b in range(2)], axis=0
    )


def set_rows(table, ref, p, value):
    for b in range(2):
        ref[pl.ds(first_row(table, p + b), ROWS), :] = value[b * ROWS : (b + 1) * ROWS]


def put_parts(mine_ref, other_ref, chunk, value):
    ref = mine_ref if chunk < 2 else other_ref
    for b in range(2):
        ref[2 * (chunk % 2) + b] = value[b * ROWS : (b + 1) * ROWS].astype(ref.dtype)


PARTS = [((4, ROWS, D), bf16), ((4, ROWS, D), bf16)]
ORDER = (2, 3, 0, 1)


def extra_rows(out_ref, pairs, lines):
    row = lax.broadcasted_iota(jnp.int32, (64, 128), 0) % 8
    for shard in range(16):
        columns = slice(64 * shard, 64 * shard + 64)
        block = jnp.zeros((64, 128), f32)
        for r, (left, right) in enumerate(pairs):
            line = jnp.concatenate([left[:, columns], right[:, columns]], axis=1)
            block = jnp.where(row == r, line, block)
        for r, line in enumerate(lines):
            block = jnp.where(row == len(pairs) + r, line, block)
        out_ref[64 * shard : 64 * shard + 64, :] = block.astype(bf16)


def deal_kernel(weight_ref, small_ref, up_ref, out_ref, up_out):
    small = small_ref[...]

    def piece(kind, head):
        start = kind * D + head * HEAD
        return weight_ref[:, start : start + HEAD]

    for y in range(4):
        for x in range(2):
            for c in range(2):
                shard = 4 * y + 2 * x + c
                twin = shard ^ 2
                out_ref[shard, 0:64, :] = jnp.concatenate(
                    [
                        piece(kind, head) for kind in range(3) for head in (shard, twin)
                    ],
                    axis=1,
                )
                out_ref[shard, 64:80, :] = small
                up_out[shard, :, 0:256] = up_ref[:, 256 * shard : 256 * shard + 256]
                up_out[shard, :, 256:512] = up_ref[:, 256 * twin : 256 * twin + 256]


def swap(pairs):
    return jnp.concatenate(
        [pairs[:, 64:128], pairs[:, 0:64], pairs[:, 192:256], pairs[:, 128:192]], axis=1
    )


def first_kernel(table, shard_ref, *refs):
    pieces, arrived = refs[0:8], refs[8]
    kv_ref, send_ref, normed_ref, normal_ref, project_ref, vector_ref, bias_ref = refs[9:16]
    inputs, sems = refs[16:18]
    copies = assemble(table, pieces, inputs, sems)
    for r in range(16):
        project_ref[64 * r : 64 * r + 64, :] = arrived[r, 0:64, :]
    rows = [arrived[r, 64:80, :].astype(f32) for r in range(16)]
    for g in range(6):
        vector_ref[g : g + 1, :] = jnp.concatenate(
            [rows[r][0:1, 64 * g : 64 * g + 64] for r in range(16)], axis=1
        )
    shard = shard_ref[0]
    mine = arrived[shard, 64:80, :].astype(f32)[1:2]
    twin = arrived[shard ^ 2, 64:80, :].astype(f32)[1:2]
    bias_ref[0:1, :] = jnp.concatenate([mine[:, 128:], twin[:, 128:]], axis=1)
    bias_ref[1:2, 0:128] = jnp.concatenate([mine[:, 0:64], twin[:, 0:64]], axis=1)
    bias = jnp.concatenate(
        [jnp.zeros((1, 2 * HEAD), f32), mine[:, 64:128], twin[:, 64:128]], axis=1
    )
    gain = vector_ref[0:1, :]
    offset = vector_ref[1:2, :]
    for copy in copies:
        copy.wait()
    for chunk in range(4):
        rows = slice(chunk * TILE, (chunk + 1) * TILE)
        normal, unused = normalize(inputs[rows, :].astype(f32))
        normal_ref[rows, :] = normal.astype(bf16)
        normed = (normal * gain + offset).astype(bf16)
        normed_ref[rows, :] = normed
        heads = (dot(normed, project_ref[:, 128:384]) + bias).astype(bf16)
        kv_ref[rows, :] = heads
        send_ref[rows, :] = swap(heads)


def query_kernel(normed_ref, project_ref, bias_ref, query_ref):
    bias = bias_ref[1:2, 0:128]
    for chunk in range(4):
        rows = slice(chunk * TILE, (chunk + 1) * TILE)
        value = dot(normed_ref[rows, :], project_ref[:, 0:128]) + bias
        query_ref[rows, :] = value.astype(bf16)


def queries(normed, project, bias):
    return call(
        query_kernel, "queries", [((1024, 128), bf16)], [], 27 * 10**7, 3 * 10**6, 0,
        (normed, project, bias),
    )[0]


def first_heads(table, shard, pieces, arrived):
    return call(
        first_kernel, "first_heads",
        [
            ((1024, 256), bf16), ((1024, 256), bf16), ((1024, D), bf16), ((1024, D), bf16),
            ((D, 384), bf16), ((8, D), f32), ((8, 512), f32),
        ],
        [((1024, D), bf16), pltpu.SemaphoreType.DMA((8,))],
        8 * 10**8, 10**7, 10**4, (table, shard, *pieces, arrived), 2, 8,
    )


def in_head(shape, head):
    lane = lax.broadcasted_iota(jnp.int32, shape, 1)
    return (lane < HEAD) if head == 0 else (lane >= HEAD)


def stage_queries(query, head):
    lane = lax.broadcasted_iota(jnp.int32, query.shape, 1) - (HEAD if head == 0 else 0)
    ones = jnp.where((lane >= 0) & (lane < 3), 1.0, 0.0)
    scaled = query.astype(f32) * score_scale
    return jnp.where(in_head(query.shape, head), scaled, ones).astype(bf16)


def stage_keys(key, head, slope, first):
    shape = key.shape
    lane = lax.broadcasted_iota(jnp.int32, shape, 1) - (HEAD if head == 0 else 0)
    row = lax.broadcasted_iota(jnp.int32, shape, 0)
    place = slope * (row + first).astype(f32)
    high = place.astype(bf16).astype(f32)
    rest = place - high
    middle = rest.astype(bf16).astype(f32)
    low = rest - middle
    extra = jnp.where(
        lane == 0, high, jnp.where(lane == 1, middle, jnp.where(lane == 2, low, 0.0))
    )
    return jnp.where(in_head(shape, head), key.astype(f32), extra).astype(bf16)


def fold(tile, op):
    parts = [tile[8 * g : 8 * g + 8] for g in range(TILE // 8)]
    while len(parts) > 1:
        parts = [op(parts[2 * g], parts[2 * g + 1]) for g in range(len(parts) // 2)]
    return parts[0]


def future():
    key = lax.broadcasted_iota(jnp.int32, (TILE, TILE), 0)
    query = lax.broadcasted_iota(jnp.int32, (TILE, TILE), 1)
    return key > query


def tile_rows(t):
    return slice(t * TILE, (t + 1) * TILE)


def stage(half, slopes, own_ref, other_ref, ka, emit_rest):
    for t in range(4):
        for side, ref in enumerate((own_ref, other_ref)):
            slot = tile_rows(2 * t + side)
            pair = ref[tile_rows(t), :]
            first = TILE * (2 * t + (half[0] if side == 0 else 1 - half[0])) - LENGTH // 2
            for head in range(2):
                ka[head, slot, :] = stage_keys(pair[:, 0:128], head, slopes[head], first)
            emit_rest(slot, pair)


def masked(s, t, slot, hidden, ahead):
    if slot == 2 * t:
        return jnp.where(hidden, -1e30, s)
    return s + ahead if slot == 2 * t + 1 else s


def forward_kernel(half, slopes, q_ref, own_ref, other_ref, out_ref, lse_ref, ka, vt, s_sc, p_sc):
    def rest(slot, pair):
        vt[:, slot] = pair[:, 128:256].astype(f32).T.astype(bf16)

    stage(half, slopes, own_ref, other_ref, ka, rest)
    hidden = future()
    ahead = jnp.where(half[0] == 1, 0.0, -1e30)
    for t in range(4):
        query = q_ref[tile_rows(t), :]
        n = (2 * t + 2) * TILE
        outs = []
        for head in range(2):
            q = stage_queries(query, head)
            peak = None
            for slot in range(2 * t + 2):
                rows = tile_rows(slot)
                s = masked(dot_nt(ka[head, rows, :], q), t, slot, hidden, ahead)
                s_sc[head, rows, :] = s
                top = fold(s, jnp.maximum)
                peak = top if peak is None else jnp.maximum(peak, top)
            peak = jnp.max(peak, axis=0, keepdims=True)
            total = None
            for slot in range(2 * t + 2):
                rows = tile_rows(slot)
                p = jnp.exp(s_sc[head, rows, :] - peak)
                p_sc[head, rows, :] = p.astype(bf16)
                part = fold(p, jnp.add)
                total = part if total is None else total + part
            total = jnp.sum(total, axis=0, keepdims=True)
            outs.append(dot(vt[head * HEAD : (head + 1) * HEAD, 0:n], p_sc[head, 0:n, :]) / total)
            lse_ref[2 * t + head] = peak + jnp.log(total)
        out_ref[tile_rows(t), :] = jnp.concatenate(outs, axis=0).T.astype(bf16)


def attention_forward(half, slopes, query, own, other):
    return call(
        forward_kernel, "attention_forward",
        [((1024, 128), bf16), ((8, 1, TILE), f32)],
        [
            ((2, LENGTH, 128), bf16), ((128, LENGTH), bf16), ((2, LENGTH, TILE), f32),
            ((2, LENGTH, TILE), bf16),
        ],
        3 * 10**9, 2 * 10**6, 24 * 10**5, (half, slopes, query, own, other), 2,
    )


def backward_kernel(
    half, slopes, q_ref, own_ref, other_ref, grad_ref, lse_ref,
    dq_ref, down_ref, send_ref,
    ka, kt, va, dk, dv, p_sc, dp_sc, ds_sc,
):
    def rest(slot, pair):
        va[slot, :] = pair[:, 128:256]
        kt[:, slot] = pair[:, 0:128].astype(f32).T.astype(bf16)

    stage(half, slopes, own_ref, other_ref, ka, rest)
    hidden = future()
    ahead = jnp.where(half[0] == 1, 0.0, -1e30)
    for t in range(4):
        query = q_ref[tile_rows(t), :]
        grad = grad_ref[tile_rows(t), :]
        n = (2 * t + 2) * TILE
        grads = [
            jnp.where(in_head(grad.shape, head), grad.astype(f32), 0.0).astype(bf16)
            for head in range(2)
        ]
        plain = [
            jnp.where(in_head(query.shape, head), query.astype(f32) * score_scale, 0.0).astype(bf16)
            for head in range(2)
        ]
        queries = [stage_queries(query, head) for head in range(2)]
        grad_rows = jnp.concatenate(grads, axis=0)
        plain_rows = jnp.concatenate(plain, axis=0)
        delta = [None, None]
        for slot in range(2 * t + 2):
            rows = tile_rows(slot)
            low = []
            for head in range(2):
                s = masked(dot_nt(ka[head, rows, :], queries[head]), t, slot, hidden, ahead)
                p = jnp.exp(s - lse_ref[2 * t + head])
                dp = dot_nt(va[rows, :], grads[head])
                p_sc[head, rows, :] = p
                dp_sc[head, rows, :] = dp
                part = fold(p * dp, jnp.add)
                delta[head] = part if delta[head] is None else delta[head] + part
                low.append(p.astype(bf16))
            value = dot(jnp.concatenate(low, axis=1), grad_rows)
            dv[rows, :] = value if slot >= 2 * t else dv[rows, :] + value
        delta = [jnp.sum(item, axis=0, keepdims=True) for item in delta]
        for slot in range(2 * t + 2):
            rows = tile_rows(slot)
            low = []
            for head in range(2):
                ds = (p_sc[head, rows, :] * (dp_sc[head, rows, :] - delta[head])).astype(bf16)
                ds_sc[head, rows, :] = ds
                low.append(ds)
            key = dot(jnp.concatenate(low, axis=1), plain_rows)
            dk[rows, :] = key if slot >= 2 * t else dk[rows, :] + key
        outs = [
            dot(kt[head * HEAD : (head + 1) * HEAD, 0:n], ds_sc[head, 0:n, :]) for head in range(2)
        ]
        dq_ref[tile_rows(t), :] = (jnp.concatenate(outs, axis=0) * score_scale).T.astype(bf16)
    for t in range(4):
        rows = tile_rows(t)
        down_ref[rows, 0:128] = dk[tile_rows(2 * t), :]
        down_ref[rows, 128:256] = dv[tile_rows(2 * t), :]
        pair = jnp.concatenate([dk[tile_rows(2 * t + 1), :], dv[tile_rows(2 * t + 1), :]], axis=1)
        send_ref[rows, :] = swap(pair.astype(bf16))


def attention_backward(half, slopes, query, own, other, grad, lse):
    return call(
        backward_kernel, "attention_backward",
        [((1024, 128), bf16), ((1024, 256), f32), ((1024, 256), bf16)],
        [
            ((2, LENGTH, 128), bf16), ((128, LENGTH), bf16), ((LENGTH, 128), bf16),
            ((LENGTH, 128), f32), ((LENGTH, 128), f32), ((2, LENGTH, TILE), f32),
            ((2, LENGTH, TILE), f32), ((2, LENGTH, TILE), bf16),
        ],
        6 * 10**9, 3 * 10**6, 24 * 10**5, (half, slopes, query, own, other, grad, lse), 2,
    )


def output_kernel(table, mixed_ref, weight_ref, rows_ref, mine_part, other_part):
    weight = jnp.concatenate([weight_ref[...], rows_ref[...]], axis=0)
    for chunk in ORDER:
        put_parts(mine_part, other_part, chunk, dot(rows_of(table, mixed_ref, 2 * chunk), weight))


def output_parts(table, mixed, weight, rows):
    return call(
        output_kernel, "output_parts", PARTS, [], 27 * 10**7, 4 * 10**6, 0,
        (table, mixed, weight, rows), 1,
    )


def feed_kernel(table, *refs):
    up_ref, down_ref, rows_ref, bias_ref = refs[16:20]
    mine_part, other_part, act_ref, grad_ref, second_ref, cotangent_ref, extra_ref = refs[20:27]
    sems, more = refs[27:29]
    copies = assemble(table, refs[0:8], second_ref, sems)
    cotangent_copies = assemble(table, refs[8:16], cotangent_ref, more)
    bias = bias_ref[0:1, :]
    for chunk in ORDER:
        cotangent_copies[2 * chunk].wait()
        cotangent_copies[2 * chunk + 1].wait()
        cotangents = rows_of(table, cotangent_ref, 2 * chunk)
        back = jnp.concatenate(
            [dot_nt(cotangents, down_ref[...]), dot_nt(cotangents, rows_ref[...])], axis=1
        )
        copies[2 * chunk].wait()
        copies[2 * chunk + 1].wait()
        up = dot(rows_of(table, second_ref, 2 * chunk), up_ref[...]) + bias
        square = up * up
        bend = jnp.tanh(0.7978845608028654 * (up + 0.044715 * square * up))
        half = 0.5 * (1.0 + bend)
        set_rows(table, act_ref, 2 * chunk, (up * half).astype(bf16))
        slope = half + 0.5 * up * (1.0 - bend * bend) * (
            0.7978845608028654 * (1.0 + 0.134145 * square)
        )
        grad = (back * slope).astype(bf16)
        set_rows(table, grad_ref, 2 * chunk, grad)
        part = jnp.sum(grad.astype(f32), axis=0, keepdims=True)
        total = part if chunk == ORDER[0] else total + part
        put_parts(mine_part, other_part, chunk, dot_nt(grad, up_ref[...]))
    extra_rows(extra_ref, [], [total[:, 128 * g : 128 * g + 128] for g in range(4)])


def feed_parts(table, pieces, cotangents, up, down, rows, bias):
    return call(
        feed_kernel, "feed_parts", PARTS + [((1024, 512), bf16)] * 2 + [((1024, D), bf16)] * 2 + [((1024, 128), bf16)],
        [pltpu.SemaphoreType.DMA((8,)), pltpu.SemaphoreType.DMA((8,))],
        32 * 10**8, 2 * 10**7, 5 * 10**5, (table, *pieces, *cotangents, up, down, rows, bias), 1,
        16,
    )


def out_kernel(table, act_ref, down_ref, rows_ref, mine_part, other_part):
    for chunk in ORDER:
        act = rows_of(table, act_ref, 2 * chunk)
        value = dot(act[:, 0:256], down_ref[...]) + dot(act[:, 256:512], rows_ref[...])
        put_parts(mine_part, other_part, chunk, value)


def out_parts(table, act, down, rows):
    return call(
        out_kernel, "out_parts", PARTS, [], 11 * 10**8, 5 * 10**6, 0, (table, act, down, rows), 1
    )


def mixed_kernel(table, *refs):
    pieces, weight_ref, rows_ref = refs[0:8], refs[8], refs[9]
    grad_ref, all_ref, sems = refs[10:13]
    copies = assemble(table, pieces, all_ref, sems)
    weight = jnp.concatenate([weight_ref[...], rows_ref[...]], axis=0)
    for chunk in range(4):
        copies[2 * chunk].wait()
        copies[2 * chunk + 1].wait()
        grads = dot_nt(rows_of(table, all_ref, 2 * chunk), weight).astype(bf16)
        set_rows(table, grad_ref, 2 * chunk, grads)


def mixed_back(table, pieces, weight, rows):
    return call(
        mixed_kernel, "mixed_back",
        [((1024, 128), bf16), ((1024, D), bf16)],
        [pltpu.SemaphoreType.DMA((8,))],
        27 * 10**7, 4 * 10**6, 0, (table, *pieces, weight, rows), 1, 8,
    )


def last_kernel(
    table, query_ref, own_ref, other_ref, project_ref, normal_ref, middle_ref,
    mine_part, other_part, joined_ref, extra_ref,
):
    gain = None
    for chunk in ORDER:
        own = rows_of(table, own_ref, 2 * chunk)
        other = rows_of(table, other_ref, 2 * chunk).astype(f32)
        joined = jnp.concatenate(
            [rows_of(table, query_ref, 2 * chunk), (own + other).astype(bf16)], axis=1
        )
        set_rows(table, joined_ref, 2 * chunk, joined)
        bias = jnp.sum(joined.astype(f32), axis=0, keepdims=True)
        biases = bias if chunk == ORDER[0] else biases + bias
        value = dot_nt(joined, project_ref[...])
        put_parts(mine_part, other_part, chunk, value)
        normal = rows_of(table, normal_ref, 2 * chunk).astype(f32)
        tilted = jnp.sum(value * normal, axis=0, keepdims=True)
        plain = jnp.sum(value, axis=0, keepdims=True)
        gain = tilted if gain is None else gain + tilted
        offset = plain if chunk == ORDER[0] else offset + plain
    pairs = [
        (gain, offset), (middle_ref[0:1, :], middle_ref[1:2, :]),
        (middle_ref[2:3, :], middle_ref[3:4, :]),
    ]
    extra_rows(extra_ref, pairs, [biases[:, 0:128], biases[:, 256:384]])


def last_parts(table, query, own, other, project, normal, sums):
    return call(
        last_kernel, "last_parts", PARTS + [((1024, 384), bf16), ((1024, 128), bf16)], [],
        8 * 10**8, 7 * 10**6, 0, (table, query, own, other, project, normal, sums), 1,
    )


def join_kernel(mine_ref, core_ref, here_ref, near_ref, far_ref, back_ref):
    for d, ref in enumerate((here_ref, near_ref, far_ref, back_ref)):
        ref[...] = (mine_ref[d] + core_ref[d].astype(f32)).astype(ref.dtype)


def join(mine, core):
    return call(
        join_kernel, "join", [((ROWS, D), f32)] + [((ROWS, D), bf16)] * 3, [], 10**6, 4 * 10**6, 0,
        (mine, core),
    )


def landed(refs):
    here, near, far, back = [ref[...].astype(f32) for ref in refs]
    return here + near + far + back


def middle_kernel(*refs):
    input_ref, vector_ref, mid_ref, normal_ref, inverse_ref, normed_ref = refs[4:10]
    mid = input_ref[...].astype(f32) + (landed(refs[0:4]) + vector_ref[2:3, :])
    normal, inverse = normalize(mid)
    mid_ref[...] = mid
    normal_ref[...] = normal
    inverse_ref[...] = inverse
    normed_ref[...] = (normal * vector_ref[3:4, :] + vector_ref[4:5, :]).astype(bf16)


def middle(ends, inputs, vectors):
    return call(
        middle_kernel, "middle",
        [((ROWS, D), f32), ((ROWS, D), f32), ((ROWS, 1), f32), ((ROWS, D), bf16)], [],
        10**6, 3 * 10**6, 0, (*ends, inputs, vectors),
    )


def middle_back_kernel(*refs):
    cotangent_ref, vector_ref, normal_ref, inverse_ref, grad_ref, branch_ref, sum_ref = refs[4:11]
    second = landed(refs[0:4])
    normal = normal_ref[...]
    cotangent = cotangent_ref[...].astype(f32)
    grad = cotangent + norm_back(second, vector_ref[3:4, :], normal, inverse_ref[...])
    grad_ref[...] = grad
    branch = grad.astype(bf16)
    branch_ref[...] = branch
    sum_ref[0:1, :] = jnp.sum(second * normal, axis=0, keepdims=True)
    sum_ref[1:2, :] = jnp.sum(second, axis=0, keepdims=True)
    sum_ref[2:3, :] = jnp.sum(branch.astype(f32), axis=0, keepdims=True)
    sum_ref[3:4, :] = jnp.sum(cotangent, axis=0, keepdims=True)


def middle_back(ends, cotangent, vectors, normal, inverse):
    return call(
        middle_back_kernel, "middle_back",
        [((ROWS, D), f32), ((ROWS, D), bf16), ((8, D), f32)], [],
        10**6, 3 * 10**6, 0, (*ends, cotangent, vectors, normal, inverse),
    )


def block_kernel(*refs):
    mid_ref, vector_ref, out_ref = refs[4:7]
    out_ref[...] = (mid_ref[...] + landed(refs[0:4]) + vector_ref[5:6, :]).astype(bf16)


def block_end(ends, mid, vectors):
    return call(
        block_kernel, "block_end", [((ROWS, D), bf16)], [], 10**6, 2 * 10**6, 0,
        (*ends, mid, vectors),
    )[0]


def input_kernel(*refs):
    input_ref, vector_ref, grad_ref, out_ref = refs[4:8]
    normal, inverse = normalize(input_ref[...].astype(f32))
    out_ref[...] = grad_ref[...] + norm_back(
        landed(refs[0:4]), vector_ref[0:1, :], normal, inverse
    )


def input_end(ends, inputs, vectors, grad):
    return call(
        input_kernel, "input_end", [((ROWS, D), f32)], [], 10**6, 3 * 10**6, 0,
        (*ends, inputs, vectors, grad),
    )[0]


def over_seq(ref, shard, columns):
    value = ref[8 * shard, :, columns].astype(f32)
    for q in range(1, 8):
        value = value + ref[8 * shard + q, :, columns].astype(f32)
    return value


def early_kernel(whose, rows_ref, up_ref, total_ref, small_ref, up_small):
    rows = rows_ref[0].astype(f32)
    for q in range(1, 8):
        rows = rows + rows_ref[q].astype(f32)
    ups = []
    for shard in range(16):
        up_small[shard] = over_seq(up_ref, shard, slice(512, 640))
        ups.append(over_seq(up_ref, shard, slice(0, 512)))
    pieces = [rows]
    for block in range(4):
        pieces.append(
            jnp.concatenate(
                [
                    ups[shard][:, 0:256] + ups[shard ^ 2][:, 256:512]
                    for shard in range(4 * block, 4 * block + 4)
                ],
                axis=1,
            )
        )
    pieces.append(jnp.zeros((8, D), f32))
    total_ref[...] = jnp.concatenate(pieces, axis=0).astype(bf16)
    mine, twin = up_small[whose[0]], up_small[whose[0] ^ 2]
    small_ref[0:1, :] = jnp.concatenate([mine[0:1] + twin[2:3], mine[1:2] + twin[3:4]], axis=1)


def early_totals(whose, rows, up):
    return call(
        early_kernel, "early_totals", [((80, D), bf16), ((8, 256), f32)],
        [((16, 8, 128), f32)], 10**6, 4 * 10**6, 0, (whose, rows, up), 1,
    )


def late_kernel(whose, last_ref, total_ref, small_ref, last_small):
    lasts = []
    for shard in range(16):
        last_small[shard] = over_seq(last_ref, shard, slice(384, 512))
        lasts.append(over_seq(last_ref, shard, slice(0, 384)))
    pieces = []
    for kind in range(3):
        start = 128 * kind
        pieces.append(
            jnp.concatenate(
                [
                    lasts[shard][:, start : start + 64]
                    + lasts[shard ^ 2][:, start + 64 : start + 128]
                    for shard in range(16)
                ],
                axis=1,
            )
        )
    pieces.append(jnp.zeros((8, D), f32))
    total = jnp.concatenate(pieces, axis=0).astype(bf16)
    for q in range(8):
        total_ref[q] = total
    last_sum = last_small[0]
    for shard in range(1, 16):
        last_sum = last_sum + last_small[shard]
    mine, twin = last_small[whose[0]], last_small[whose[0] ^ 2]
    small_ref[0:3, :] = last_sum[0:3]
    small_ref[3:4, :] = jnp.concatenate(
        [mine[3:4, 0:64] + twin[3:4, 64:128], mine[4:5, 0:64] + twin[4:5, 64:128]], axis=1
    )


def late_totals(whose, last):
    return call(
        late_kernel, "late_totals", [((8, 32, D), bf16), ((8, 128), f32)],
        [((16, 8, 128), f32)], 10**6, 2 * 10**6, 0, (whose, last), 1,
    )


def early_out_kernel(order, *refs):
    output_ref, down_ref, up_ref = refs[4:7]
    for k in range(4):
        for e in range(2):
            q = order[2 * k + e]
            total = refs[k][80 * e : 80 * e + 80, :].astype(f32)
            eight = pl.multiple_of(8 * q, 8)
            output_ref[pl.ds(eight, 8), :] = total[0:8]
            down_ref[pl.ds(pl.multiple_of(32 * q, 32), 32), :] = total[8:40]
            for block in range(4):
                up_ref[pl.ds(eight, 8), D * block : D * block + D] = total[
                    40 + 8 * block : 48 + 8 * block
                ]


def early_out(order, pieces):
    return call(
        early_out_kernel, "early_out", [((64, D), f32), ((256, D), f32), ((64, FF), f32)], [],
        10**6, 4 * 10**6, 0, (order, *pieces), 1,
    )


def late_out_kernel(total_ref, attention_ref):
    for q in range(8):
        total = total_ref[q].astype(f32)
        for kind in range(3):
            attention_ref[8 * q : 8 * q + 8, D * kind : D * kind + D] = total[
                8 * kind : 8 * kind + 8
            ]


def late_out(total):
    return call(
        late_out_kernel, "late_out", [((64, 3 * D), f32)], [], 10**6, 10**6, 0, (total,)
    )[0]


def shift(value, axis, step):
    size = lax.axis_size(axis)
    return lax.ppermute(value, axis, [(i, (i + step) % size) for i in range(size)])


def gather(own, *first):
    mine = [shift(own, "y", -step) for step in (1, 2, 3)]
    if first:
        mine = list(lax.optimization_barrier((*mine, *first))[0:3])
    mine = [own, *mine]
    return mine + [shift(block, "c", 1) for block in mine]


def joined(mine, other, *first):
    core = shift(other, "c", 1)
    return join(mine, after(core, *first) if first else core)


def spread(here, near, far, back):
    return here, shift(near, "y", 1), shift(far, "y", 2), shift(back, "y", 3)


def scatter(mine, other, *first):
    return spread(*joined(mine, other, *first))


def exchange(value, axes):
    return lax.all_to_all(value, axes, split_axis=0, concat_axis=0, tiled=True)


def after(value, *others):
    return lax.optimization_barrier((value, *others))[0]


def normalize(values):
    centre = jnp.mean(values, axis=-1, keepdims=True)
    centred = values - centre
    spread = jnp.mean(centred * centred, axis=-1, keepdims=True)
    inverse = lax.rsqrt(spread + epsilon)
    return centred * inverse, inverse


def norm_back(grad, gain, normal, inverse):
    scaled = grad * gain
    return inverse * (
        scaled
        - jnp.mean(scaled, axis=-1, keepdims=True)
        - normal * jnp.mean(scaled * normal, axis=-1, keepdims=True)
    )


def on_device(
    block_input,
    first_gain,
    first_shift,
    attention_weight,
    query_bias,
    value_bias,
    output_weight,
    output_bias,
    second_gain,
    second_shift,
    upward_weight,
    upward_bias,
    downward_weight,
    downward_bias,
    cotangent,
):
    y = lax.axis_index("y")
    xh = lax.axis_index("xh")
    c = lax.axis_index("c")
    shard = 4 * y + 2 * xh + c
    piece = np.arange(8)
    table = (2 * ((y + piece % 4) % 4) + (c ^ (piece // 4))).astype(jnp.int32)
    half = xh[None].astype(jnp.int32)
    whose = shard[None].astype(jnp.int32)
    slopes = jnp.exp2(-8.0 * (jnp.stack([shard, shard ^ 2]) + 1).astype(f32) / HEADS)

    with jax.named_scope("weights_attention"):
        vectors_own = [
            first_gain, first_shift, output_bias, second_gain, second_shift, downward_bias
        ]
        small = sum(
            jnp.pad(item[None], ((0, 15), (64 * g, 320 - 64 * g)))
            for g, item in enumerate(vectors_own)
        )
        small = small + jnp.pad(query_bias[None], ((1, 14), (0, 320)))
        small = small + jnp.pad(value_bias[None], ((1, 14), (64, 256)))
        small = small + jnp.pad(upward_bias[None], ((1, 14), (128, 0)))
        payload, up_payload = call(
            deal_kernel, "deal", [((16, 80, 384), bf16), ((16, 64, 512), bf16)], [],
            0, 4 * 10**6, 0, (attention_weight, small, upward_weight),
        )
        arrived = exchange(payload, FSDP)

    with jax.named_scope("first"):
        inputs = gather(block_input)
        heads_own, heads_send, normed_first, normal_first, project, vectors, bias_up = (
            first_heads(table, whose, inputs, arrived)
        )
        query = queries(normed_first, project, bias_up)
        heads_arrived = shift(heads_send, "xh", 1)
        cotangents = gather(after(cotangent, heads_send))
    with jax.named_scope("weights_upward"):
        upward_pair = exchange(after(up_payload, arrived), FSDP).reshape(D, 512)
    with jax.named_scope("weights_pair"):
        output_rows = shift(after(output_weight, arrived), "xh", 1)
        downward_rows = shift(after(downward_weight, heads_arrived), "xh", 1)
    with jax.named_scope("attention"):
        mixed, lse = attention_forward(half, slopes, query, heads_own, heads_arrived)
    with jax.named_scope("output"):
        mixed = after(mixed, upward_pair, *cotangents)
        mine, other = output_parts(table, mixed, output_weight, output_rows)
        residual_mid, normal_second, inverse_second, normed_second = middle(
            scatter(mine, other), block_input, vectors
        )

    with jax.named_scope("feed"):
        mine, other, activated, upward_grad, seconds, all_cotangents, extra = feed_parts(
            table, gather(normed_second), cotangents, upward_pair, downward_weight,
            downward_rows, bias_up,
        )
        sums_near = joined(mine, other)
        ends = spread(*sums_near)

    with jax.named_scope("upward_gradients"):
        late_grad, late_act = lax.optimization_barrier((upward_grad, activated, sums_near[0]))[0:2]
        upward_weight_grad = dot_tn(seconds, late_grad).astype(bf16)
        downward_grad = dot_tn(late_act, all_cotangents)
        downward_other = downward_grad[256:].astype(bf16)
        out_mine, out_other = out_parts(table, late_act, downward_weight, downward_rows)
    with jax.named_scope("feed"):
        ends = lax.optimization_barrier(
            (*ends, upward_weight_grad, downward_other, out_mine)
        )[0:4]
        mid_grad, branch_grad, sums = middle_back(
            ends, cotangent, vectors, normal_second, inverse_second
        )

    with jax.named_scope("upward_gradients"):
        shares = jnp.concatenate([upward_weight_grad, extra], axis=-1).reshape(128, 8, 640)
    with jax.named_scope("mixed_back"):
        mixed_grad, branch_grads = mixed_back(
            table, gather(branch_grad, shares), output_weight, output_rows
        )
        output_grad = dot_tn(mixed, branch_grads)
        output_other = output_grad[64:].astype(bf16)
        mixed_grad = after(mixed_grad, output_other)
    with jax.named_scope("upward_sums"):
        arrived_up = exchange(shares, FSDP + SEQ)
    with jax.named_scope("attention_back"):
        output_arrived = shift(output_other, "xh", 1)
        query_grad, back_own, back_send = attention_backward(
            half, slopes, query, heads_own, heads_arrived, mixed_grad, lse
        )
        back_send = after(back_send, arrived_up)
        back_arrived = shift(back_send, "xh", 1)
    with jax.named_scope("feed_out"):
        out_near = joined(out_mine, after(out_other, back_send))
        out_ends = spread(*out_near)
        block_output = block_end(out_ends, residual_mid, vectors)
    with jax.named_scope("row_gradients"):
        downward_arrived = shift(after(downward_other, branch_grad), "xh", 1)
        downward_sum = (downward_grad[:256] + downward_arrived.astype(f32)).astype(bf16)
        output_sum = (output_grad[:64] + output_arrived.astype(f32)).astype(bf16)
        rows_sent = jnp.concatenate(
            [output_sum.reshape(8, 8, D), downward_sum.reshape(8, 32, D)], axis=1
        )
        rows_all = exchange(after(rows_sent, arrived_up), SEQ)
    with jax.named_scope("first_back"):
        back_arrived = after(back_arrived, out_near[0])
        mine, other, head_grads, last_extra = last_parts(
            table, query_grad, back_own, back_arrived, project, normal_first, sums
        )
        last_near = joined(mine, other)
        ends = spread(*last_near)
        input_gradient = input_end(ends, block_input, vectors, mid_grad)
    with jax.named_scope("attention_gradients"):
        weight_grad = dot_tn(normed_first, head_grads).astype(bf16)
        shares = jnp.concatenate([weight_grad, last_extra], axis=-1).reshape(128, 8, 512)
        shares = after(shares, rows_all, *out_ends[1:4])
        arrived_last = exchange(shares, FSDP + SEQ)
    with jax.named_scope("early_totals"):
        early, early_small = early_totals(whose, after(rows_all, shares), arrived_up)
        early_pair = jnp.concatenate([early, shift(early, "xl", 1)], axis=0)
        early_all = [early_pair] + [shift(early_pair, "z", -step) for step in (1, 2, 3)]
        z = lax.axis_index("z")
        xl = lax.axis_index("xl")
        order = (2 * ((z + piece // 2) % 4) + (xl ^ (piece % 2))).astype(jnp.int32)
        output_weight_gradient, downward_weight_gradient, upward_weight_gradient = early_out(
            order, early_all
        )
    with jax.named_scope("late_totals"):
        late, late_small = late_totals(
            whose, after(arrived_last, input_gradient, early_pair)
        )
        attention_weight_gradient = late_out(exchange(late, SEQ))

    return (
        block_output,
        input_gradient,
        late_small[0, 0:64],
        late_small[0, 64:128],
        attention_weight_gradient,
        late_small[3, 0:64],
        late_small[3, 64:128],
        output_weight_gradient,
        late_small[2, 0:64],
        late_small[1, 0:64],
        late_small[1, 64:128],
        upward_weight_gradient,
        early_small[0],
        downward_weight_gradient,
        late_small[2, 64:128],
    )


def solution(mesh):
    grid = Mesh(mesh.devices.reshape(4, 2, 4, 2, 2), ALL)
    tokens = P(ALL, None)
    rows = P(FSDP, None)
    line = P(FSDP)
    return jax.shard_map(
        on_device,
        mesh=grid,
        in_specs=(
            tokens, line, line, rows, line, line, rows, line, line, line, rows, line, rows, line,
            tokens,
        ),
        out_specs=(
            tokens, tokens, line, line, rows, line, line, rows, line, line, line, rows, line, rows,
            line,
        ),
        check_vma=False,
    )
```

```python
import jax
import jax.numpy as jnp
import numpy as np
from jax import lax
from jax.experimental import pallas as pl
from jax.experimental.pallas import tpu as pltpu
from jax.sharding import Mesh
from jax.sharding import PartitionSpec as P

D = 1024
HEADS = 16
HEAD = 64
FF = 4096

epsilon = 1e-05
score_scale = 0.125
bf16 = jnp.bfloat16
f32 = jnp.float32

SEQ = ("z", "xl")
FSDP = ("y", "xh", "c")
ALL = SEQ + FSDP
ROWS = 128
TILE = 256
TILES = 8
LENGTH = TILE * TILES

NT = (((1,), (1,)), ((), ()))


def dot(a, b):
    return jnp.dot(a, b, preferred_element_type=f32)


def dot_nt(a, b):
    return lax.dot_general(a, b, NT, preferred_element_type=f32)


def dot_tn(a, b):
    return lax.dot_general(a, b, (((0,), (0,)), ((), ())), preferred_element_type=f32)


smem = pl.BlockSpec(memory_space=pltpu.SMEM)
vmem = pl.BlockSpec(memory_space=pltpu.VMEM)


def call(kernel, name, outs, scratch, flops, moved, transcendentals, args, scalars=0, pieces=0):
    rest = len(args) - scalars - pieces
    return pl.pallas_call(
        kernel,
        out_shape=tuple(jax.ShapeDtypeStruct(shape, kind) for shape, kind in outs),
        in_specs=[smem] * scalars + [pl.BlockSpec(memory_space=pl.ANY)] * pieces + [vmem] * rest,
        out_specs=(vmem,) * len(outs),
        scratch_shapes=[
            pltpu.VMEM(*item) if isinstance(item, tuple) else item for item in scratch
        ],
        compiler_params=pltpu.CompilerParams(vmem_limit_bytes=60 * 2**20),
        cost_estimate=pl.CostEstimate(
            flops=flops, bytes_accessed=moved, transcendentals=transcendentals
        ),
        name=name,
    )(*args)


def first_row(table, p):
    return pl.multiple_of(table[p] * ROWS, ROWS)


def assemble(table, refs, out, sems):
    copies = [
        pltpu.make_async_copy(refs[p], out.at[pl.ds(first_row(table, p), ROWS), :], sems.at[p])
        for p in range(8)
    ]
    for copy in copies:
        copy.start()
    return copies


def rows_of(table, ref, p):
    return jnp.concatenate(
        [ref[pl.ds(first_row(table, p + b), ROWS), :] for b in range(2)], axis=0
    )


def set_rows(table, ref, p, value):
    for b in range(2):
        ref[pl.ds(first_row(table, p + b), ROWS), :] = value[b * ROWS : (b + 1) * ROWS]


def put_parts(mine_ref, other_ref, chunk, value):
    ref = mine_ref if chunk < 2 else other_ref
    for b in range(2):
        ref[2 * (chunk % 2) + b] = value[b * ROWS : (b + 1) * ROWS].astype(ref.dtype)


PARTS = [((4, ROWS, D), bf16), ((4, ROWS, D), bf16)]
ORDER = (2, 3, 0, 1)


def extra_rows(out_ref, lanes, pairs, lines):
    row = lax.broadcasted_iota(jnp.int32, (64, 128), 0) % 8
    for shard in range(16):
        columns = slice(64 * shard, 64 * shard + 64)
        block = jnp.zeros((64, 128), f32)
        for r, (left, right) in enumerate(pairs):
            line = jnp.concatenate([left[:, columns], right[:, columns]], axis=1)
            block = jnp.where(row == r, line, block)
        for r, line in enumerate(lines):
            block = jnp.where(row == len(pairs) + r, line, block)
        out_ref[64 * shard : 64 * shard + 64, lanes] = block.astype(bf16)


def deal_kernel(weight_ref, small_ref, up_ref, out_ref, up_out):
    small = small_ref[...]

    def piece(kind, head):
        start = kind * D + head * HEAD
        return weight_ref[:, start : start + HEAD]

    for y in range(4):
        for x in range(2):
            for c in range(2):
                shard = 4 * y + 2 * x + c
                twin = shard ^ 2
                out_ref[shard, 0:64, :] = jnp.concatenate(
                    [
                        piece(kind, head) for kind in range(3) for head in (shard, twin)
                    ],
                    axis=1,
                )
                out_ref[shard, 64:80, :] = small
                up_out[shard, :, 0:256] = up_ref[:, 256 * shard : 256 * shard + 256]
                up_out[shard, :, 256:512] = up_ref[:, 256 * twin : 256 * twin + 256]


def swap(pairs):
    return jnp.concatenate(
        [pairs[:, 64:128], pairs[:, 0:64], pairs[:, 192:256], pairs[:, 128:192]], axis=1
    )


def first_kernel(table, shard_ref, *refs):
    pieces, arrived = refs[0:8], refs[8]
    kv_ref, send_ref, normed_ref, normal_ref, project_ref, vector_ref, bias_ref = refs[9:16]
    inputs, sems = refs[16:18]
    copies = assemble(table, pieces, inputs, sems)
    for r in range(16):
        project_ref[64 * r : 64 * r + 64, :] = arrived[r, 0:64, :]
    rows = [arrived[r, 64:80, :].astype(f32) for r in range(16)]
    for g in range(6):
        vector_ref[g : g + 1, :] = jnp.concatenate(
            [rows[r][0:1, 64 * g : 64 * g + 64] for r in range(16)], axis=1
        )
    shard = shard_ref[0]
    mine = arrived[shard, 64:80, :].astype(f32)[1:2]
    twin = arrived[shard ^ 2, 64:80, :].astype(f32)[1:2]
    bias_ref[0:1, :] = jnp.concatenate([mine[:, 128:], twin[:, 128:]], axis=1)
    bias_ref[1:2, 0:128] = jnp.concatenate([mine[:, 0:64], twin[:, 0:64]], axis=1)
    bias = jnp.concatenate(
        [jnp.zeros((1, 2 * HEAD), f32), mine[:, 64:128], twin[:, 64:128]], axis=1
    )
    gain = vector_ref[0:1, :]
    offset = vector_ref[1:2, :]
    for copy in copies:
        copy.wait()
    for chunk in range(4):
        rows = slice(chunk * TILE, (chunk + 1) * TILE)
        normal, unused = normalize(inputs[rows, :].astype(f32))
        normal_ref[rows, :] = normal.astype(bf16)
        normed = (normal * gain + offset).astype(bf16)
        normed_ref[rows, :] = normed
        heads = (dot(normed, project_ref[:, 128:384]) + bias).astype(bf16)
        kv_ref[rows, :] = heads
        send_ref[rows, :] = swap(heads)


def query_kernel(normed_ref, project_ref, bias_ref, query_ref):
    bias = bias_ref[1:2, 0:128]
    for chunk in range(4):
        rows = slice(chunk * TILE, (chunk + 1) * TILE)
        value = dot(normed_ref[rows, :], project_ref[:, 0:128]) + bias
        query_ref[rows, :] = value.astype(bf16)


def queries(normed, project, bias):
    return call(
        query_kernel, "queries", [((1024, 128), bf16)], [], 27 * 10**7, 3 * 10**6, 0,
        (normed, project, bias),
    )[0]


def first_heads(table, shard, pieces, arrived):
    return call(
        first_kernel, "first_heads",
        [
            ((1024, 256), bf16), ((1024, 256), bf16), ((1024, D), bf16), ((1024, D), bf16),
            ((D, 384), bf16), ((8, D), f32), ((8, 512), f32),
        ],
        [((1024, D), bf16), pltpu.SemaphoreType.DMA((8,))],
        8 * 10**8, 10**7, 10**4, (table, shard, *pieces, arrived), 2, 8,
    )


def in_head(shape, head):
    lane = lax.broadcasted_iota(jnp.int32, shape, 1)
    return (lane < HEAD) if head == 0 else (lane >= HEAD)


def stage_queries(query, head):
    lane = lax.broadcasted_iota(jnp.int32, query.shape, 1) - (HEAD if head == 0 else 0)
    ones = jnp.where((lane >= 0) & (lane < 3), 1.0, 0.0)
    scaled = query.astype(f32) * score_scale
    return jnp.where(in_head(query.shape, head), scaled, ones).astype(bf16)


def stage_keys(key, head, slope, first):
    shape = key.shape
    lane = lax.broadcasted_iota(jnp.int32, shape, 1) - (HEAD if head == 0 else 0)
    row = lax.broadcasted_iota(jnp.int32, shape, 0)
    place = slope * (row + first).astype(f32)
    high = place.astype(bf16).astype(f32)
    rest = place - high
    middle = rest.astype(bf16).astype(f32)
    low = rest - middle
    extra = jnp.where(
        lane == 0, high, jnp.where(lane == 1, middle, jnp.where(lane == 2, low, 0.0))
    )
    return jnp.where(in_head(shape, head), key.astype(f32), extra).astype(bf16)


def fold(tile, op):
    parts = [tile[8 * g : 8 * g + 8] for g in range(TILE // 8)]
    while len(parts) > 1:
        parts = [op(parts[2 * g], parts[2 * g + 1]) for g in range(len(parts) // 2)]
    return parts[0]


def future():
    key = lax.broadcasted_iota(jnp.int32, (TILE, TILE), 0)
    query = lax.broadcasted_iota(jnp.int32, (TILE, TILE), 1)
    return key > query


def tile_rows(t):
    return slice(t * TILE, (t + 1) * TILE)


def stage(half, slopes, own_ref, other_ref, ka, emit_rest):
    for t in range(4):
        for side, ref in enumerate((own_ref, other_ref)):
            slot = tile_rows(2 * t + side)
            pair = ref[tile_rows(t), :]
            first = TILE * (2 * t + (half[0] if side == 0 else 1 - half[0])) - LENGTH // 2
            for head in range(2):
                ka[head, slot, :] = stage_keys(pair[:, 0:128], head, slopes[head], first)
            emit_rest(slot, pair)


def masked(s, t, slot, hidden, ahead):
    if slot == 2 * t:
        return jnp.where(hidden, -1e30, s)
    return s + ahead if slot == 2 * t + 1 else s


def forward_kernel(half, slopes, q_ref, own_ref, other_ref, out_ref, lse_ref, ka, vt, s_sc, p_sc):
    def rest(slot, pair):
        vt[:, slot] = pair[:, 128:256].astype(f32).T.astype(bf16)

    stage(half, slopes, own_ref, other_ref, ka, rest)
    hidden = future()
    ahead = jnp.where(half[0] == 1, 0.0, -1e30)
    for t in range(4):
        query = q_ref[tile_rows(t), :]
        n = (2 * t + 2) * TILE
        outs = []
        for head in range(2):
            q = stage_queries(query, head)
            peak = None
            for slot in range(2 * t + 2):
                rows = tile_rows(slot)
                s = masked(dot_nt(ka[head, rows, :], q), t, slot, hidden, ahead)
                s_sc[head, rows, :] = s
                top = fold(s, jnp.maximum)
                peak = top if peak is None else jnp.maximum(peak, top)
            peak = jnp.max(peak, axis=0, keepdims=True)
            total = None
            for slot in range(2 * t + 2):
                rows = tile_rows(slot)
                p = jnp.exp(s_sc[head, rows, :] - peak)
                p_sc[head, rows, :] = p.astype(bf16)
                part = fold(p, jnp.add)
                total = part if total is None else total + part
            total = jnp.sum(total, axis=0, keepdims=True)
            outs.append(dot(vt[head * HEAD : (head + 1) * HEAD, 0:n], p_sc[head, 0:n, :]) / total)
            lse_ref[2 * t + head] = peak + jnp.log(total)
        out_ref[tile_rows(t), :] = jnp.concatenate(outs, axis=0).T.astype(bf16)


def attention_forward(half, slopes, query, own, other):
    return call(
        forward_kernel, "attention_forward",
        [((1024, 128), bf16), ((8, 1, TILE), f32)],
        [
            ((2, LENGTH, 128), bf16), ((128, LENGTH), bf16), ((2, LENGTH, TILE), f32),
            ((2, LENGTH, TILE), bf16),
        ],
        3 * 10**9, 2 * 10**6, 24 * 10**5, (half, slopes, query, own, other), 2,
    )


def backward_kernel(
    half, slopes, q_ref, own_ref, other_ref, grad_ref, lse_ref,
    dq_ref, down_ref, send_ref,
    ka, kt, va, dk, dv, p_sc, dp_sc, ds_sc,
):
    def rest(slot, pair):
        va[slot, :] = pair[:, 128:256]
        kt[:, slot] = pair[:, 0:128].astype(f32).T.astype(bf16)

    stage(half, slopes, own_ref, other_ref, ka, rest)
    hidden = future()
    ahead = jnp.where(half[0] == 1, 0.0, -1e30)
    for t in range(4):
        query = q_ref[tile_rows(t), :]
        grad = grad_ref[tile_rows(t), :]
        n = (2 * t + 2) * TILE
        grads = [
            jnp.where(in_head(grad.shape, head), grad.astype(f32), 0.0).astype(bf16)
            for head in range(2)
        ]
        plain = [
            jnp.where(in_head(query.shape, head), query.astype(f32) * score_scale, 0.0).astype(bf16)
            for head in range(2)
        ]
        queries = [stage_queries(query, head) for head in range(2)]
        grad_rows = jnp.concatenate(grads, axis=0)
        plain_rows = jnp.concatenate(plain, axis=0)
        delta = [None, None]
        for slot in range(2 * t + 2):
            rows = tile_rows(slot)
            low = []
            for head in range(2):
                s = masked(dot_nt(ka[head, rows, :], queries[head]), t, slot, hidden, ahead)
                p = jnp.exp(s - lse_ref[2 * t + head])
                dp = dot_nt(va[rows, :], grads[head])
                p_sc[head, rows, :] = p
                dp_sc[head, rows, :] = dp
                part = fold(p * dp, jnp.add)
                delta[head] = part if delta[head] is None else delta[head] + part
                low.append(p.astype(bf16))
            value = dot(jnp.concatenate(low, axis=1), grad_rows)
            dv[rows, :] = value if slot >= 2 * t else dv[rows, :] + value
        delta = [jnp.sum(item, axis=0, keepdims=True) for item in delta]
        for slot in range(2 * t + 2):
            rows = tile_rows(slot)
            low = []
            for head in range(2):
                ds = (p_sc[head, rows, :] * (dp_sc[head, rows, :] - delta[head])).astype(bf16)
                ds_sc[head, rows, :] = ds
                low.append(ds)
            key = dot(jnp.concatenate(low, axis=1), plain_rows)
            dk[rows, :] = key if slot >= 2 * t else dk[rows, :] + key
        outs = [
            dot(kt[head * HEAD : (head + 1) * HEAD, 0:n], ds_sc[head, 0:n, :]) for head in range(2)
        ]
        dq_ref[tile_rows(t), :] = (jnp.concatenate(outs, axis=0) * score_scale).T.astype(bf16)
    for t in range(4):
        rows = tile_rows(t)
        down_ref[rows, 0:128] = dk[tile_rows(2 * t), :]
        down_ref[rows, 128:256] = dv[tile_rows(2 * t), :]
        pair = jnp.concatenate([dk[tile_rows(2 * t + 1), :], dv[tile_rows(2 * t + 1), :]], axis=1)
        send_ref[rows, :] = swap(pair.astype(bf16))


def attention_backward(half, slopes, query, own, other, grad, lse):
    return call(
        backward_kernel, "attention_backward",
        [((1024, 128), bf16), ((1024, 256), f32), ((1024, 256), bf16)],
        [
            ((2, LENGTH, 128), bf16), ((128, LENGTH), bf16), ((LENGTH, 128), bf16),
            ((LENGTH, 128), f32), ((LENGTH, 128), f32), ((2, LENGTH, TILE), f32),
            ((2, LENGTH, TILE), f32), ((2, LENGTH, TILE), bf16),
        ],
        3 * 10**9, 3 * 10**6, 24 * 10**5, (half, slopes, query, own, other, grad, lse), 2,
    )


def output_kernel(table, mixed_ref, weight_ref, rows_ref, mine_part, other_part):
    weight = jnp.concatenate([weight_ref[...], rows_ref[...]], axis=0)
    for chunk in ORDER:
        put_parts(mine_part, other_part, chunk, dot(rows_of(table, mixed_ref, 2 * chunk), weight))


def output_parts(table, mixed, weight, rows):
    return call(
        output_kernel, "output_parts", PARTS, [], 27 * 10**7, 4 * 10**6, 0,
        (table, mixed, weight, rows), 1,
    )


def feed_kernel(table, *refs):
    up_ref, down_ref, rows_ref, bias_ref = refs[16:20]
    mine_part, other_part, act_ref, grad_ref, second_ref, cotangent_ref, sum_ref = refs[20:27]
    sems, more = refs[27:29]
    copies = assemble(table, refs[0:8], second_ref, sems)
    cotangent_copies = assemble(table, refs[8:16], cotangent_ref, more)
    bias = bias_ref[0:1, :]
    for chunk in ORDER:
        cotangent_copies[2 * chunk].wait()
        cotangent_copies[2 * chunk + 1].wait()
        cotangents = rows_of(table, cotangent_ref, 2 * chunk)
        back = jnp.concatenate(
            [dot_nt(cotangents, down_ref[...]), dot_nt(cotangents, rows_ref[...])], axis=1
        )
        copies[2 * chunk].wait()
        copies[2 * chunk + 1].wait()
        up = dot(rows_of(table, second_ref, 2 * chunk), up_ref[...]) + bias
        square = up * up
        bend = jnp.tanh(0.7978845608028654 * (up + 0.044715 * square * up))
        half = 0.5 * (1.0 + bend)
        set_rows(table, act_ref, 2 * chunk, (up * half).astype(bf16))
        slope = half + 0.5 * up * (1.0 - bend * bend) * (
            0.7978845608028654 * (1.0 + 0.134145 * square)
        )
        grad = (back * slope).astype(bf16)
        set_rows(table, grad_ref, 2 * chunk, grad)
        part = jnp.sum(grad.astype(f32), axis=0, keepdims=True)
        total = part if chunk == ORDER[0] else total + part
        put_parts(mine_part, other_part, chunk, dot_nt(grad, up_ref[...]))
    sum_ref[0:1, :] = total


def feed_parts(table, pieces, cotangents, up, down, rows, bias):
    return call(
        feed_kernel, "feed_parts", PARTS + [((1024, 512), bf16)] * 2 + [((1024, D), bf16)] * 2 + [((8, 512), f32)],
        [pltpu.SemaphoreType.DMA((8,)), pltpu.SemaphoreType.DMA((8,))],
        32 * 10**8, 2 * 10**7, 5 * 10**5, (table, *pieces, *cotangents, up, down, rows, bias), 1,
        16,
    )


def out_kernel(table, act_ref, down_ref, rows_ref, mine_part, other_part):
    for chunk in ORDER:
        act = rows_of(table, act_ref, 2 * chunk)
        value = dot(act[:, 0:256], down_ref[...]) + dot(act[:, 256:512], rows_ref[...])
        put_parts(mine_part, other_part, chunk, value)


def out_parts(table, act, down, rows):
    return call(
        out_kernel, "out_parts", PARTS, [], 11 * 10**8, 5 * 10**6, 0, (table, act, down, rows), 1
    )


def mixed_kernel(table, *refs):
    pieces, weight_ref, rows_ref = refs[0:8], refs[8], refs[9]
    grad_ref, all_ref, sems = refs[10:13]
    copies = assemble(table, pieces, all_ref, sems)
    weight = jnp.concatenate([weight_ref[...], rows_ref[...]], axis=0)
    for chunk in range(4):
        copies[2 * chunk].wait()
        copies[2 * chunk + 1].wait()
        grads = dot_nt(rows_of(table, all_ref, 2 * chunk), weight).astype(bf16)
        set_rows(table, grad_ref, 2 * chunk, grads)


def mixed_back(table, pieces, weight, rows):
    return call(
        mixed_kernel, "mixed_back",
        [((1024, 128), bf16), ((1024, D), bf16)],
        [pltpu.SemaphoreType.DMA((8,))],
        27 * 10**7, 4 * 10**6, 0, (table, *pieces, weight, rows), 1, 8,
    )


def last_kernel(
    table, query_ref, own_ref, other_ref, project_ref, normal_ref, middle_ref,
    hidden_ref, mine_part, other_part, joined_ref, extra_ref,
):
    gain = None
    for chunk in ORDER:
        own = rows_of(table, own_ref, 2 * chunk)
        other = rows_of(table, other_ref, 2 * chunk).astype(f32)
        joined = jnp.concatenate(
            [rows_of(table, query_ref, 2 * chunk), (own + other).astype(bf16)], axis=1
        )
        set_rows(table, joined_ref, 2 * chunk, joined)
        bias = jnp.sum(joined.astype(f32), axis=0, keepdims=True)
        biases = bias if chunk == ORDER[0] else biases + bias
        value = dot_nt(joined, project_ref[...])
        put_parts(mine_part, other_part, chunk, value)
        normal = rows_of(table, normal_ref, 2 * chunk).astype(f32)
        tilted = jnp.sum(value * normal, axis=0, keepdims=True)
        plain = jnp.sum(value, axis=0, keepdims=True)
        gain = tilted if gain is None else gain + tilted
        offset = plain if chunk == ORDER[0] else offset + plain
    pairs = [
        (gain, offset), (middle_ref[0:1, :], middle_ref[1:2, :]),
        (middle_ref[2:3, :], middle_ref[3:4, :]),
    ]
    extra_rows(extra_ref, slice(0, 128), pairs, [biases[:, 0:128], biases[:, 256:384]])
    lines = [hidden_ref[0:1, 128 * g : 128 * g + 128] for g in range(4)]
    extra_rows(extra_ref, slice(128, 256), [], lines)


def last_parts(table, query, own, other, project, normal, sums, hidden):
    return call(
        last_kernel, "last_parts", PARTS + [((1024, 384), bf16), ((1024, 256), bf16)], [],
        8 * 10**8, 7 * 10**6, 0, (table, query, own, other, project, normal, sums, hidden), 1,
    )


def join_kernel(mine_ref, core_ref, here_ref, near_ref, far_ref, back_ref):
    for d, ref in enumerate((here_ref, near_ref, far_ref, back_ref)):
        ref[...] = (mine_ref[d] + core_ref[d].astype(f32)).astype(ref.dtype)


def join(mine, core):
    return call(
        join_kernel, "join", [((ROWS, D), f32)] + [((ROWS, D), bf16)] * 3, [], 10**6, 4 * 10**6, 0,
        (mine, core),
    )


def landed(refs):
    here, near, far, back = [ref[...].astype(f32) for ref in refs]
    return here + near + far + back


def middle_kernel(*refs):
    input_ref, vector_ref, mid_ref, normal_ref, inverse_ref, normed_ref = refs[4:10]
    mid = input_ref[...].astype(f32) + (landed(refs[0:4]) + vector_ref[2:3, :])
    normal, inverse = normalize(mid)
    mid_ref[...] = mid
    normal_ref[...] = normal
    inverse_ref[...] = inverse
    normed_ref[...] = (normal * vector_ref[3:4, :] + vector_ref[4:5, :]).astype(bf16)


def middle(ends, inputs, vectors):
    return call(
        middle_kernel, "middle",
        [((ROWS, D), f32), ((ROWS, D), f32), ((ROWS, 1), f32), ((ROWS, D), bf16)], [],
        10**6, 3 * 10**6, 0, (*ends, inputs, vectors),
    )


def middle_back_kernel(*refs):
    cotangent_ref, vector_ref, normal_ref, inverse_ref, grad_ref, branch_ref, sum_ref = refs[4:11]
    second = landed(refs[0:4])
    normal = normal_ref[...]
    cotangent = cotangent_ref[...].astype(f32)
    grad = cotangent + norm_back(second, vector_ref[3:4, :], normal, inverse_ref[...])
    grad_ref[...] = grad
    branch = grad.astype(bf16)
    branch_ref[...] = branch
    sum_ref[0:1, :] = jnp.sum(second * normal, axis=0, keepdims=True)
    sum_ref[1:2, :] = jnp.sum(second, axis=0, keepdims=True)
    sum_ref[2:3, :] = jnp.sum(branch.astype(f32), axis=0, keepdims=True)
    sum_ref[3:4, :] = jnp.sum(cotangent, axis=0, keepdims=True)


def middle_back(ends, cotangent, vectors, normal, inverse):
    return call(
        middle_back_kernel, "middle_back",
        [((ROWS, D), f32), ((ROWS, D), bf16), ((8, D), f32)], [],
        10**6, 3 * 10**6, 0, (*ends, cotangent, vectors, normal, inverse),
    )


def block_kernel(*refs):
    mid_ref, vector_ref, out_ref = refs[4:7]
    out_ref[...] = (mid_ref[...] + landed(refs[0:4]) + vector_ref[5:6, :]).astype(bf16)


def block_end(ends, mid, vectors):
    return call(
        block_kernel, "block_end", [((ROWS, D), bf16)], [], 10**6, 2 * 10**6, 0,
        (*ends, mid, vectors),
    )[0]


def input_kernel(*refs):
    input_ref, vector_ref, grad_ref, out_ref = refs[4:8]
    normal, inverse = normalize(input_ref[...].astype(f32))
    out_ref[...] = grad_ref[...] + norm_back(
        landed(refs[0:4]), vector_ref[0:1, :], normal, inverse
    )


def input_end(ends, inputs, vectors, grad):
    return call(
        input_kernel, "input_end", [((ROWS, D), f32)], [], 10**6, 3 * 10**6, 0,
        (*ends, inputs, vectors, grad),
    )[0]


def over_seq(ref, shard, columns):
    value = ref[8 * shard, :, columns].astype(f32)
    for q in range(1, 8):
        value = value + ref[8 * shard + q, :, columns].astype(f32)
    return value


def early_kernel(rows_ref, up_ref, total_ref):
    rows = rows_ref[0].astype(f32)
    for q in range(1, 8):
        rows = rows + rows_ref[q].astype(f32)
    ups = [over_seq(up_ref, shard, slice(0, 512)) for shard in range(16)]
    pieces = [rows]
    for block in range(4):
        pieces.append(
            jnp.concatenate(
                [
                    ups[shard][:, 0:256] + ups[shard ^ 2][:, 256:512]
                    for shard in range(4 * block, 4 * block + 4)
                ],
                axis=1,
            )
        )
    pieces.append(jnp.zeros((8, D), f32))
    total_ref[...] = jnp.concatenate(pieces, axis=0).astype(bf16)


def early_totals(rows, up):
    return call(
        early_kernel, "early_totals", [((80, D), bf16)], [], 10**6, 4 * 10**6, 0, (rows, up)
    )[0]


def late_kernel(whose, last_ref, total_ref, small_ref, last_small):
    lasts = []
    for shard in range(16):
        last_small[shard] = over_seq(last_ref, shard, slice(384, 640))
        lasts.append(over_seq(last_ref, shard, slice(0, 384)))
    pieces = []
    for kind in range(3):
        start = 128 * kind
        pieces.append(
            jnp.concatenate(
                [
                    lasts[shard][:, start : start + 64]
                    + lasts[shard ^ 2][:, start + 64 : start + 128]
                    for shard in range(16)
                ],
                axis=1,
            )
        )
    pieces.append(jnp.zeros((8, D), f32))
    total = jnp.concatenate(pieces, axis=0).astype(bf16)
    for q in range(8):
        total_ref[q] = total
    last_sum = last_small[0]
    for shard in range(1, 16):
        last_sum = last_sum + last_small[shard]
    mine, twin = last_small[whose[0]], last_small[whose[0] ^ 2]
    small_ref[0:3, :] = last_sum[0:3]
    small_ref[3:4, 0:128] = jnp.concatenate(
        [mine[3:4, 0:64] + twin[3:4, 64:128], mine[4:5, 0:64] + twin[4:5, 64:128]], axis=1
    )
    small_ref[4:5, :] = jnp.concatenate(
        [mine[0:1, 128:256] + twin[2:3, 128:256], mine[1:2, 128:256] + twin[3:4, 128:256]], axis=1
    )


def late_totals(whose, last):
    return call(
        late_kernel, "late_totals", [((8, 32, D), bf16), ((8, 256), f32)],
        [((16, 8, 256), f32)], 10**6, 2 * 10**6, 0, (whose, last), 1,
    )


def early_out_kernel(order, *refs):
    output_ref, down_ref, up_ref = refs[4:7]
    for k in range(4):
        for e in range(2):
            q = order[2 * k + e]
            total = refs[k][80 * e : 80 * e + 80, :].astype(f32)
            eight = pl.multiple_of(8 * q, 8)
            output_ref[pl.ds(eight, 8), :] = total[0:8]
            down_ref[pl.ds(pl.multiple_of(32 * q, 32), 32), :] = total[8:40]
            for block in range(4):
                up_ref[pl.ds(eight, 8), D * block : D * block + D] = total[
                    40 + 8 * block : 48 + 8 * block
                ]


def early_out(order, pieces):
    return call(
        early_out_kernel, "early_out", [((64, D), f32), ((256, D), f32), ((64, FF), f32)], [],
        10**6, 4 * 10**6, 0, (order, *pieces), 1,
    )


def late_out_kernel(total_ref, attention_ref):
    for q in range(8):
        total = total_ref[q].astype(f32)
        for kind in range(3):
            attention_ref[8 * q : 8 * q + 8, D * kind : D * kind + D] = total[
                8 * kind : 8 * kind + 8
            ]


def late_out(total):
    return call(
        late_out_kernel, "late_out", [((64, 3 * D), f32)], [], 10**6, 10**6, 0, (total,)
    )[0]


def shift(value, axis, step):
    size = lax.axis_size(axis)
    return lax.ppermute(value, axis, [(i, (i + step) % size) for i in range(size)])


def gather(own, *first):
    mine = [shift(own, "y", -step) for step in (1, 2, 3)]
    if first:
        mine = list(lax.optimization_barrier((*mine, *first))[0:3])
    mine = [own, *mine]
    return mine + [shift(block, "c", 1) for block in mine]


def joined(mine, other, *first):
    core = shift(other, "c", 1)
    return join(mine, after(core, *first) if first else core)


def spread(here, near, far, back):
    return here, shift(near, "y", 1), shift(far, "y", 2), shift(back, "y", 3)


def scatter(mine, other, *first):
    return spread(*joined(mine, other, *first))


def exchange(value, axes):
    return lax.all_to_all(value, axes, split_axis=0, concat_axis=0, tiled=True)


def after(value, *others):
    return lax.optimization_barrier((value, *others))[0]


def normalize(values):
    centre = jnp.mean(values, axis=-1, keepdims=True)
    centred = values - centre
    spread = jnp.mean(centred * centred, axis=-1, keepdims=True)
    inverse = lax.rsqrt(spread + epsilon)
    return centred * inverse, inverse


def norm_back(grad, gain, normal, inverse):
    scaled = grad * gain
    return inverse * (
        scaled
        - jnp.mean(scaled, axis=-1, keepdims=True)
        - normal * jnp.mean(scaled * normal, axis=-1, keepdims=True)
    )


def on_device(
    block_input,
    first_gain,
    first_shift,
    attention_weight,
    query_bias,
    value_bias,
    output_weight,
    output_bias,
    second_gain,
    second_shift,
    upward_weight,
    upward_bias,
    downward_weight,
    downward_bias,
    cotangent,
):
    y = lax.axis_index("y")
    xh = lax.axis_index("xh")
    c = lax.axis_index("c")
    shard = 4 * y + 2 * xh + c
    piece = np.arange(8)
    table = (2 * ((y + piece % 4) % 4) + (c ^ (piece // 4))).astype(jnp.int32)
    half = xh[None].astype(jnp.int32)
    whose = shard[None].astype(jnp.int32)
    slopes = jnp.exp2(-8.0 * (jnp.stack([shard, shard ^ 2]) + 1).astype(f32) / HEADS)

    with jax.named_scope("weights_attention"):
        vectors_own = [
            first_gain, first_shift, output_bias, second_gain, second_shift, downward_bias
        ]
        small = sum(
            jnp.pad(item[None], ((0, 15), (64 * g, 320 - 64 * g)))
            for g, item in enumerate(vectors_own)
        )
        small = small + jnp.pad(query_bias[None], ((1, 14), (0, 320)))
        small = small + jnp.pad(value_bias[None], ((1, 14), (64, 256)))
        small = small + jnp.pad(upward_bias[None], ((1, 14), (128, 0)))
        payload, up_payload = call(
            deal_kernel, "deal", [((16, 80, 384), bf16), ((16, 64, 512), bf16)], [],
            0, 4 * 10**6, 0, (attention_weight, small, upward_weight),
        )
        arrived = exchange(payload, FSDP)

    with jax.named_scope("first"):
        inputs = gather(block_input)
        heads_own, heads_send, normed_first, normal_first, project, vectors, bias_up = (
            first_heads(table, whose, inputs, arrived)
        )
        query = queries(normed_first, project, bias_up)
        heads_arrived = shift(heads_send, "xh", 1)
        cotangents = gather(after(cotangent, heads_send))
    with jax.named_scope("weights_upward"):
        upward_pair = exchange(after(up_payload, arrived), FSDP).reshape(D, 512)
    with jax.named_scope("weights_pair"):
        output_rows = shift(after(output_weight, arrived), "xh", 1)
        downward_rows = shift(after(downward_weight, heads_arrived), "xh", 1)
    with jax.named_scope("attention"):
        mixed, lse = attention_forward(half, slopes, query, heads_own, heads_arrived)
    with jax.named_scope("output"):
        mixed = after(mixed, upward_pair, *cotangents)
        mine, other = output_parts(table, mixed, output_weight, output_rows)
        residual_mid, normal_second, inverse_second, normed_second = middle(
            scatter(mine, other), block_input, vectors
        )

    with jax.named_scope("feed"):
        mine, other, activated, upward_grad, seconds, all_cotangents, hidden_sums = feed_parts(
            table, gather(normed_second), cotangents, upward_pair, downward_weight,
            downward_rows, bias_up,
        )
        sums_near = joined(mine, other)
        ends = spread(*sums_near)

    with jax.named_scope("upward_gradients"):
        late_grad, late_act = lax.optimization_barrier((upward_grad, activated, sums_near[0]))[0:2]
        upward_weight_grad = dot_tn(seconds, late_grad).astype(bf16)
        downward_grad = dot_tn(late_act, all_cotangents)
        downward_other = downward_grad[256:].astype(bf16)
        out_mine, out_other = out_parts(table, late_act, downward_weight, downward_rows)
    with jax.named_scope("feed"):
        ends = lax.optimization_barrier(
            (*ends, upward_weight_grad, downward_other, out_mine)
        )[0:4]
        mid_grad, branch_grad, sums = middle_back(
            ends, cotangent, vectors, normal_second, inverse_second
        )

    with jax.named_scope("upward_gradients"):
        shares = after(upward_weight_grad, branch_grad).reshape(128, 8, 512)
    with jax.named_scope("mixed_back"):
        mixed_grad, branch_grads = mixed_back(
            table, gather(branch_grad, shares), output_weight, output_rows
        )
        output_grad = dot_tn(mixed, branch_grads)
        output_other = output_grad[64:].astype(bf16)
        mixed_grad = after(mixed_grad, output_other)
    with jax.named_scope("upward_sums"):
        arrived_up = exchange(shares, FSDP + SEQ)
    with jax.named_scope("attention_back"):
        output_arrived = shift(output_other, "xh", 1)
        query_grad, back_own, back_send = attention_backward(
            half, slopes, query, heads_own, heads_arrived, mixed_grad, lse
        )
        back_send = after(back_send, arrived_up)
        back_arrived = shift(back_send, "xh", 1)
    with jax.named_scope("feed_out"):
        out_near = joined(out_mine, after(out_other, back_send))
        out_ends = spread(*out_near)
        block_output = block_end(out_ends, residual_mid, vectors)
    with jax.named_scope("row_gradients"):
        downward_arrived = shift(after(downward_other, branch_grad), "xh", 1)
        downward_sum = (downward_grad[:256] + downward_arrived.astype(f32)).astype(bf16)
        output_sum = (output_grad[:64] + output_arrived.astype(f32)).astype(bf16)
        rows_sent = jnp.concatenate(
            [output_sum.reshape(8, 8, D), downward_sum.reshape(8, 32, D)], axis=1
        )
        rows_all = exchange(after(rows_sent, arrived_up), SEQ)
    with jax.named_scope("first_back"):
        back_arrived = after(back_arrived, out_near[0])
        mine, other, head_grads, last_extra = last_parts(
            table, query_grad, back_own, back_arrived, project, normal_first, sums, hidden_sums
        )
        last_near = joined(mine, other)
        ends = spread(*last_near)
        input_gradient = input_end(ends, block_input, vectors, mid_grad)
    with jax.named_scope("attention_gradients"):
        weight_grad = dot_tn(normed_first, head_grads).astype(bf16)
        shares = jnp.concatenate([weight_grad, last_extra], axis=-1).reshape(128, 8, 640)
        shares = after(shares, rows_all, *out_ends[1:4])
        arrived_last = exchange(shares, FSDP + SEQ)
    with jax.named_scope("early_totals"):
        early = early_totals(after(rows_all, shares), arrived_up)
        early_pair = jnp.concatenate([early, shift(early, "xl", 1)], axis=0)
        early_all = [early_pair] + [shift(early_pair, "z", -step) for step in (1, 2, 3)]
        z = lax.axis_index("z")
        xl = lax.axis_index("xl")
        order = (2 * ((z + piece // 2) % 4) + (xl ^ (piece % 2))).astype(jnp.int32)
        output_weight_gradient, downward_weight_gradient, upward_weight_gradient = early_out(
            order, early_all
        )
    with jax.named_scope("late_totals"):
        late, late_small = late_totals(
            whose, after(arrived_last, input_gradient, early_pair)
        )
        attention_weight_gradient = late_out(exchange(late, SEQ))

    return (
        block_output,
        input_gradient,
        late_small[0, 0:64],
        late_small[0, 64:128],
        attention_weight_gradient,
        late_small[3, 0:64],
        late_small[3, 64:128],
        output_weight_gradient,
        late_small[2, 0:64],
        late_small[1, 0:64],
        late_small[1, 64:128],
        upward_weight_gradient,
        late_small[4],
        downward_weight_gradient,
        late_small[2, 64:128],
    )


def solution(mesh):
    grid = Mesh(mesh.devices.reshape(4, 2, 4, 2, 2), ALL)
    tokens = P(ALL, None)
    rows = P(FSDP, None)
    line = P(FSDP)
    return jax.shard_map(
        on_device,
        mesh=grid,
        in_specs=(
            tokens, line, line, rows, line, line, rows, line, line, line, rows, line, rows, line,
            tokens,
        ),
        out_specs=(
            tokens, tokens, line, line, rows, line, line, rows, line, line, line, rows, line, rows,
            line,
        ),
        check_vma=False,
    )
```

```python
import jax
import jax.numpy as jnp
import numpy as np
from jax import lax
from jax.experimental import pallas as pl
from jax.experimental.pallas import tpu as pltpu
from jax.sharding import Mesh
from jax.sharding import PartitionSpec as P

D = 1024
HEADS = 16
HEAD = 64
FF = 4096

epsilon = 1e-05
score_scale = 0.125
bf16 = jnp.bfloat16
f32 = jnp.float32

SEQ = ("z", "xl")
FSDP = ("y", "xh", "c")
ALL = SEQ + FSDP
ROWS = 128
TILE = 256
TILES = 8
LENGTH = TILE * TILES

NT = (((1,), (1,)), ((), ()))


def dot(a, b):
    return jnp.dot(a, b, preferred_element_type=f32)


def dot_nt(a, b):
    return lax.dot_general(a, b, NT, preferred_element_type=f32)


def dot_tn(a, b):
    return lax.dot_general(a, b, (((0,), (0,)), ((), ())), preferred_element_type=f32)


smem = pl.BlockSpec(memory_space=pltpu.SMEM)
vmem = pl.BlockSpec(memory_space=pltpu.VMEM)


def call(kernel, name, outs, scratch, flops, moved, transcendentals, args, scalars=0, pieces=0):
    rest = len(args) - scalars - pieces
    return pl.pallas_call(
        kernel,
        out_shape=tuple(jax.ShapeDtypeStruct(shape, kind) for shape, kind in outs),
        in_specs=[smem] * scalars + [pl.BlockSpec(memory_space=pl.ANY)] * pieces + [vmem] * rest,
        out_specs=(vmem,) * len(outs),
        scratch_shapes=[
            pltpu.VMEM(*item) if isinstance(item, tuple) else item for item in scratch
        ],
        compiler_params=pltpu.CompilerParams(vmem_limit_bytes=60 * 2**20),
        cost_estimate=pl.CostEstimate(
            flops=flops, bytes_accessed=moved, transcendentals=transcendentals
        ),
        name=name,
    )(*args)


def first_row(table, p):
    return pl.multiple_of(table[p] * ROWS, ROWS)


def assemble(table, refs, out, sems):
    copies = [
        pltpu.make_async_copy(refs[p], out.at[pl.ds(first_row(table, p), ROWS), :], sems.at[p])
        for p in range(8)
    ]
    for copy in copies:
        copy.start()
    return copies


def rows_of(table, ref, p):
    return jnp.concatenate(
        [ref[pl.ds(first_row(table, p + b), ROWS), :] for b in range(2)], axis=0
    )


def set_rows(table, ref, p, value):
    for b in range(2):
        ref[pl.ds(first_row(table, p + b), ROWS), :] = value[b * ROWS : (b + 1) * ROWS]


def put_parts(mine_ref, other_ref, chunk, value):
    ref = mine_ref if chunk < 2 else other_ref
    for b in range(2):
        ref[2 * (chunk % 2) + b] = value[b * ROWS : (b + 1) * ROWS].astype(ref.dtype)


PARTS = [((4, ROWS, D), bf16), ((4, ROWS, D), bf16)]
ORDER = (2, 3, 0, 1)


def extra_rows(out_ref, lanes, pairs, lines):
    row = lax.broadcasted_iota(jnp.int32, (64, 128), 0) % 8
    for shard in range(16):
        columns = slice(64 * shard, 64 * shard + 64)
        block = jnp.zeros((64, 128), f32)
        for r, (left, right) in enumerate(pairs):
            line = jnp.concatenate([left[:, columns], right[:, columns]], axis=1)
            block = jnp.where(row == r, line, block)
        for r, line in enumerate(lines):
            block = jnp.where(row == len(pairs) + r, line, block)
        out_ref[64 * shard : 64 * shard + 64, lanes] = block.astype(bf16)


def deal_kernel(weight_ref, small_ref, up_ref, out_ref, up_out):
    small = small_ref[...]

    def piece(kind, head):
        start = kind * D + head * HEAD
        return weight_ref[:, start : start + HEAD]

    for y in range(4):
        for x in range(2):
            for c in range(2):
                shard = 4 * y + 2 * x + c
                twin = shard ^ 2
                out_ref[shard, 0:64, :] = jnp.concatenate(
                    [
                        piece(kind, head) for kind in range(3) for head in (shard, twin)
                    ],
                    axis=1,
                )
                out_ref[shard, 64:80, :] = small
                up_out[shard, :, 0:256] = up_ref[:, 256 * shard : 256 * shard + 256]
                up_out[shard, :, 256:512] = up_ref[:, 256 * twin : 256 * twin + 256]


def swap(pairs):
    return jnp.concatenate(
        [pairs[:, 64:128], pairs[:, 0:64], pairs[:, 192:256], pairs[:, 128:192]], axis=1
    )


def first_kernel(table, shard_ref, *refs):
    pieces, arrived = refs[0:8], refs[8]
    kv_ref, send_ref, normed_ref, normal_ref, project_ref, vector_ref, bias_ref = refs[9:16]
    inputs, sems = refs[16:18]
    copies = assemble(table, pieces, inputs, sems)
    for r in range(16):
        project_ref[64 * r : 64 * r + 64, :] = arrived[r, 0:64, :]
    rows = [arrived[r, 64:80, :].astype(f32) for r in range(16)]
    for g in range(6):
        vector_ref[g : g + 1, :] = jnp.concatenate(
            [rows[r][0:1, 64 * g : 64 * g + 64] for r in range(16)], axis=1
        )
    shard = shard_ref[0]
    mine = arrived[shard, 64:80, :].astype(f32)[1:2]
    twin = arrived[shard ^ 2, 64:80, :].astype(f32)[1:2]
    bias_ref[0:1, :] = jnp.concatenate([mine[:, 128:], twin[:, 128:]], axis=1)
    bias_ref[1:2, 0:128] = jnp.concatenate([mine[:, 0:64], twin[:, 0:64]], axis=1)
    bias = jnp.concatenate(
        [jnp.zeros((1, 2 * HEAD), f32), mine[:, 64:128], twin[:, 64:128]], axis=1
    )
    gain = vector_ref[0:1, :]
    offset = vector_ref[1:2, :]
    for copy in copies:
        copy.wait()
    for chunk in range(4):
        rows = slice(chunk * TILE, (chunk + 1) * TILE)
        normal, unused = normalize(inputs[rows, :].astype(f32))
        normal_ref[rows, :] = normal.astype(bf16)
        normed = (normal * gain + offset).astype(bf16)
        normed_ref[rows, :] = normed
        heads = (dot(normed, project_ref[:, 128:384]) + bias).astype(bf16)
        kv_ref[rows, :] = heads
        send_ref[rows, :] = swap(heads)


def query_kernel(normed_ref, project_ref, bias_ref, query_ref):
    bias = bias_ref[1:2, 0:128]
    for chunk in range(4):
        rows = slice(chunk * TILE, (chunk + 1) * TILE)
        value = dot(normed_ref[rows, :], project_ref[:, 0:128]) + bias
        query_ref[rows, :] = value.astype(bf16)


def queries(normed, project, bias):
    return call(
        query_kernel, "queries", [((1024, 128), bf16)], [], 27 * 10**7, 3 * 10**6, 0,
        (normed, project, bias),
    )[0]


def first_heads(table, shard, pieces, arrived):
    return call(
        first_kernel, "first_heads",
        [
            ((1024, 256), bf16), ((1024, 256), bf16), ((1024, D), bf16), ((1024, D), bf16),
            ((D, 384), bf16), ((8, D), f32), ((8, 512), f32),
        ],
        [((1024, D), bf16), pltpu.SemaphoreType.DMA((8,))],
        8 * 10**8, 10**7, 10**4, (table, shard, *pieces, arrived), 2, 8,
    )


def in_head(shape, head):
    lane = lax.broadcasted_iota(jnp.int32, shape, 1)
    return (lane < HEAD) if head == 0 else (lane >= HEAD)


def stage_queries(query, head):
    lane = lax.broadcasted_iota(jnp.int32, query.shape, 1) - (HEAD if head == 0 else 0)
    ones = jnp.where((lane >= 0) & (lane < 3), 1.0, 0.0)
    scaled = query.astype(f32) * score_scale
    return jnp.where(in_head(query.shape, head), scaled, ones).astype(bf16)


def stage_keys(key, head, slope, first):
    shape = key.shape
    lane = lax.broadcasted_iota(jnp.int32, shape, 1) - (HEAD if head == 0 else 0)
    row = lax.broadcasted_iota(jnp.int32, shape, 0)
    place = slope * (row + first).astype(f32)
    high = place.astype(bf16).astype(f32)
    rest = place - high
    middle = rest.astype(bf16).astype(f32)
    low = rest - middle
    extra = jnp.where(
        lane == 0, high, jnp.where(lane == 1, middle, jnp.where(lane == 2, low, 0.0))
    )
    return jnp.where(in_head(shape, head), key.astype(f32), extra).astype(bf16)


def fold(tile, op):
    parts = [tile[8 * g : 8 * g + 8] for g in range(TILE // 8)]
    while len(parts) > 1:
        parts = [op(parts[2 * g], parts[2 * g + 1]) for g in range(len(parts) // 2)]
    return parts[0]


def future():
    key = lax.broadcasted_iota(jnp.int32, (TILE, TILE), 0)
    query = lax.broadcasted_iota(jnp.int32, (TILE, TILE), 1)
    return key > query


def tile_rows(t):
    return slice(t * TILE, (t + 1) * TILE)


def stage(half, slopes, own_ref, other_ref, ka, emit_rest):
    for t in range(4):
        for side, ref in enumerate((own_ref, other_ref)):
            slot = tile_rows(2 * t + side)
            pair = ref[tile_rows(t), :]
            first = TILE * (2 * t + (half[0] if side == 0 else 1 - half[0])) - LENGTH // 2
            for head in range(2):
                ka[head, slot, :] = stage_keys(pair[:, 0:128], head, slopes[head], first)
            emit_rest(slot, pair)


def masked(s, t, slot, hidden, ahead):
    if slot == 2 * t:
        return jnp.where(hidden, -1e30, s)
    return s + ahead if slot == 2 * t + 1 else s


def forward_kernel(half, slopes, q_ref, own_ref, other_ref, out_ref, lse_ref, ka, vt, s_sc, p_sc):
    def rest(slot, pair):
        vt[:, slot] = pair[:, 128:256].astype(f32).T.astype(bf16)

    stage(half, slopes, own_ref, other_ref, ka, rest)
    hidden = future()
    ahead = jnp.where(half[0] == 1, 0.0, -1e30)
    for t in range(4):
        query = q_ref[tile_rows(t), :]
        n = (2 * t + 2) * TILE
        outs = []
        for head in range(2):
            q = stage_queries(query, head)
            peak = None
            for slot in range(2 * t + 2):
                rows = tile_rows(slot)
                s = masked(dot_nt(ka[head, rows, :], q), t, slot, hidden, ahead)
                s_sc[head, rows, :] = s
                top = fold(s, jnp.maximum)
                peak = top if peak is None else jnp.maximum(peak, top)
            peak = jnp.max(peak, axis=0, keepdims=True)
            total = None
            for slot in range(2 * t + 2):
                rows = tile_rows(slot)
                p = jnp.exp(s_sc[head, rows, :] - peak)
                p_sc[head, rows, :] = p.astype(bf16)
                part = fold(p, jnp.add)
                total = part if total is None else total + part
            total = jnp.sum(total, axis=0, keepdims=True)
            outs.append(dot(vt[head * HEAD : (head + 1) * HEAD, 0:n], p_sc[head, 0:n, :]) / total)
            lse_ref[2 * t + head] = peak + jnp.log(total)
        out_ref[tile_rows(t), :] = jnp.concatenate(outs, axis=0).T.astype(bf16)


def attention_forward(half, slopes, query, own, other):
    return call(
        forward_kernel, "attention_forward",
        [((1024, 128), bf16), ((8, 1, TILE), f32)],
        [
            ((2, LENGTH, 128), bf16), ((128, LENGTH), bf16), ((2, LENGTH, TILE), f32),
            ((2, LENGTH, TILE), bf16),
        ],
        3 * 10**9, 2 * 10**6, 24 * 10**5, (half, slopes, query, own, other), 2,
    )


def backward_kernel(
    half, slopes, q_ref, own_ref, other_ref, grad_ref, lse_ref,
    dq_ref, down_ref, send_ref,
    ka, kt, va, dk, dv, p_sc, dp_sc, ds_sc,
):
    def rest(slot, pair):
        va[slot, :] = pair[:, 128:256]
        kt[:, slot] = pair[:, 0:128].astype(f32).T.astype(bf16)

    stage(half, slopes, own_ref, other_ref, ka, rest)
    hidden = future()
    ahead = jnp.where(half[0] == 1, 0.0, -1e30)
    for t in range(4):
        query = q_ref[tile_rows(t), :]
        grad = grad_ref[tile_rows(t), :]
        n = (2 * t + 2) * TILE
        grads = [
            jnp.where(in_head(grad.shape, head), grad.astype(f32), 0.0).astype(bf16)
            for head in range(2)
        ]
        plain = [
            jnp.where(in_head(query.shape, head), query.astype(f32) * score_scale, 0.0).astype(bf16)
            for head in range(2)
        ]
        queries = [stage_queries(query, head) for head in range(2)]
        grad_rows = jnp.concatenate(grads, axis=0)
        plain_rows = jnp.concatenate(plain, axis=0)
        delta = [None, None]
        for slot in range(2 * t + 2):
            rows = tile_rows(slot)
            low = []
            for head in range(2):
                s = masked(dot_nt(ka[head, rows, :], queries[head]), t, slot, hidden, ahead)
                p = jnp.exp(s - lse_ref[2 * t + head])
                dp = dot_nt(va[rows, :], grads[head])
                p_sc[head, rows, :] = p
                dp_sc[head, rows, :] = dp
                part = fold(p * dp, jnp.add)
                delta[head] = part if delta[head] is None else delta[head] + part
                low.append(p.astype(bf16))
            value = dot(jnp.concatenate(low, axis=1), grad_rows)
            dv[rows, :] = value if slot >= 2 * t else dv[rows, :] + value
        delta = [jnp.sum(item, axis=0, keepdims=True) for item in delta]
        for slot in range(2 * t + 2):
            rows = tile_rows(slot)
            low = []
            for head in range(2):
                ds = (p_sc[head, rows, :] * (dp_sc[head, rows, :] - delta[head])).astype(bf16)
                ds_sc[head, rows, :] = ds
                low.append(ds)
            key = dot(jnp.concatenate(low, axis=1), plain_rows)
            dk[rows, :] = key if slot >= 2 * t else dk[rows, :] + key
        outs = [
            dot(kt[head * HEAD : (head + 1) * HEAD, 0:n], ds_sc[head, 0:n, :]) for head in range(2)
        ]
        dq_ref[tile_rows(t), :] = (jnp.concatenate(outs, axis=0) * score_scale).T.astype(bf16)
    for t in range(4):
        rows = tile_rows(t)
        down_ref[rows, 0:128] = dk[tile_rows(2 * t), :]
        down_ref[rows, 128:256] = dv[tile_rows(2 * t), :]
        pair = jnp.concatenate([dk[tile_rows(2 * t + 1), :], dv[tile_rows(2 * t + 1), :]], axis=1)
        send_ref[rows, :] = swap(pair.astype(bf16))


def attention_backward(half, slopes, query, own, other, grad, lse):
    return call(
        backward_kernel, "attention_backward",
        [((1024, 128), bf16), ((1024, 256), f32), ((1024, 256), bf16)],
        [
            ((2, LENGTH, 128), bf16), ((128, LENGTH), bf16), ((LENGTH, 128), bf16),
            ((LENGTH, 128), f32), ((LENGTH, 128), f32), ((2, LENGTH, TILE), f32),
            ((2, LENGTH, TILE), f32), ((2, LENGTH, TILE), bf16),
        ],
        3 * 10**9, 3 * 10**6, 24 * 10**5, (half, slopes, query, own, other, grad, lse), 2,
    )


def output_kernel(table, mixed_ref, weight_ref, rows_ref, mine_part, other_part):
    weight = jnp.concatenate([weight_ref[...], rows_ref[...]], axis=0)
    for chunk in ORDER:
        put_parts(mine_part, other_part, chunk, dot(rows_of(table, mixed_ref, 2 * chunk), weight))


def output_parts(table, mixed, weight, rows):
    return call(
        output_kernel, "output_parts", PARTS, [], 27 * 10**7, 4 * 10**6, 0,
        (table, mixed, weight, rows), 1,
    )


def feed_kernel(table, *refs):
    up_ref, down_ref, rows_ref, bias_ref = refs[16:20]
    mine_part, other_part, act_ref, grad_ref, second_ref, cotangent_ref, sum_ref = refs[20:27]
    sems, more = refs[27:29]
    copies = assemble(table, refs[0:8], second_ref, sems)
    cotangent_copies = assemble(table, refs[8:16], cotangent_ref, more)
    bias = bias_ref[0:1, :]
    for chunk in ORDER:
        cotangent_copies[2 * chunk].wait()
        cotangent_copies[2 * chunk + 1].wait()
        cotangents = rows_of(table, cotangent_ref, 2 * chunk)
        back = jnp.concatenate(
            [dot_nt(cotangents, down_ref[...]), dot_nt(cotangents, rows_ref[...])], axis=1
        )
        copies[2 * chunk].wait()
        copies[2 * chunk + 1].wait()
        up = dot(rows_of(table, second_ref, 2 * chunk), up_ref[...]) + bias
        square = up * up
        bend = jnp.tanh(0.7978845608028654 * (up + 0.044715 * square * up))
        half = 0.5 * (1.0 + bend)
        set_rows(table, act_ref, 2 * chunk, (up * half).astype(bf16))
        slope = half + 0.5 * up * (1.0 - bend * bend) * (
            0.7978845608028654 * (1.0 + 0.134145 * square)
        )
        grad = (back * slope).astype(bf16)
        set_rows(table, grad_ref, 2 * chunk, grad)
        part = jnp.sum(grad.astype(f32), axis=0, keepdims=True)
        total = part if chunk == ORDER[0] else total + part
        put_parts(mine_part, other_part, chunk, dot_nt(grad, up_ref[...]))
    sum_ref[0:1, :] = total


def feed_parts(table, pieces, cotangents, up, down, rows, bias):
    return call(
        feed_kernel, "feed_parts", PARTS + [((1024, 512), bf16)] * 2 + [((1024, D), bf16)] * 2 + [((8, 512), f32)],
        [pltpu.SemaphoreType.DMA((8,)), pltpu.SemaphoreType.DMA((8,))],
        32 * 10**8, 2 * 10**7, 5 * 10**5, (table, *pieces, *cotangents, up, down, rows, bias), 1,
        16,
    )


def out_kernel(table, act_ref, down_ref, rows_ref, mine_part, other_part):
    for chunk in ORDER:
        act = rows_of(table, act_ref, 2 * chunk)
        value = dot(act[:, 0:256], down_ref[...]) + dot(act[:, 256:512], rows_ref[...])
        put_parts(mine_part, other_part, chunk, value)


def out_parts(table, act, down, rows):
    return call(
        out_kernel, "out_parts", PARTS, [], 11 * 10**8, 5 * 10**6, 0, (table, act, down, rows), 1
    )


def mixed_kernel(table, *refs):
    pieces, weight_ref, rows_ref = refs[0:8], refs[8], refs[9]
    grad_ref, all_ref, sems = refs[10:13]
    copies = assemble(table, pieces, all_ref, sems)
    weight = jnp.concatenate([weight_ref[...], rows_ref[...]], axis=0)
    for chunk in range(4):
        copies[2 * chunk].wait()
        copies[2 * chunk + 1].wait()
        grads = dot_nt(rows_of(table, all_ref, 2 * chunk), weight).astype(bf16)
        set_rows(table, grad_ref, 2 * chunk, grads)


def mixed_back(table, pieces, weight, rows):
    return call(
        mixed_kernel, "mixed_back",
        [((1024, 128), bf16), ((1024, D), bf16)],
        [pltpu.SemaphoreType.DMA((8,))],
        27 * 10**7, 4 * 10**6, 0, (table, *pieces, weight, rows), 1, 8,
    )


def last_kernel(
    table, query_ref, own_ref, other_ref, project_ref, normal_ref, middle_ref,
    hidden_ref, mine_part, other_part, joined_ref, extra_ref,
):
    gain = None
    for chunk in ORDER:
        own = rows_of(table, own_ref, 2 * chunk)
        other = rows_of(table, other_ref, 2 * chunk).astype(f32)
        joined = jnp.concatenate(
            [rows_of(table, query_ref, 2 * chunk), (own + other).astype(bf16)], axis=1
        )
        set_rows(table, joined_ref, 2 * chunk, joined)
        bias = jnp.sum(joined.astype(f32), axis=0, keepdims=True)
        biases = bias if chunk == ORDER[0] else biases + bias
        value = dot_nt(joined, project_ref[...])
        put_parts(mine_part, other_part, chunk, value)
        normal = rows_of(table, normal_ref, 2 * chunk).astype(f32)
        tilted = jnp.sum(value * normal, axis=0, keepdims=True)
        plain = jnp.sum(value, axis=0, keepdims=True)
        gain = tilted if gain is None else gain + tilted
        offset = plain if chunk == ORDER[0] else offset + plain
    pairs = [
        (gain, offset), (middle_ref[0:1, :], middle_ref[1:2, :]),
        (middle_ref[2:3, :], middle_ref[3:4, :]),
    ]
    extra_rows(extra_ref, slice(0, 128), pairs, [biases[:, 0:128], biases[:, 256:384]])
    lines = [hidden_ref[0:1, 128 * g : 128 * g + 128] for g in range(4)]
    extra_rows(extra_ref, slice(128, 256), [], lines)


def last_parts(table, query, own, other, project, normal, sums, hidden):
    return call(
        last_kernel, "last_parts", PARTS + [((1024, 384), bf16), ((1024, 256), bf16)], [],
        8 * 10**8, 7 * 10**6, 0, (table, query, own, other, project, normal, sums, hidden), 1,
    )


def join_kernel(mine_ref, core_ref, here_ref, near_ref, far_ref, back_ref):
    for d, ref in enumerate((here_ref, near_ref, far_ref, back_ref)):
        ref[...] = (mine_ref[d] + core_ref[d].astype(f32)).astype(ref.dtype)


def join(mine, core):
    return call(
        join_kernel, "join", [((ROWS, D), f32)] + [((ROWS, D), bf16)] * 3, [], 10**6, 4 * 10**6, 0,
        (mine, core),
    )


def landed(refs):
    here, near, far, back = [ref[...].astype(f32) for ref in refs]
    return here + near + far + back


def middle_kernel(*refs):
    input_ref, vector_ref, mid_ref, normal_ref, inverse_ref, normed_ref = refs[4:10]
    mid = input_ref[...].astype(f32) + (landed(refs[0:4]) + vector_ref[2:3, :])
    normal, inverse = normalize(mid)
    mid_ref[...] = mid
    normal_ref[...] = normal
    inverse_ref[...] = inverse
    normed_ref[...] = (normal * vector_ref[3:4, :] + vector_ref[4:5, :]).astype(bf16)


def middle(ends, inputs, vectors):
    return call(
        middle_kernel, "middle",
        [((ROWS, D), f32), ((ROWS, D), f32), ((ROWS, 1), f32), ((ROWS, D), bf16)], [],
        10**6, 3 * 10**6, 0, (*ends, inputs, vectors),
    )


def middle_back_kernel(*refs):
    cotangent_ref, vector_ref, normal_ref, inverse_ref, grad_ref, branch_ref, sum_ref = refs[4:11]
    second = landed(refs[0:4])
    normal = normal_ref[...]
    cotangent = cotangent_ref[...].astype(f32)
    grad = cotangent + norm_back(second, vector_ref[3:4, :], normal, inverse_ref[...])
    grad_ref[...] = grad
    branch = grad.astype(bf16)
    branch_ref[...] = branch
    sum_ref[0:1, :] = jnp.sum(second * normal, axis=0, keepdims=True)
    sum_ref[1:2, :] = jnp.sum(second, axis=0, keepdims=True)
    sum_ref[2:3, :] = jnp.sum(branch.astype(f32), axis=0, keepdims=True)
    sum_ref[3:4, :] = jnp.sum(cotangent, axis=0, keepdims=True)


def middle_back(ends, cotangent, vectors, normal, inverse):
    return call(
        middle_back_kernel, "middle_back",
        [((ROWS, D), f32), ((ROWS, D), bf16), ((8, D), f32)], [],
        10**6, 3 * 10**6, 0, (*ends, cotangent, vectors, normal, inverse),
    )


def block_kernel(*refs):
    mid_ref, vector_ref, out_ref = refs[4:7]
    out_ref[...] = (mid_ref[...] + landed(refs[0:4]) + vector_ref[5:6, :]).astype(bf16)


def block_end(ends, mid, vectors):
    return call(
        block_kernel, "block_end", [((ROWS, D), bf16)], [], 10**6, 2 * 10**6, 0,
        (*ends, mid, vectors),
    )[0]


def input_kernel(*refs):
    input_ref, vector_ref, grad_ref, out_ref = refs[4:8]
    normal, inverse = normalize(input_ref[...].astype(f32))
    out_ref[...] = grad_ref[...] + norm_back(
        landed(refs[0:4]), vector_ref[0:1, :], normal, inverse
    )


def input_end(ends, inputs, vectors, grad):
    return call(
        input_kernel, "input_end", [((ROWS, D), f32)], [], 10**6, 3 * 10**6, 0,
        (*ends, inputs, vectors, grad),
    )[0]


def over_seq(ref, shard, columns):
    value = ref[8 * shard, :, columns].astype(f32)
    for q in range(1, 8):
        value = value + ref[8 * shard + q, :, columns].astype(f32)
    return value


def early_kernel(rows_ref, up_ref, total_ref):
    rows = rows_ref[0].astype(f32)
    for q in range(1, 8):
        rows = rows + rows_ref[q].astype(f32)
    ups = [over_seq(up_ref, shard, slice(0, 512)) for shard in range(16)]
    pieces = [rows]
    for block in range(4):
        pieces.append(
            jnp.concatenate(
                [
                    ups[shard][:, 0:256] + ups[shard ^ 2][:, 256:512]
                    for shard in range(4 * block, 4 * block + 4)
                ],
                axis=1,
            )
        )
    pieces.append(jnp.zeros((8, D), f32))
    total_ref[...] = jnp.concatenate(pieces, axis=0).astype(bf16)


def early_totals(rows, up):
    return call(
        early_kernel, "early_totals", [((80, D), bf16)], [], 10**6, 4 * 10**6, 0, (rows, up)
    )[0]


def late_kernel(whose, last_ref, total_ref, small_ref, last_small):
    lasts = []
    for shard in range(16):
        last_small[shard] = over_seq(last_ref, shard, slice(384, 640))
        lasts.append(over_seq(last_ref, shard, slice(0, 384)))
    pieces = []
    for kind in range(3):
        start = 128 * kind
        pieces.append(
            jnp.concatenate(
                [
                    lasts[shard][:, start : start + 64]
                    + lasts[shard ^ 2][:, start + 64 : start + 128]
                    for shard in range(16)
                ],
                axis=1,
            )
        )
    pieces.append(jnp.zeros((8, D), f32))
    total = jnp.concatenate(pieces, axis=0).astype(bf16)
    for q in range(8):
        total_ref[q] = total
    last_sum = last_small[0]
    for shard in range(1, 16):
        last_sum = last_sum + last_small[shard]
    mine, twin = last_small[whose[0]], last_small[whose[0] ^ 2]
    small_ref[0:3, :] = last_sum[0:3]
    small_ref[3:4, 0:128] = jnp.concatenate(
        [mine[3:4, 0:64] + twin[3:4, 64:128], mine[4:5, 0:64] + twin[4:5, 64:128]], axis=1
    )
    small_ref[4:5, :] = jnp.concatenate(
        [mine[0:1, 128:256] + twin[2:3, 128:256], mine[1:2, 128:256] + twin[3:4, 128:256]], axis=1
    )


def late_totals(whose, last):
    return call(
        late_kernel, "late_totals", [((8, 32, D), bf16), ((8, 256), f32)],
        [((16, 8, 256), f32)], 10**6, 2 * 10**6, 0, (whose, last), 1,
    )


def early_out_kernel(order, *refs):
    output_ref, down_ref, up_ref = refs[4:7]
    for k in range(4):
        for e in range(2):
            q = order[2 * k + e]
            total = refs[k][80 * e : 80 * e + 80, :].astype(f32)
            eight = pl.multiple_of(8 * q, 8)
            output_ref[pl.ds(eight, 8), :] = total[0:8]
            down_ref[pl.ds(pl.multiple_of(32 * q, 32), 32), :] = total[8:40]
            for block in range(4):
                up_ref[pl.ds(eight, 8), D * block : D * block + D] = total[
                    40 + 8 * block : 48 + 8 * block
                ]


def early_out(order, pieces):
    return call(
        early_out_kernel, "early_out", [((64, D), f32), ((256, D), f32), ((64, FF), f32)], [],
        10**6, 4 * 10**6, 0, (order, *pieces), 1,
    )


def late_out_kernel(total_ref, attention_ref):
    for q in range(8):
        total = total_ref[q].astype(f32)
        for kind in range(3):
            attention_ref[8 * q : 8 * q + 8, D * kind : D * kind + D] = total[
                8 * kind : 8 * kind + 8
            ]


def late_out(total):
    return call(
        late_out_kernel, "late_out", [((64, 3 * D), f32)], [], 10**6, 10**6, 0, (total,)
    )[0]


def shift(value, axis, step):
    size = lax.axis_size(axis)
    return lax.ppermute(value, axis, [(i, (i + step) % size) for i in range(size)])


def gather(own, *first):
    mine = [shift(own, "y", -step) for step in (1, 2, 3)]
    if first:
        mine = list(lax.optimization_barrier((*mine, *first))[0:3])
    mine = [own, *mine]
    return mine + [shift(block, "c", 1) for block in mine]


def joined(mine, other, *first):
    core = shift(other, "c", 1)
    return join(mine, after(core, *first) if first else core)


def spread(here, near, far, back):
    return here, shift(near, "y", 1), shift(far, "y", 2), shift(back, "y", 3)


def scatter(mine, other, *first):
    return spread(*joined(mine, other, *first))


def exchange(value, axes):
    return lax.all_to_all(value, axes, split_axis=0, concat_axis=0, tiled=True)


def after(value, *others):
    return lax.optimization_barrier((value, *others))[0]


def normalize(values):
    centre = jnp.mean(values, axis=-1, keepdims=True)
    centred = values - centre
    spread = jnp.mean(centred * centred, axis=-1, keepdims=True)
    inverse = lax.rsqrt(spread + epsilon)
    return centred * inverse, inverse


def norm_back(grad, gain, normal, inverse):
    scaled = grad * gain
    return inverse * (
        scaled
        - jnp.mean(scaled, axis=-1, keepdims=True)
        - normal * jnp.mean(scaled * normal, axis=-1, keepdims=True)
    )


def on_device(
    block_input,
    first_gain,
    first_shift,
    attention_weight,
    query_bias,
    value_bias,
    output_weight,
    output_bias,
    second_gain,
    second_shift,
    upward_weight,
    upward_bias,
    downward_weight,
    downward_bias,
    cotangent,
):
    y = lax.axis_index("y")
    xh = lax.axis_index("xh")
    c = lax.axis_index("c")
    shard = 4 * y + 2 * xh + c
    piece = np.arange(8)
    table = (2 * ((y + piece % 4) % 4) + (c ^ (piece // 4))).astype(jnp.int32)
    half = xh[None].astype(jnp.int32)
    whose = shard[None].astype(jnp.int32)
    slopes = jnp.exp2(-8.0 * (jnp.stack([shard, shard ^ 2]) + 1).astype(f32) / HEADS)

    with jax.named_scope("weights_attention"):
        vectors_own = [
            first_gain, first_shift, output_bias, second_gain, second_shift, downward_bias
        ]
        small = sum(
            jnp.pad(item[None], ((0, 15), (64 * g, 320 - 64 * g)))
            for g, item in enumerate(vectors_own)
        )
        small = small + jnp.pad(query_bias[None], ((1, 14), (0, 320)))
        small = small + jnp.pad(value_bias[None], ((1, 14), (64, 256)))
        small = small + jnp.pad(upward_bias[None], ((1, 14), (128, 0)))
        payload, up_payload = call(
            deal_kernel, "deal", [((16, 80, 384), bf16), ((16, 64, 512), bf16)], [],
            0, 4 * 10**6, 0, (attention_weight, small, upward_weight),
        )
        arrived = exchange(payload, FSDP)

    with jax.named_scope("first"):
        inputs = gather(block_input)
        heads_own, heads_send, normed_first, normal_first, project, vectors, bias_up = (
            first_heads(table, whose, inputs, arrived)
        )
        query = queries(normed_first, project, bias_up)
        heads_arrived = shift(heads_send, "xh", 1)
        cotangents = gather(after(cotangent, heads_send))
    with jax.named_scope("weights_upward"):
        upward_pair = exchange(after(up_payload, arrived), FSDP).reshape(D, 512)
    with jax.named_scope("weights_pair"):
        output_rows = shift(after(output_weight, arrived), "xh", 1)
        downward_rows = shift(after(downward_weight, heads_arrived), "xh", 1)
    with jax.named_scope("attention"):
        mixed, lse = attention_forward(half, slopes, query, heads_own, heads_arrived)
    with jax.named_scope("output"):
        mixed = after(mixed, upward_pair, *cotangents)
        mine, other = output_parts(table, mixed, output_weight, output_rows)
        residual_mid, normal_second, inverse_second, normed_second = middle(
            scatter(mine, other), block_input, vectors
        )

    with jax.named_scope("feed"):
        mine, other, activated, upward_grad, seconds, all_cotangents, hidden_sums = feed_parts(
            table, gather(normed_second), cotangents, upward_pair, downward_weight,
            downward_rows, bias_up,
        )
        sums_near = joined(mine, other)
        ends = spread(*sums_near)

    with jax.named_scope("upward_gradients"):
        late_grad, late_act = lax.optimization_barrier((upward_grad, activated, sums_near[0]))[0:2]
        upward_weight_grad = dot_tn(seconds, late_grad).astype(bf16)
        downward_grad = dot_tn(late_act, all_cotangents)
        downward_other = downward_grad[256:].astype(bf16)
        out_mine, out_other = out_parts(table, late_act, downward_weight, downward_rows)
    with jax.named_scope("feed"):
        ends = lax.optimization_barrier(
            (*ends, upward_weight_grad, downward_other, out_mine)
        )[0:4]
        mid_grad, branch_grad, sums = middle_back(
            ends, cotangent, vectors, normal_second, inverse_second
        )

    with jax.named_scope("upward_gradients"):
        shares = after(upward_weight_grad, branch_grad).reshape(128, 8, 512)
    with jax.named_scope("mixed_back"):
        mixed_grad, branch_grads = mixed_back(
            table, gather(branch_grad, shares), output_weight, output_rows
        )
        output_grad = dot_tn(mixed, branch_grads)
        output_other = output_grad[64:].astype(bf16)
        mixed_grad = after(mixed_grad, output_other)
    with jax.named_scope("upward_sums"):
        arrived_up = exchange(shares, FSDP + SEQ)
    with jax.named_scope("attention_back"):
        output_arrived = shift(output_other, "xh", 1)
        query_grad, back_own, back_send = attention_backward(
            half, slopes, query, heads_own, heads_arrived, mixed_grad, lse
        )
        back_send = after(back_send, arrived_up)
        back_arrived = shift(back_send, "xh", 1)
    with jax.named_scope("feed_out"):
        out_near = joined(out_mine, after(out_other, back_send))
        out_ends = spread(*out_near)
        block_output = block_end(out_ends, residual_mid, vectors)
    with jax.named_scope("row_gradients"):
        downward_arrived = shift(after(downward_other, branch_grad), "xh", 1)
        downward_sum = (downward_grad[:256] + downward_arrived.astype(f32)).astype(bf16)
        output_sum = (output_grad[:64] + output_arrived.astype(f32)).astype(bf16)
        rows_sent = jnp.concatenate(
            [output_sum.reshape(8, 8, D), downward_sum.reshape(8, 32, D)], axis=1
        )
        rows_all = exchange(after(rows_sent, arrived_up), SEQ)
    with jax.named_scope("first_back"):
        back_arrived = after(back_arrived, out_near[0])
        mine, other, head_grads, last_extra = last_parts(
            table, query_grad, back_own, back_arrived, project, normal_first, sums, hidden_sums
        )
        last_near = joined(mine, other)
        ends = spread(*last_near)
        input_gradient = input_end(ends, block_input, vectors, mid_grad)
    with jax.named_scope("attention_gradients"):
        weight_grad = dot_tn(normed_first, head_grads).astype(bf16)
        shares = jnp.concatenate([weight_grad, last_extra], axis=-1).reshape(128, 8, 640)
        shares = after(shares, rows_all, *out_ends[1:4])
        arrived_last = exchange(shares, FSDP + SEQ)
    with jax.named_scope("early_totals"):
        early = early_totals(after(rows_all, shares), arrived_up)
        early_pair = jnp.concatenate([early, shift(early, "xl", 1)], axis=0)
        early_all = [early_pair] + [shift(early_pair, "z", -step) for step in (1, 2, 3)]
        z = lax.axis_index("z")
        xl = lax.axis_index("xl")
        order = (2 * ((z + piece // 2) % 4) + (xl ^ (piece % 2))).astype(jnp.int32)
        output_weight_gradient, downward_weight_gradient, upward_weight_gradient = early_out(
            order, early_all
        )
    with jax.named_scope("late_totals"):
        late, late_small = late_totals(
            whose, after(arrived_last, last_near[0], early_pair)
        )
        attention_weight_gradient = late_out(exchange(late, SEQ))

    return (
        block_output,
        input_gradient,
        late_small[0, 0:64],
        late_small[0, 64:128],
        attention_weight_gradient,
        late_small[3, 0:64],
        late_small[3, 64:128],
        output_weight_gradient,
        late_small[2, 0:64],
        late_small[1, 0:64],
        late_small[1, 64:128],
        upward_weight_gradient,
        late_small[4],
        downward_weight_gradient,
        late_small[2, 64:128],
    )


def solution(mesh):
    grid = Mesh(mesh.devices.reshape(4, 2, 4, 2, 2), ALL)
    tokens = P(ALL, None)
    rows = P(FSDP, None)
    line = P(FSDP)
    return jax.shard_map(
        on_device,
        mesh=grid,
        in_specs=(
            tokens, line, line, rows, line, line, rows, line, line, line, rows, line, rows, line,
            tokens,
        ),
        out_specs=(
            tokens, tokens, line, line, rows, line, line, rows, line, line, line, rows, line, rows,
            line,
        ),
        check_vma=False,
    )
```
